256 devices in a mesh: seq: 16 (over z, core), expert: 16 (over y, x).
Axes of the slice: x: 4, y: 4, z: 8, core: 2. Of those that a mesh axis runs over, the one named last changes fastest.
Arguments:
- hidden_in: bfloat16 [2048, 2, 4096], P(('seq', 'expert')), may hold values from -6 to 6
- mamba_x: bfloat16 [2048, 2, 4096], P('seq', None, 'expert'), may hold values from -6 to 6
- mamba_z: bfloat16 [2048, 2, 4096], P('seq', None, 'expert'), may hold values from -6 to 6
- x_proj: bfloat16 [4096, 288], P('expert'), may hold values from -0.01171875 to 0.01171875
- dt_weight: bfloat16 [256, 4096], P(None, 'expert'), may hold values from -3 to 3
- dt_bias: float32 [4096], P('expert'), may hold values from -3 to -1
- state_rates: float32 [4096, 16], P('expert'), may hold values from 0 to 1
- skip_gain: float32 [4096], P('expert'), may hold values from 0.5 to 1.5
- out_weight: bfloat16 [4096, 4096], P('expert', 'seq'), may hold values from -0.09375 to 0.09375
- norm_gain: float32 [4096], replicated, may hold values from 0.5 to 1.5
- router_weight: bfloat16 [4096, 16], replicated, may hold values from -0.09375 to 0.09375
- expert_ids: int32 [2048, 2, 2], P(('seq', 'expert')), may hold values from 0 to 15, all different within a row; in each aligned block of 16 rows (0 to 15, 16 to 31, ..., all dimensions but the last counted through in order) at most 5 rows name the same one
- w_gate: bfloat16 [16, 4096, 7168], P('expert', None, 'seq'), may hold values from -0.09375 to 0.09375
- w_up: bfloat16 [16, 4096, 7168], P('expert', None, 'seq'), may hold values from -0.09375 to 0.09375
- w_down: bfloat16 [16, 4096, 7168], P('expert', None, 'seq'), may hold values from -0.0625 to 0.0625
Outputs:
- layer_out: bfloat16 [2048, 2, 4096], P(('seq', 'expert'))
The draws below stay inside these ranges and needn't reach their ends.
Inputs may be any that keep to these rules, and one draw needn't show every extreme that they name: `expert_ids`: each row names 2 different experts. Taking positions and documents together in position-major order, within each aligned block of 16 rows (the rows of one device) no expert is named by more than 5 rows, a bound that some block reaches.
All inputs are finite; a program needn't handle non-finite values.
Results may differ from the reference program's by a relative error of at most 0.009.
Values may be sent and summed in bfloat16 or wider, within the bound.
A program may use at most 128 MiB of HBM per device.

```python
import math
import jax
import jax.numpy as jnp
import numpy as np
from jax import lax

D = 4096
INNER = 4096
STATE = 16
RANK = 256
HID = 7168
TOPK = 2
DOCS = 2
EXPERTS = 16
SEQLEN = 2048
TOK_DEV = 16
CAP = 5
N_SEQ = 16
N_EXPERT = 16


def draw_state_rates(key, part):
    key = jax.random.fold_in(key, 7)
    first_key, second_key = jax.random.split(key)
    lowest = 8.0 / SEQLEN
    highest = 0.3
    levels = jax.random.uniform(first_key, (INNER, 1), jnp.float32)
    jitter = jax.random.uniform(second_key, (INNER, STATE), jnp.float32)
    reach = jnp.maximum(0.0, 2.0 * levels - 1.0)
    logs = jnp.log(lowest) + reach * jnp.log(highest / lowest) + 0.7 * jitter
    return jnp.exp(logs).astype(jnp.float32)


def steps_of(stream_key, dims, cuts, smallest, top_value):
    level = 1.0
    for axis_at, parts in cuts:
        steps = jax.random.uniform(jax.random.fold_in(jax.random.fold_in(stream_key, 6), axis_at), (parts,), jnp.float32, smallest / len(cuts), top_value / len(cuts))
        level = level * jnp.repeat(jnp.exp(steps), dims[axis_at] // parts).reshape((-1,) + (1,) * (len(dims) - 1 - axis_at))
    return level


def routed_block(key, own, number, rows, number_of, top, bound, skew):
    order = jax.random.permutation(key, number_of)
    crowded, ordinary = shares(number_of, rows * top, bound, skew, True), shares(number_of, rows * top, bound, skew, False)
    places = jnp.arange(number_of)

    def named(tallies, offset_by):
        used = int((tallies > 0).sum())
        fixed = max(1, used // 4)
        shifted = fixed + (places - fixed + offset_by * (used - fixed)) % max(1, number_of - fixed)
        return jnp.zeros((number_of,), jnp.int32).at[order[jnp.where(places < fixed, places, shifted)]].set(jnp.asarray(tallies, jnp.int32))

    tallies = jnp.where(number % 4 == 0, named(crowded, number // 4), named(ordinary, number - number // 4 - 1))
    mixed = jax.random.permutation(jax.random.fold_in(own, 3), number_of)
    source_of, sink = mixed[0:number_of // 2 * 2:2], mixed[1:number_of // 2 * 2:2]
    slack = jnp.minimum(tallies[source_of] - 1, bound - tallies[sink]) // 2
    slack = jnp.where((source_of == order[0]) | (sink == order[0]) | (tallies[sink] == 0), 0, jnp.maximum(slack, 0))
    shifted = jax.random.randint(jax.random.fold_in(own, 4), (number_of // 2,), 0, 1 << 20) % (slack + 1)
    tallies = tallies.at[source_of].add(-shifted).at[sink].add(shifted)
    items = jnp.searchsorted(jnp.cumsum(tallies), jnp.arange(rows * top), side="right").astype(jnp.int32)
    grid = items.reshape(top, rows).T
    grid = grid[jax.random.permutation(jax.random.fold_in(own, 1), rows)]
    offset_by = jax.random.randint(jax.random.fold_in(own, 2), (rows, 1), 0, top)
    return jnp.take_along_axis(grid, (jnp.arange(top)[None, :] + offset_by) % top, axis=1)


def shares(count, total, most, skew, full):
    loads = [(1 << 20) // math.isqrt(rank ** skew) + 1 for rank in range(1, count + 1)]
    largest = most if full else min(most, max(-(-total // count), total * loads[0] // sum(loads)))
    least = 1 if total - largest >= count - 1 else 0
    counts, rest = [largest] + [least] * (count - 1), total - largest - least * (count - 1)
    while rest > 0:
        candidates = [i for i in range(1, count) if counts[i] < largest] or [i for i in range(1, count) if counts[i] < most]
        mass, remaining = sum([loads[i] for i in candidates]), rest
        for i in candidates:
            extra = min(most - counts[i], max(1, remaining * loads[i] // mass), rest)
            counts[i] = counts[i] + extra
            rest = rest - extra
    return np.array(counts)


def normal_values(rng, dims, scale, limit, cuts=(), kind=jnp.bfloat16):
    gain = steps_of(rng, dims, cuts, -0.22, 0.18) if cuts else 1.0
    values = jax.random.normal(rng, dims, jnp.float32) * scale * gain
    return jnp.minimum(jnp.maximum(values, -limit), limit).astype(kind)


def setup_inputs(seed: int = 0) -> dict:
    arg_keys = jax.random.split(jax.random.key(seed), 16)
    hidden_in = normal_values(arg_keys[0], (SEQLEN, DOCS, D), 1.0, 6.0, ((0, 256),))
    mamba_x = normal_values(arg_keys[1], (SEQLEN, DOCS, INNER), 1.0, 6.0, ((0, 16), (2, 16)))
    mamba_z = normal_values(arg_keys[2], (SEQLEN, DOCS, INNER), 1.0, 6.0, ((0, 16), (2, 16)))
    x_proj = normal_values(arg_keys[3], (INNER, RANK + 2 * STATE), (64 * INNER) ** -0.5, 0.01171875, ((0, 16),))
    dt_weight = normal_values(arg_keys[4], (RANK, INNER), (max(1, RANK // 64)) ** -0.5, 3.0, ((1, 16),))
    dt_bias = jnp.clip(-3.0 + 2.0 * jax.random.uniform(arg_keys[5], (INNER,), jnp.float32) ** steps_of(arg_keys[5], (INNER,), ((0, 16),), -0.2, 0.2), -3.0, -1.0)
    state_rates = draw_state_rates(jax.random.fold_in(arg_keys[15], 71), 0)
    skip_gain = jnp.clip(0.5 + 1.0 * jax.random.uniform(arg_keys[7], (INNER,), jnp.float32) ** steps_of(arg_keys[7], (INNER,), ((0, 16),), -0.2, 0.2), 0.5, 1.5)
    out_weight = normal_values(arg_keys[8], (INNER, D), INNER ** -0.5, 0.09375, ((0, 16), (1, 16)))
    norm_gain = jnp.clip(jax.random.uniform(arg_keys[9], (D,), jnp.float32, 0.5, 1.5), 0.5, 1.5)
    router_weight = normal_values(arg_keys[10], (D, EXPERTS), D ** -0.5, 0.09375)
    expert_ids_keys = jax.random.split(jax.random.fold_in(arg_keys[11], 1), SEQLEN * DOCS // TOK_DEV)
    expert_ids_turns = jax.random.permutation(jax.random.fold_in(arg_keys[11], 3), SEQLEN * DOCS // TOK_DEV)
    expert_ids = jax.vmap(lambda own, number: routed_block(jax.random.fold_in(arg_keys[11], 2), own, number, TOK_DEV, EXPERTS, TOPK, CAP, 1))(expert_ids_keys, expert_ids_turns).reshape((SEQLEN, DOCS, TOPK))
    w_gate = normal_values(arg_keys[12], (EXPERTS, D, HID), D ** -0.5, 0.09375, ((0, 16), (2, 16)))
    w_up = normal_values(arg_keys[13], (EXPERTS, D, HID), D ** -0.5, 0.09375, ((0, 16), (2, 16)))
    w_down = normal_values(arg_keys[14], (EXPERTS, D, HID), HID ** -0.5, 0.0625, ((0, 16), (2, 16)))
    return {"hidden_in": hidden_in, "mamba_x": mamba_x, "mamba_z": mamba_z, "x_proj": x_proj, "dt_weight": dt_weight, "dt_bias": dt_bias, "state_rates": state_rates, "skip_gain": skip_gain, "out_weight": out_weight, "norm_gain": norm_gain, "router_weight": router_weight, "expert_ids": expert_ids, "w_gate": w_gate, "w_up": w_up, "w_down": w_down}


EPS = 1e-05

def advance_states(step_sizes, drive_in, b_terms, c_terms, rates):

    def advance(carried, inputs):
        sizes_now, drive_now, b_row, c_row = inputs
        decays = jnp.exp(-sizes_now[:, :, None] * rates[None])
        carried = decays * carried + (sizes_now * drive_now)[:, :, None] * b_row[:, None, :]
        return (carried, lax.optimization_barrier(jnp.sum(carried * c_row[:, None, :], axis=-1)))
    initial = jnp.zeros((DOCS, INNER, STATE), jnp.float32)
    _, readings = lax.scan(advance, initial, (step_sizes, drive_in, b_terms, c_terms))
    return readings

def expert_apply(operands):
    rows, gate_all, up_all, down_all = operands
    width = HID // N_SEQ

    def add_block(index, total):
        lower = (index * width).astype(jnp.int32)
        gate_part = lax.dynamic_slice_in_dim(gate_all, lower, width, 1)
        up_part = lax.dynamic_slice_in_dim(up_all, lower, width, 1)
        down_part = lax.dynamic_slice_in_dim(down_all, lower, width, 1)
        hidden = (jax.nn.silu(jnp.dot(rows, gate_part, preferred_element_type=jnp.float32)) * jnp.dot(rows, up_part, preferred_element_type=jnp.float32)).astype(jnp.bfloat16)
        product = lax.dot_general(hidden, down_part, (((1,), (1,)), ((), ())), preferred_element_type=jnp.float32)
        rounded = lax.optimization_barrier(product.astype(jnp.bfloat16))
        return total + rounded.astype(jnp.float32)
    total = lax.fori_loop(0, N_SEQ, add_block, jnp.zeros((rows.shape[0], D), jnp.float32))
    return total.astype(jnp.bfloat16)

def reference(hidden_in, mamba_x, mamba_z, x_proj, dt_weight, dt_bias, state_rates, skip_gain, out_weight, norm_gain, router_weight, expert_ids, w_gate, w_up, w_down):
    rows_all = SEQLEN * DOCS
    flat_x = mamba_x.reshape(rows_all, INNER)
    proj = jnp.dot(flat_x, x_proj, preferred_element_type=jnp.float32)
    dt_low = proj[:, :RANK].astype(jnp.bfloat16)
    step_sizes = jax.nn.softplus(jnp.dot(dt_low, dt_weight, preferred_element_type=jnp.float32) + dt_bias)
    b_terms = proj[:, RANK:RANK + STATE].reshape(SEQLEN, DOCS, STATE)
    c_terms = proj[:, RANK + STATE:].reshape(SEQLEN, DOCS, STATE)
    drive = mamba_x.astype(jnp.float32)
    readings = advance_states(step_sizes.reshape(SEQLEN, DOCS, INNER), drive, b_terms, c_terms, state_rates)
    gated = ((readings + skip_gain * drive) * jax.nn.silu(mamba_z.astype(jnp.float32))).astype(jnp.bfloat16)
    mixer = jnp.dot(gated.reshape(rows_all, INNER), out_weight, preferred_element_type=jnp.float32)
    mixed = (hidden_in.reshape(rows_all, D).astype(jnp.float32) + mixer).astype(jnp.bfloat16)
    wide = lax.optimization_barrier(mixed).astype(jnp.float32)
    normed = (wide * lax.rsqrt(lax.optimization_barrier(jnp.mean(wide * wide, axis=-1, keepdims=True)) + EPS) * norm_gain).astype(jnp.bfloat16)
    logits = jnp.dot(normed, router_weight, preferred_element_type=jnp.float32)
    chosen_ids = expert_ids.reshape(rows_all, TOPK)
    picked = jnp.take_along_axis(logits, chosen_ids, axis=1)
    scores = jax.nn.sigmoid(picked)
    gates = scores / lax.optimization_barrier(jnp.sum(scores, axis=1, keepdims=True))
    blocks = N_SEQ * N_EXPERT
    per_block = TOK_DEV * TOPK
    flat_ids = chosen_ids.reshape(blocks, per_block)
    marks = (flat_ids[:, :, None] == jnp.arange(EXPERTS, dtype=jnp.int32)[None, None, :]).astype(jnp.int32)
    slots = lax.optimization_barrier(jnp.sum((jnp.cumsum(marks, axis=1) - 1) * marks, axis=2)).astype(jnp.int32)
    block_ids = jnp.broadcast_to(jnp.arange(blocks, dtype=jnp.int32)[:, None], (blocks, per_block))
    sources = jnp.repeat(normed, TOPK, axis=0).reshape(blocks, per_block, D)
    buffers = jnp.zeros((EXPERTS, blocks, CAP, D), jnp.bfloat16).at[flat_ids, block_ids, slots].set(sources)
    returned = lax.map(expert_apply, (buffers.reshape(EXPERTS, blocks * CAP, D), w_gate, w_up, w_down))
    returned = returned.reshape(EXPERTS, blocks, CAP, D)
    collected = returned[flat_ids, block_ids, slots].astype(jnp.float32).reshape(rows_all, TOPK, D)
    routed = lax.optimization_barrier(jnp.sum(gates[:, :, None] * collected, axis=1))
    result = (wide + routed).astype(jnp.bfloat16)
    return result.reshape(SEQLEN, DOCS, D)
```

```python
import functools

import jax
import jax.numpy as jnp
from jax import lax
from jax.experimental import pallas as pl
from jax.experimental.pallas import tpu as pltpu
from jax.sharding import PartitionSpec as P

EPS = 1e-05
F32 = jnp.float32
BF16 = jnp.bfloat16
BLOCK = 16
VMEM = pl.BlockSpec(memory_space=pltpu.VMEM)
HBM = pl.BlockSpec(memory_space=pl.ANY)


def remote(src, dst, send, recv, where):
    return pltpu.make_async_remote_copy(
        src_ref=src,
        dst_ref=dst,
        send_sem=send,
        recv_sem=recv,
        device_id=where,
        device_id_type=pl.DeviceIdType.MESH,
    )


def greet(ns, ne, seq, expert):
    barrier = pltpu.get_barrier_semaphore()

    def to_seq(o, _):
        pl.semaphore_signal(
            barrier, inc=1, device_id={"seq": lax.rem(seq + o, ns)}, device_id_type=pl.DeviceIdType.MESH
        )
        return 0

    def to_expert(o, _):
        pl.semaphore_signal(
            barrier, inc=1, device_id={"expert": lax.rem(expert + o, ne)}, device_id_type=pl.DeviceIdType.MESH
        )
        return 0

    lax.fori_loop(1, ns, to_seq, 0)
    lax.fori_loop(1, ne, to_expert, 0)
    pl.semaphore_wait(barrier, ns + ne - 2)


def mixer_kernel(
    ns, ne,
    x_ref, z_ref, xp_ref, dtw_ref, dtb_ref, rates_ref, skip_ref, w_ref, hid_ref, wg_ref, wu_ref, wd_ref,
    mixed_ref, wg2_ref, wu2_ref, wd2_ref,
    part, part_in, part_sum, proj, sizes, running, reading, bc, state, state_in, gated, wf, product, product_in, total,
    pair_send, pair_recv, p1_send, p1_recv, p2_send, p2_recv, s_send, s_recv, ring_send, ring_recv,
    sib_send, sib_recv, o_send, o_recv,
):
    seq, expert = lax.axis_index("seq"), lax.axis_index("expert")
    nz = ns // 2
    hops, back = nz // 2, nz - 1 - nz // 2
    plane, core = seq // 2, lax.rem(seq, 2)
    right = lax.rem(plane + 1, nz) * 2 + core
    left = lax.rem(plane + nz - 1, nz) * 2 + core
    sibling = plane * 2 + 1 - core
    rank = dtw_ref.shape[0]
    tokens, channels = x_ref.shape
    state_n = rates_ref.shape[0]
    own = tokens // ne
    blocks = tokens // (2 * BLOCK)
    span = 2 * BLOCK
    columns = w_ref.shape[1]

    def ring_copy(stage, forward):
        if forward:
            index = lax.rem(plane + nz - (stage - 1), nz) * 2 + core
            return remote(wf.at[index], wf.at[index], ring_send.at[0, stage - 1], ring_recv.at[0, stage - 1], {"seq": right})
        index = lax.rem(plane + stage - 1, nz) * 2 + core
        return remote(wf.at[index], wf.at[index], ring_send.at[1, stage - 1], ring_recv.at[1, stage - 1], {"seq": left})

    def sibling_copy(index):
        return remote(wf.at[index], wf.at[index], sib_send.at[index // 2], sib_recv.at[index // 2], {"seq": sibling})

    def ring_stage(stage):
        if 1 < stage <= hops + 1:
            ring_copy(stage - 1, True).wait_recv()
            sibling_copy(lax.rem(plane + nz - (stage - 1), nz) * 2 + core).start()
        if 1 < stage <= back + 1:
            ring_copy(stage - 1, False).wait_recv()
            sibling_copy(lax.rem(plane + stage - 1, nz) * 2 + core).start()
        if stage <= hops:
            ring_copy(stage, True).start()
        if stage <= back:
            ring_copy(stage, False).start()

    with jax.named_scope("greet"):
        wf[seq] = w_ref[...]
        greet(ns, ne, seq, expert)
        ring_stage(1)
        sibling_copy(seq).start()
        weight_copies = [
            remote(src, dst, pair_send.at[i], pair_recv.at[i], {"seq": sibling})
            for i, (src, dst) in enumerate(((wg_ref, wg2_ref), (wu_ref, wu2_ref), (wd_ref, wd2_ref)))
        ]
        for copy in weight_copies:
            copy.start()

    with jax.named_scope("proj"):
        partial = jnp.dot(x_ref[...], xp_ref[...], preferred_element_type=F32).astype(BF16)
        part[...] = partial.reshape(part.shape)

        def part_copy(o):
            to = lax.rem(expert + o, ne)
            return remote(part.at[to], part_in.at[o - 1], p1_send.at[o - 1], p1_recv.at[o - 1], {"expert": to})

        def start_part(o, _):
            part_copy(o).start()
            return 0

        lax.fori_loop(1, ne, start_part, 0)
        ring_stage(2)

        def add_part(o, acc):
            part_copy(o).wait_recv()
            return acc + part_in[o - 1].astype(F32)

        summed = lax.fori_loop(1, ne, add_part, part[expert].astype(F32))
        part_sum[...] = summed.astype(BF16)
        proj[expert] = part_sum[...]

        def proj_copy(o):
            to = lax.rem(expert + o, ne)
            return remote(part_sum, proj.at[expert], p2_send.at[o - 1], p2_recv.at[o - 1], {"expert": to})

        def start_proj(o, _):
            proj_copy(o).start()
            return 0

        def wait_proj(o, _):
            proj_copy(o).wait_recv()
            return 0

        lax.fori_loop(1, ne, start_proj, 0)
        ring_stage(3)
        lax.fori_loop(1, ne, wait_proj, 0)

    with jax.named_scope("sizes"):
        low = proj[:, :, :rank].reshape(tokens, rank)
        raw = jnp.dot(low, dtw_ref[...], preferred_element_type=F32) + dtb_ref[...]
        sizes[...] = jnp.maximum(raw, 0.0) + jnp.log1p(jnp.exp(-jnp.abs(raw)))
        turned = proj[:, :, rank:].reshape(tokens, proj.shape[2] - rank).astype(F32).T
        for b in range(blocks):
            bc[b, :, :span] = turned[: 2 * state_n, b * span : (b + 1) * span]

    with jax.named_scope("scan"):
        rates = -rates_ref[...]
        zero_state = jnp.zeros((state_n, channels), F32)
        zero_row = jnp.zeros((1, channels), F32)

        def scan_block(b, carry):
            states, sums = [carry[0], carry[1]], [carry[2], carry[3]]
            first = pl.multiple_of(b * span, span)
            size_block = sizes[pl.ds(first, span), :]
            drive_block = size_block * x_ref[pl.ds(first, span), :].astype(F32)
            terms = bc[b]
            for r in range(span):
                d = r % 2
                size = size_block[r : r + 1]
                states[d] = (
                    jnp.exp(size * rates) * states[d] + drive_block[r : r + 1] * terms[:state_n, r : r + 1]
                )
                reading[pl.ds(first + r, 1), :] = jnp.sum(
                    states[d] * terms[state_n : 2 * state_n, r : r + 1], axis=0, keepdims=True
                )
                sums[d] = sums[d] + size
                running[pl.ds(first + r, 1), :] = sums[d]
            return states[0], states[1], sums[0], sums[1]

        end0, end1, sum0, sum1 = lax.fori_loop(
            0, blocks, scan_block, (zero_state, zero_state, zero_row, zero_row)
        )
        state[:state_n, :] = end0
        state[state_n : 2 * state_n, :] = end1
        state[2 * state_n : 2 * state_n + 8, :] = jnp.concatenate(
            [sum0, sum1, jnp.zeros((6, channels), F32)], axis=0
        )

    with jax.named_scope("states"):

        def state_copy(to, source):
            return remote(state, state_in.at[source], s_send.at[to], s_recv.at[source], {"seq": to})

        def start_state(to, _):
            state_copy(to, seq).start()
            return 0

        lax.fori_loop(seq + 1, ns, start_state, 0)
        for stage in range(4, hops + 2):
            ring_stage(stage)

        def combine(source, carry):
            state_copy(seq, source).wait_recv()
            message = state_in[source]
            through0 = jnp.exp(message[2 * state_n : 2 * state_n + 1] * rates)
            through1 = jnp.exp(message[2 * state_n + 1 : 2 * state_n + 2] * rates)
            return (
                through0 * carry[0] + message[:state_n],
                through1 * carry[1] + message[state_n : 2 * state_n],
            )

        incoming = lax.fori_loop(0, seq, combine, (zero_state, zero_state))

    with jax.named_scope("gate"):
        skip = skip_ref[...]

        def gate_block(b, _):
            first = pl.multiple_of(b * span, span)
            sum_block = running[pl.ds(first, span), :]
            terms = bc[b]
            for r in range(span):
                carried = jnp.exp(sum_block[r : r + 1] * rates) * incoming[r % 2]
                reading[pl.ds(first + r, 1), :] += jnp.sum(
                    carried * terms[state_n : 2 * state_n, r : r + 1], axis=0, keepdims=True
                )
            drive = x_ref[pl.ds(first, span), :].astype(F32)
            gate = z_ref[pl.ds(first, span), :].astype(F32)
            value = (reading[pl.ds(first, span), :] + skip * drive) * (gate / (1.0 + jnp.exp(-gate)))
            gated[pl.ds(first, span), :] = value.astype(BF16)
            return 0

        lax.fori_loop(0, blocks, gate_block, 0)

    with jax.named_scope("project"):

        def sibling_wait(i, _):
            sibling_copy(2 * i + 1 - core).wait_recv()
            return 0

        lax.fori_loop(0, nz, sibling_wait, 0)

        def multiply(b, _):
            at = pl.multiple_of(b * columns, columns)
            out = jnp.dot(gated[...], wf[b], preferred_element_type=F32).astype(BF16)
            product[:, :, pl.ds(at, columns)] = out.reshape(ne, own, columns)
            return 0

        lax.fori_loop(0, ns, multiply, 0)

        def product_copy(o):
            to = lax.rem(expert + o, ne)
            return remote(product.at[to], product_in.at[o - 1], o_send.at[o - 1], o_recv.at[o - 1], {"expert": to})

        def start_product(o, _):
            product_copy(o).start()
            return 0

        lax.fori_loop(1, ne, start_product, 0)
        total[...] = hid_ref[...].astype(F32) + product[expert].astype(F32)

        def add_product(o, _):
            product_copy(o).wait_recv()
            total[...] += product_in[o - 1].astype(F32)
            return 0

        lax.fori_loop(1, ne, add_product, 0)
        mixed_ref[...] = total[...].astype(BF16)

    with jax.named_scope("finish"):

        def sent_peers(o, _):
            part_copy(o).wait_send()
            proj_copy(o).wait_send()
            product_copy(o).wait_send()
            return 0

        lax.fori_loop(1, ne, sent_peers, 0)

        def sent_state(to, _):
            state_copy(to, seq).wait_send()
            return 0

        lax.fori_loop(seq + 1, ns, sent_state, 0)
        for stage in range(1, hops + 1):
            ring_copy(stage, True).wait_send()
        for stage in range(1, back + 1):
            ring_copy(stage, False).wait_send()

        def sent_sibling(i, _):
            sibling_copy(2 * i + core).wait_send()
            return 0

        lax.fori_loop(0, nz, sent_sibling, 0)
        for copy in weight_copies:
            copy.wait()


def mixer_call(ns, ne, x, z, xp, dtw, dtb, rates, skip, w, hid, wg, wu, wd):
    tokens, channels = x.shape
    own, width = hid.shape
    state_n = rates.shape[0]
    lanes = xp.shape[1]
    nz = ns // 2
    hops = nz // 2
    dma = pltpu.SemaphoreType.DMA
    return pl.pallas_call(
        functools.partial(mixer_kernel, ns, ne),
        out_shape=(
            jax.ShapeDtypeStruct((own, width), BF16),
            jax.ShapeDtypeStruct(wg.shape, BF16),
            jax.ShapeDtypeStruct(wu.shape, BF16),
            jax.ShapeDtypeStruct(wd.shape, BF16),
        ),
        in_specs=[VMEM] * 9 + [HBM] * 3,
        out_specs=(VMEM, HBM, HBM, HBM),
        scratch_shapes=[
            pltpu.VMEM((ne, own, lanes), BF16),
            pltpu.VMEM((ne - 1, own, lanes), BF16),
            pltpu.VMEM((own, lanes), BF16),
            pltpu.VMEM((ne, own, lanes), BF16),
            pltpu.VMEM((tokens, channels), F32),
            pltpu.VMEM((tokens, channels), F32),
            pltpu.VMEM((tokens, channels), F32),
            pltpu.VMEM((tokens // (2 * BLOCK), 2 * state_n, 128), F32),
            pltpu.VMEM((2 * state_n + 8, channels), F32),
            pltpu.VMEM((ns, 2 * state_n + 8, channels), F32),
            pltpu.VMEM((tokens, channels), BF16),
            pltpu.VMEM((ns,) + w.shape, BF16),
            pltpu.VMEM((ne, own, width), BF16),
            pltpu.VMEM((ne - 1, own, width), BF16),
            pltpu.VMEM((own, width), F32),
            dma((3,)), dma((3,)),
            dma((ne - 1,)), dma((ne - 1,)),
            dma((ne - 1,)), dma((ne - 1,)),
            dma((ns,)), dma((ns,)),
            dma((2, hops)), dma((2, hops)),
            dma((nz,)), dma((nz,)),
            dma((ne - 1,)), dma((ne - 1,)),
        ],
        compiler_params=pltpu.CompilerParams(
            collective_id=0, has_side_effects=True, vmem_limit_bytes=48 * 1024 * 1024
        ),
    )(x, z, xp, dtw, dtb, rates, skip, w, hid, wg, wu, wd)


def expert_kernel(
    ns,
    rows_ref, wg_ref, wu_ref, wd_ref, wg2_ref, wu2_ref, wd2_ref,
    out_ref,
    held, parts, from_left, from_right, gate_w, up_w, down_w, hidden,
    w_sem, g_send, g_recv, r_send, r_recv,
):
    seq = lax.axis_index("seq")
    nz = ns // 2
    hops = nz // 2
    plane, core = seq // 2, lax.rem(seq, 2)
    right = {"seq": lax.rem(plane + 1, nz) * 2 + core}
    left = {"seq": lax.rem(plane + nz - 1, nz) * 2 + core}
    count, width = rows_ref.shape
    half = width // 2
    low, high = pl.ds(0, half), pl.ds(half, half)

    def gather_copy(stage, forward):
        side = 0 if forward else 1
        source = held.at[2 * (stage - 1) + (0 if forward or stage == 1 else 1)]
        if stage < hops:
            target = held.at[2 * stage + side]
        else:
            columns = low if forward else high
            source, target = source.at[:, columns], held.at[1, :, columns]
        return remote(
            source, target, g_send.at[side, stage - 1], g_recv.at[side, stage - 1], right if forward else left
        )

    def return_copy(stage, forward):
        side = 0 if forward else 1
        buffer = from_left if forward else from_right
        distance = hops - stage + 1
        if stage == 1:
            columns = low if forward else high
            source, target = parts.at[1, :, columns], buffer.at[0, :, columns]
        else:
            source, target = parts.at[2 * distance + (1 if forward else 0)], buffer.at[stage - 1]
        return remote(
            source, target, r_send.at[side, stage - 1], r_recv.at[side, stage - 1], right if forward else left
        )

    with jax.named_scope("load"):
        loads = [
            pltpu.make_async_copy(src, dst.at[i], w_sem.at[j, i])
            for j, (pair, dst) in enumerate(
                (((wg_ref, wg2_ref), gate_w), ((wu_ref, wu2_ref), up_w), ((wd_ref, wd2_ref), down_w))
            )
            for i, src in enumerate(pair)
        ]
        for copy in loads:
            copy.start()
        held[0] = rows_ref[...]
        barrier = pltpu.get_barrier_semaphore()
        for to in (left, right):
            pl.semaphore_signal(barrier, inc=1, device_id=to, device_id_type=pl.DeviceIdType.MESH)
        pl.semaphore_wait(barrier, 2)
        gather_copy(1, True).start()
        gather_copy(1, False).start()

    def compute(pair):
        rows = held[2 * pair : 2 * pair + 2].reshape(2 * count, width)
        for i in range(2):
            gate = jnp.dot(rows, gate_w[i], preferred_element_type=F32)
            up = jnp.dot(rows, up_w[i], preferred_element_type=F32)
            hidden[i] = (gate / (1.0 + jnp.exp(-gate)) * up).astype(BF16)
        step = min(width, 512)

        def down(b, _):
            at = pl.multiple_of(b * step, step)
            out = sum(
                lax.dot_general(
                    hidden[i], down_w[i, pl.ds(at, step), :], (((1,), (1,)), ((), ())), preferred_element_type=F32
                )
                for i in range(2)
            )
            parts[2 * pair : 2 * pair + 2, :, pl.ds(at, step)] = out.astype(BF16).reshape(2, count, step)
            return 0

        lax.fori_loop(0, width // step, down, 0)

    for stage in range(1, hops + 1):
        with jax.named_scope("gather"):
            gather_copy(stage, True).wait_recv()
            gather_copy(stage, False).wait_recv()
            if stage < hops:
                gather_copy(stage + 1, True).start()
                gather_copy(stage + 1, False).start()
            if stage == 1:
                for copy in loads:
                    copy.wait()
        with jax.named_scope("experts"):
            compute(stage if stage < hops else 0)

    for stage in range(1, hops + 1):
        with jax.named_scope("combine"):
            if stage > 1:
                distance = hops - stage + 1
                for forward, buffer in ((True, from_left), (False, from_right)):
                    return_copy(stage - 1, forward).wait_recv()
                    slot = 2 * distance + (1 if forward else 0)
                    if stage == 2:
                        columns = low if forward else high
                        parts[slot, :, columns] = (
                            parts[slot, :, columns].astype(F32) + buffer[0, :, columns].astype(F32)
                        ).astype(BF16)
                    else:
                        parts[slot] = (parts[slot].astype(F32) + buffer[stage - 2].astype(F32)).astype(BF16)
                    return_copy(stage, forward).start()
            else:
                return_copy(1, True).start()
                return_copy(1, False).start()

    with jax.named_scope("last"):
        return_copy(hops, True).wait_recv()
        return_copy(hops, False).wait_recv()
        if hops > 1:
            total = from_left[hops - 1].astype(F32) + from_right[hops - 1].astype(F32)
            out_ref[...] = (parts[0].astype(F32) + total).astype(BF16)
        else:
            out_ref[:, low] = (parts[0, :, low].astype(F32) + from_left[0, :, low].astype(F32)).astype(BF16)
            out_ref[:, high] = (parts[0, :, high].astype(F32) + from_right[0, :, high].astype(F32)).astype(BF16)
        for stage in range(1, hops + 1):
            for forward in (True, False):
                gather_copy(stage, forward).wait_send()
                return_copy(stage, forward).wait_send()


def expert_call(ns, rows, wg, wu, wd, wg2, wu2, wd2):
    count, width = rows.shape
    hid = wg.shape[1]
    nz = ns // 2
    hops = nz // 2
    dma = pltpu.SemaphoreType.DMA
    return pl.pallas_call(
        functools.partial(expert_kernel, ns),
        out_shape=jax.ShapeDtypeStruct((count, width), BF16),
        in_specs=[VMEM] + [HBM] * 6,
        out_specs=VMEM,
        scratch_shapes=[
            pltpu.VMEM((nz, count, width), BF16),
            pltpu.VMEM((nz, count, width), BF16),
            pltpu.VMEM((hops, count, width), BF16),
            pltpu.VMEM((hops, count, width), BF16),
            pltpu.VMEM((2, width, hid), BF16),
            pltpu.VMEM((2, width, hid), BF16),
            pltpu.VMEM((2, width, hid), BF16),
            pltpu.VMEM((2, 2 * count, hid), BF16),
            dma((3, 2)),
            dma((2, hops)), dma((2, hops)),
            dma((2, hops)), dma((2, hops)),
        ],
        compiler_params=pltpu.CompilerParams(
            collective_id=1, has_side_effects=True, vmem_limit_bytes=60 * 1024 * 1024
        ),
    )(rows, wg, wu, wd, wg2, wu2, wd2)


def body(
    hidden_in,
    mamba_x,
    mamba_z,
    x_proj,
    dt_weight,
    dt_bias,
    state_rates,
    skip_gain,
    out_weight,
    norm_gain,
    router_weight,
    expert_ids,
    w_gate,
    w_up,
    w_down,
):
    ns, ne = lax.axis_size("seq"), lax.axis_size("expert")
    slice_len, docs, channels = mamba_x.shape
    model_width = hidden_in.shape[2]
    token_rows = hidden_in.shape[0] * docs
    lanes = -(-x_proj.shape[1] // 128) * 128
    mixed, wg2, wu2, wd2 = mixer_call(
        ns,
        ne,
        mamba_x.reshape(slice_len * docs, channels),
        mamba_z.reshape(slice_len * docs, channels),
        jnp.pad(x_proj, ((0, 0), (0, lanes - x_proj.shape[1]))),
        dt_weight,
        dt_bias[None],
        state_rates.T,
        skip_gain[None],
        out_weight,
        hidden_in.reshape(token_rows, model_width),
        w_gate[0],
        w_up[0],
        w_down[0],
    )
    wide = mixed.astype(jnp.float32)
    normed = (
        wide * lax.rsqrt(jnp.mean(wide * wide, axis=-1, keepdims=True) + EPS) * norm_gain
    ).astype(jnp.bfloat16)
    logits = jnp.dot(normed, router_weight, preferred_element_type=jnp.float32)
    experts = router_weight.shape[1]
    top_count = expert_ids.shape[2]
    chosen_ids = expert_ids.reshape(token_rows, top_count)
    expert_range = jnp.arange(experts, dtype=jnp.int32)
    id_marks = chosen_ids[:, :, None] == expert_range[None, None, :]
    picked = jnp.sum(jnp.where(id_marks, logits[:, None, :], 0.0), axis=2)
    scores = jax.nn.sigmoid(picked)
    gates = scores / jnp.sum(scores, axis=1, keepdims=True)
    capacity = max(2, min(token_rows, token_rows * top_count * 5 // (2 * experts)))
    flat_ids = chosen_ids.reshape(-1)
    marks = (flat_ids[:, None] == expert_range[None, :]).astype(jnp.int32)
    slots = jnp.sum((jnp.cumsum(marks, axis=0) - 1) * marks, axis=1)
    targets = flat_ids * capacity + slots
    placement = (
        jnp.arange(experts * capacity, dtype=jnp.int32)[:, None] == targets[None, :]
    ).astype(jnp.bfloat16)
    sources = jnp.repeat(normed, top_count, axis=0)
    outgoing_rows = jnp.dot(placement, sources, preferred_element_type=jnp.float32).astype(
        jnp.bfloat16
    )
    outgoing_rows = outgoing_rows.reshape(experts, capacity, model_width)
    arrived = lax.all_to_all(outgoing_rows, "expert", split_axis=0, concat_axis=0, tiled=True)
    rows = arrived.reshape(-1, model_width)
    summed = expert_call(ns, rows, w_gate[0], w_up[0], w_down[0], wg2, wu2, wd2)
    expert_back = summed.reshape(arrived.shape)
    returned = lax.all_to_all(expert_back, "expert", split_axis=0, concat_axis=0, tiled=True)
    back_rows = lax.dot_general(
        placement,
        returned.reshape(-1, model_width),
        (((0,), (0,)), ((), ())),
        preferred_element_type=jnp.float32,
    )
    collected = back_rows.reshape(token_rows, top_count, model_width)
    routed = jnp.sum(gates[:, :, None] * collected, axis=1)
    result = (wide + routed).astype(jnp.bfloat16)
    return result.reshape(hidden_in.shape)


def solution(mesh):
    placed = (
        P(("seq", "expert"), None, None),
        P("seq", None, "expert"),
        P("seq", None, "expert"),
        P("expert", None),
        P(None, "expert"),
        P("expert"),
        P("expert", None),
        P("expert"),
        P("expert", "seq"),
        P(),
        P(),
        P(("seq", "expert"), None, None),
        P("expert", None, "seq"),
        P("expert", None, "seq"),
        P("expert", None, "seq"),
    )
    return jax.shard_map(
        body,
        mesh=mesh,
        in_specs=placed,
        out_specs=P(("seq", "expert"), None, None),
        check_vma=False,
    )
```

```python
import functools

import jax
import jax.numpy as jnp
from jax import lax
from jax.experimental import pallas as pl
from jax.experimental.pallas import tpu as pltpu
from jax.sharding import PartitionSpec as P

EPS = 1e-05
F32 = jnp.float32
BF16 = jnp.bfloat16
BLOCK = 16
VMEM = pl.BlockSpec(memory_space=pltpu.VMEM)
HBM = pl.BlockSpec(memory_space=pl.ANY)


def remote(src, dst, send, recv, where):
    return pltpu.make_async_remote_copy(
        src_ref=src,
        dst_ref=dst,
        send_sem=send,
        recv_sem=recv,
        device_id=where,
        device_id_type=pl.DeviceIdType.MESH,
    )


def greet(ns, ne, seq, expert):
    barrier = pltpu.get_barrier_semaphore()

    def to_seq(o, _):
        pl.semaphore_signal(
            barrier, inc=1, device_id={"seq": lax.rem(seq + o, ns)}, device_id_type=pl.DeviceIdType.MESH
        )
        return 0

    def to_expert(o, _):
        pl.semaphore_signal(
            barrier, inc=1, device_id={"expert": lax.rem(expert + o, ne)}, device_id_type=pl.DeviceIdType.MESH
        )
        return 0

    lax.fori_loop(1, ns, to_seq, 0)
    lax.fori_loop(1, ne, to_expert, 0)
    pl.semaphore_wait(barrier, ns + ne - 2)


def layer_kernel(
    ns, ne, cap,
    x_ref, z_ref, xp_ref, dtw_ref, dtb_ref, rates_ref, skip_ref, w_ref, hid_ref,
    gain_ref, router_ref, place_ref, pick_ref, put_ref, wg_ref, wu_ref, wd_ref,
    out_ref,
    part, part_in, part_sum, proj, sizes, running, reading, bc,
    state, state_sib, state_chip, state_in, incoming, gated, wf,
    product, row_in, row_sum, row_last, col_in, col_sum, col_last,
    wide, combine_w, flat, packed_out, packed_in, back_out, back_in, returned,
    held, parts, from_left, from_right, gate_w, up_w, down_w, hidden,
    load_sem, pair_send, pair_recv, p1_send, p1_recv, p2_send, p2_recv,
    h_send, h_recv, s_send, s_recv, ring_send, ring_recv, sib_send, sib_recv,
    a_send, a_recv, b_send, b_recv, d_send, d_recv, e_send, e_recv,
    g_send, g_recv, r_send, r_recv,
):
    seq, expert = lax.axis_index("seq"), lax.axis_index("expert")
    nz = ns // 2
    hops, back = nz // 2, nz - 1 - nz // 2
    ny, nx = product.shape[0], product.shape[1]
    ey, ex = expert // nx, lax.rem(expert, nx)
    plane, core = seq // 2, lax.rem(seq, 2)
    right = lax.rem(plane + 1, nz) * 2 + core
    left = lax.rem(plane + nz - 1, nz) * 2 + core
    sibling = {"seq": plane * 2 + 1 - core}
    rank = dtw_ref.shape[0]
    tokens, channels = x_ref.shape
    state_n = rates_ref.shape[0]
    own, width = hid_ref.shape
    half = width // 2
    low, high = pl.ds(0, half), pl.ds(half, half)
    blocks = tokens // (2 * BLOCK)
    span = 2 * BLOCK
    columns = w_ref.shape[1]
    count = ne * cap
    units = wg_ref.shape[0]
    pieces = width // 128

    def loop(start, stop, action):
        def step(i, carry):
            action(i)
            return carry

        lax.fori_loop(start, stop, step, 0)

    def ring_copy(stage, forward):
        side, to = (0, right) if forward else (1, left)
        index = lax.rem(plane + (nz - stage + 1 if forward else stage - 1), nz) * 2 + core
        return remote(
            wf.at[index], wf.at[index], ring_send.at[side, stage - 1], ring_recv.at[side, stage - 1], {"seq": to}
        )

    def sibling_copy(index):
        return remote(wf.at[index], wf.at[index], sib_send.at[index // 2], sib_recv.at[index // 2], sibling)

    def ring_stage(stage):
        if 1 < stage <= hops + 1:
            ring_copy(stage - 1, True).wait_recv()
            sibling_copy(lax.rem(plane + nz - (stage - 1), nz) * 2 + core).start()
        if 1 < stage <= back + 1:
            ring_copy(stage - 1, False).wait_recv()
            sibling_copy(lax.rem(plane + stage - 1, nz) * 2 + core).start()
        if stage <= hops:
            ring_copy(stage, True).start()
        if stage <= back:
            ring_copy(stage, False).start()

    with jax.named_scope("greet"):
        weights = ((wg_ref, gate_w), (wu_ref, up_w), (wd_ref, down_w))
        loads = [
            pltpu.make_async_copy(src, dst.at[pl.ds(0, units)], load_sem.at[i])
            for i, (src, dst) in enumerate(weights)
        ]
        for copy in loads:
            copy.start()
        wf[seq] = w_ref[...]
        greet(ns, ne, seq, expert)
        ring_stage(1)
        sibling_copy(seq).start()

    with jax.named_scope("proj"):
        partial = lax.dot_general(
            x_ref[...], xp_ref[...], (((1,), (1,)), ((), ())), preferred_element_type=F32
        ).astype(BF16)
        spare = part.shape[2] - partial.shape[1]
        part[...] = jnp.concatenate([partial, jnp.zeros((tokens, spare), BF16)], axis=1).reshape(part.shape)

        def part_copy(o):
            to = lax.rem(expert + o, ne)
            return remote(part.at[to], part_in.at[o - 1], p1_send.at[o - 1], p1_recv.at[o - 1], {"expert": to})

        loop(1, ne, lambda o: part_copy(o).start())
        pairs = [
            remote(src, dst.at[pl.ds(units, units)], pair_send.at[i], pair_recv.at[i], sibling)
            for i, (src, dst) in enumerate(weights)
        ]

        def add_part(o, acc):
            part_copy(o).wait_recv()
            return acc + part_in[o - 1].astype(F32)

        summed = lax.fori_loop(1, ne, add_part, part[expert].astype(F32))
        part_sum[...] = summed.astype(BF16)
        proj[expert] = part_sum[...]

        def proj_copy(o):
            to = lax.rem(expert + o, ne)
            return remote(part_sum, proj.at[expert], p2_send.at[o - 1], p2_recv.at[o - 1], {"expert": to})

        loop(1, ne, lambda o: proj_copy(o).start())
        ring_stage(2)
        loop(1, ne, lambda o: proj_copy(o).wait_recv())

    with jax.named_scope("sizes"):
        proj_all = proj[...].reshape(tokens, proj.shape[2])
        raw = jnp.dot(proj_all[:, :rank], dtw_ref[...], preferred_element_type=F32) + dtb_ref[...]
        sizes[...] = jnp.maximum(raw, 0.0) + jnp.log1p(jnp.exp(-jnp.abs(raw)))
        turned = proj_all[:, rank:].astype(F32).T
        for b in range(blocks):
            bc[b, :, :span] = turned[: 2 * state_n, b * span : (b + 1) * span]

    with jax.named_scope("scan"):
        rates = -rates_ref[...]
        zero_state = jnp.zeros((state_n, channels), F32)
        zero_row = jnp.zeros((1, channels), F32)

        def scan_block(b, carry):
            states, sums = [carry[0], carry[1]], [carry[2], carry[3]]
            first = pl.multiple_of(b * span, span)
            size_block = sizes[pl.ds(first, span), :]
            drive_block = size_block * x_ref[pl.ds(first, span), :].astype(F32)
            terms = bc[b]
            for r in range(span):
                d = r % 2
                size = size_block[r : r + 1]
                states[d] = (
                    jnp.exp(size * rates) * states[d] + drive_block[r : r + 1] * terms[:state_n, r : r + 1]
                )
                reading[pl.ds(first + r, 1), :] = jnp.sum(
                    states[d] * terms[state_n : 2 * state_n, r : r + 1], axis=0, keepdims=True
                )
                sums[d] = sums[d] + size
                running[pl.ds(first + r, 1), :] = sums[d]
            return states[0], states[1], sums[0], sums[1]

        end0, end1, sum0, sum1 = lax.fori_loop(
            0, blocks, scan_block, (zero_state, zero_state, zero_row, zero_row)
        )
        state[:state_n, :] = end0
        state[state_n : 2 * state_n, :] = end1
        state[2 * state_n : 2 * state_n + 8, :] = jnp.concatenate(
            [sum0, sum1, jnp.zeros((6, channels), F32)], axis=0
        )

    with jax.named_scope("states"):
        side = channels // 2
        mine = pl.ds(pl.multiple_of(core * side, side), side)
        other = pl.ds(pl.multiple_of((1 - core) * side, side), side)
        half_copy = remote(state.at[:, other], state_sib, h_send.at[0], h_recv.at[0], sibling)
        half_copy.start()
        ring_stage(3)
        rates_mine = -rates_ref[:, mine]

        def through(message, d):
            return jnp.exp(message[2 * state_n + d : 2 * state_n + d + 1] * rates_mine)

        def ends(message, d):
            return message[d * state_n : (d + 1) * state_n]

        half_copy.wait_recv()
        first_core = core == 0
        here, there = state[:, mine], state_sib[...]
        early = jnp.where(first_core, here, there)
        late = jnp.where(first_core, there, here)
        for d in range(2):
            state_chip[d * state_n : (d + 1) * state_n, :] = through(late, d) * ends(early, d) + ends(late, d)
        state_chip[2 * state_n :, :] = early[2 * state_n :] + late[2 * state_n :]

        def state_copy(to, source):
            return remote(state_chip, state_in.at[source], s_send.at[to], s_recv.at[source], {"seq": to * 2 + core})

        loop(plane + 1, nz, lambda to: state_copy(to, plane).start())
        for copy in pairs:
            copy.start()

        def horner(source, carry):
            state_copy(plane, source).wait_recv()
            message = state_in[source]
            return tuple(through(message, d) * carry[d] + ends(message, d) for d in range(2))

        zero_half = jnp.zeros((state_n, side), F32)
        entering = lax.fori_loop(0, plane, horner, (zero_half, zero_half))
        for d in range(2):
            passed = through(early, d) * entering[d] + ends(early, d)
            state_sib[d * state_n : (d + 1) * state_n, :] = jnp.where(first_core, passed, entering[d])
            incoming[d * state_n : (d + 1) * state_n, mine] = jnp.where(first_core, entering[d], passed)
        enter_copy = remote(
            state_sib.at[pl.ds(0, 2 * state_n)], incoming.at[:, mine], h_send.at[1], h_recv.at[1], sibling
        )
        enter_copy.start()
        for stage in range(4, hops + 2):
            ring_stage(stage)
        enter_copy.wait_recv()

    with jax.named_scope("gate"):
        skip = skip_ref[...]
        entered = [incoming[d * state_n : (d + 1) * state_n, :] for d in range(2)]

        def gate_block(b):
            first = pl.multiple_of(b * span, span)
            sum_block = running[pl.ds(first, span), :]
            terms = bc[b]
            for r in range(span):
                carried = jnp.exp(sum_block[r : r + 1] * rates) * entered[r % 2]
                reading[pl.ds(first + r, 1), :] += jnp.sum(
                    carried * terms[state_n : 2 * state_n, r : r + 1], axis=0, keepdims=True
                )
            drive = x_ref[pl.ds(first, span), :].astype(F32)
            gate = z_ref[pl.ds(first, span), :].astype(F32)
            value = (reading[pl.ds(first, span), :] + skip * drive) * (gate / (1.0 + jnp.exp(-gate)))
            gated[pl.ds(first, span), :] = value.astype(BF16)

        loop(0, blocks, gate_block)

    with jax.named_scope("project"):
        loop(0, nz, lambda i: sibling_copy(2 * i + 1 - core).wait_recv())

        def multiply(b):
            at = pl.multiple_of(b * columns, columns)
            out = jnp.dot(gated[...], wf[b], preferred_element_type=F32).astype(BF16)
            product[:, :, :, pl.ds(at, columns)] = out.reshape(ny, nx, own, columns)

        def row_copy(o):
            to = lax.rem(ex + o, nx)
            return remote(
                product.at[:, to, :, low], row_in.at[o - 1], a_send.at[0, o - 1], a_recv.at[0, o - 1],
                {"expert": ey * nx + to},
            )

        def col_copy(o):
            to = lax.rem(ey + o, ny)
            return remote(
                product.at[to, :, :, high], col_in.at[o - 1], b_send.at[0, o - 1], b_recv.at[0, o - 1],
                {"expert": to * nx + ex},
            )

        def row_pass(o):
            to = lax.rem(ey + o, ny)
            return remote(
                row_sum.at[to], row_last.at[o - 1], a_send.at[1, o - 1], a_recv.at[1, o - 1],
                {"expert": to * nx + ex},
            )

        def col_pass(o):
            to = lax.rem(ex + o, nx)
            return remote(
                col_sum.at[to], col_last.at[o - 1], b_send.at[1, o - 1], b_recv.at[1, o - 1],
                {"expert": ey * nx + to},
            )

        loop(0, ns // 2, multiply)
        loop(1, nx, lambda o: row_copy(o).start())
        loop(ns // 2, ns, multiply)
        loop(1, ny, lambda o: col_copy(o).start())
        loop(1, nx, lambda o: row_copy(o).wait_recv())

        def add_row(i):
            acc = product[i, ex, :, low].astype(F32)
            for o in range(nx - 1):
                acc = acc + row_in[o, i].astype(F32)
            row_sum[i] = acc.astype(BF16)

        loop(0, ny, add_row)
        loop(1, ny, lambda o: row_pass(o).start())
        loop(1, ny, lambda o: col_copy(o).wait_recv())

        def add_col(i):
            acc = product[ey, i, :, high].astype(F32)
            for o in range(ny - 1):
                acc = acc + col_in[o, i].astype(F32)
            col_sum[i] = acc.astype(BF16)

        loop(0, nx, add_col)
        loop(1, nx, lambda o: col_pass(o).start())
        loop(1, ny, lambda o: row_pass(o).wait_recv())
        acc = hid_ref[:, low].astype(F32) + row_sum[ey].astype(F32)
        for o in range(ny - 1):
            acc = acc + row_last[o].astype(F32)
        wide[:, low] = acc.astype(BF16).astype(F32)
        loop(1, nx, lambda o: col_pass(o).wait_recv())
        acc = hid_ref[:, high].astype(F32) + col_sum[ex].astype(F32)
        for o in range(nx - 1):
            acc = acc + col_last[o].astype(F32)
        wide[:, high] = acc.astype(BF16).astype(F32)

    def spread(value_of, target):
        for j in range(pieces):
            flat[pl.ds(j, count, stride=pieces), :] = value_of(j)
        target[...] = flat[...].astype(BF16).reshape(target.shape)

    def gather_pieces(source, target):
        flat[...] = source[...].astype(F32).reshape(flat.shape)
        for j in range(pieces):
            target[:, j * 128 : (j + 1) * 128] = flat[pl.ds(j, count, stride=pieces), :].astype(BF16)

    with jax.named_scope("route"):
        mixed = wide[...]
        mean = jnp.mean(mixed * mixed, axis=-1, keepdims=True)
        normed = (mixed * lax.rsqrt(mean + EPS) * gain_ref[...]).astype(BF16)
        spread(
            lambda j: jnp.dot(
                place_ref[...], normed[:, j * 128 : (j + 1) * 128], preferred_element_type=F32
            ),
            packed_out,
        )

        def send_rows(o):
            to = lax.rem(expert + o, ne)
            return remote(
                packed_out.at[to], packed_in.at[expert], d_send.at[o - 1], d_recv.at[o - 1], {"expert": to}
            )

        loop(1, ne, lambda o: send_rows(o).start())
        packed_in[expert] = packed_out[expert]
        logits = lax.dot_general(
            normed, router_ref[...], (((1,), (1,)), ((), ())), preferred_element_type=F32
        )
        scores = []
        for k in range(pick_ref.shape[0]):
            picked = jnp.sum(pick_ref[k] * logits, axis=-1, keepdims=True)
            scores.append(1.0 / (1.0 + jnp.exp(-picked)))
        all_scores = sum(scores)
        combine_w[...] = sum((score / all_scores) * put_ref[k] for k, score in enumerate(scores))
        loop(1, ne, lambda o: send_rows(o).wait_recv())
        gather_pieces(packed_in, held.at[0])

    def gather_copy(stage, forward):
        way = 0 if forward else 1
        source = held.at[2 * (stage - 1) + (0 if forward or stage == 1 else 1)]
        if stage < hops:
            target = held.at[2 * stage + way]
        else:
            picked = low if forward else high
            source, target = source.at[:, picked], held.at[1, :, picked]
        return remote(
            source, target, g_send.at[way, stage - 1], g_recv.at[way, stage - 1], {"seq": right if forward else left}
        )

    def return_copy(stage, forward):
        way = 0 if forward else 1
        buffer = from_left if forward else from_right
        distance = hops - stage + 1
        if stage == 1:
            picked = low if forward else high
            source, target = parts.at[1, :, picked], buffer.at[0, :, picked]
        else:
            source, target = parts.at[2 * distance + (1 if forward else 0)], buffer.at[stage - 1]
        return remote(
            source, target, r_send.at[way, stage - 1], r_recv.at[way, stage - 1], {"seq": right if forward else left}
        )

    def compute(pair):
        rows = held[2 * pair : 2 * pair + 2].reshape(2 * count, width)
        across = (((1,), (1,)), ((), ()))
        gate = lax.dot_general(rows, gate_w[...], across, preferred_element_type=F32)
        up = lax.dot_general(rows, up_w[...], across, preferred_element_type=F32)
        hidden[...] = (gate / (1.0 + jnp.exp(-gate)) * up).astype(BF16)
        step = min(width, 512)

        def down(b):
            at = pl.multiple_of(b * step, step)
            out = jnp.dot(hidden[...], down_w[:, pl.ds(at, step)], preferred_element_type=F32)
            parts[2 * pair : 2 * pair + 2, :, pl.ds(at, step)] = out.astype(BF16).reshape(2, count, step)

        loop(0, width // step, down)

    with jax.named_scope("experts"):
        gather_copy(1, True).start()
        gather_copy(1, False).start()
        for copy in loads:
            copy.wait()
        for copy in pairs:
            copy.wait_recv()
        for stage in range(1, hops + 1):
            gather_copy(stage, True).wait_recv()
            gather_copy(stage, False).wait_recv()
            if stage < hops:
                gather_copy(stage + 1, True).start()
                gather_copy(stage + 1, False).start()
            compute(stage if stage < hops else 0)

    with jax.named_scope("combine"):
        return_copy(1, True).start()
        return_copy(1, False).start()
        for stage in range(2, hops + 1):
            distance = hops - stage + 1
            for forward, buffer in ((True, from_left), (False, from_right)):
                return_copy(stage - 1, forward).wait_recv()
                slot = 2 * distance + (1 if forward else 0)
                picked = pl.ds(0, width) if stage > 2 else low if forward else high
                parts[slot, :, picked] = (
                    parts[slot, :, picked].astype(F32) + buffer[stage - 2, :, picked].astype(F32)
                ).astype(BF16)
                return_copy(stage, forward).start()
        return_copy(hops, True).wait_recv()
        return_copy(hops, False).wait_recv()

    with jax.named_scope("home"):

        def summed_piece(j):
            at = pl.ds(j * 128, 128)
            value = parts[0, :, at].astype(F32)
            if hops > 1 or j < pieces // 2:
                value = value + from_left[hops - 1, :, at].astype(F32)
            if hops > 1 or j >= pieces // 2:
                value = value + from_right[hops - 1, :, at].astype(F32)
            return value

        spread(summed_piece, back_out)

        def send_back(o):
            to = lax.rem(expert + o, ne)
            return remote(
                back_out.at[to], back_in.at[expert], e_send.at[o - 1], e_recv.at[o - 1], {"expert": to}
            )

        loop(1, ne, lambda o: send_back(o).start())
        back_in[expert] = back_out[expert]
        loop(1, ne, lambda o: send_back(o).wait_recv())
        gather_pieces(back_in, returned)
        weights_high = combine_w[...].astype(BF16)
        weights_low = (combine_w[...] - weights_high.astype(F32)).astype(BF16)
        routed = jnp.dot(weights_high, returned[...], preferred_element_type=F32) + jnp.dot(
            weights_low, returned[...], preferred_element_type=F32
        )
        out_ref[...] = (wide[...] + routed).astype(BF16)

    with jax.named_scope("finish"):

        def sent_peers(o):
            part_copy(o).wait_send()
            proj_copy(o).wait_send()
            send_rows(o).wait_send()
            send_back(o).wait_send()

        loop(1, ne, sent_peers)

        def sent_rows(o):
            row_copy(o).wait_send()
            col_pass(o).wait_send()

        def sent_cols(o):
            col_copy(o).wait_send()
            row_pass(o).wait_send()

        loop(1, nx, sent_rows)
        loop(1, ny, sent_cols)
        loop(plane + 1, nz, lambda to: state_copy(to, plane).wait_send())
        half_copy.wait_send()
        enter_copy.wait_send()
        for stage in range(1, hops + 1):
            ring_copy(stage, True).wait_send()
            for forward in (True, False):
                gather_copy(stage, forward).wait_send()
                return_copy(stage, forward).wait_send()
        for stage in range(1, back + 1):
            ring_copy(stage, False).wait_send()
        loop(0, nz, lambda i: sibling_copy(2 * i + core).wait_send())
        for copy in pairs:
            copy.wait_send()


def layer_call(
    ns, ne, cap, x, z, xp, dtw, dtb, rates, skip, w, hid, gain, router, place, pick, put, wg, wu, wd
):
    tokens, channels = x.shape
    own, width = hid.shape
    state_n = rates.shape[0]
    lanes = -(-xp.shape[0] // 128) * 128
    nz = ns // 2
    hops = nz // 2
    ny = 4 if ne == 16 else 2
    nx = ne // ny
    half = width // 2
    units = wg.shape[0]
    count = ne * cap
    pieces = width // 128
    dma = pltpu.SemaphoreType.DMA
    vmem = pltpu.VMEM
    return pl.pallas_call(
        functools.partial(layer_kernel, ns, ne, cap),
        out_shape=jax.ShapeDtypeStruct((own, width), BF16),
        in_specs=[VMEM] * 14 + [HBM] * 3,
        out_specs=VMEM,
        scratch_shapes=[
            vmem((ne, own, lanes), BF16),
            vmem((ne - 1, own, lanes), BF16),
            vmem((own, lanes), BF16),
            vmem((ne, own, lanes), BF16),
            vmem((tokens, channels), F32),
            vmem((tokens, channels), F32),
            vmem((tokens, channels), F32),
            vmem((tokens // (2 * BLOCK), 2 * state_n, 128), F32),
            vmem((2 * state_n + 8, channels), F32),
            vmem((2 * state_n + 8, channels // 2), F32),
            vmem((2 * state_n + 8, channels // 2), F32),
            vmem((nz, 2 * state_n + 8, channels // 2), F32),
            vmem((2 * state_n, channels), F32),
            vmem((tokens, channels), BF16),
            vmem((ns,) + w.shape, BF16),
            vmem((ny, nx, own, width), BF16),
            vmem((nx - 1, ny, own, half), BF16),
            vmem((ny, own, half), BF16),
            vmem((ny - 1, own, half), BF16),
            vmem((ny - 1, nx, own, half), BF16),
            vmem((nx, own, half), BF16),
            vmem((nx - 1, own, half), BF16),
            vmem((own, width), F32),
            vmem((own, count), F32),
            vmem((count * pieces, 128), F32),
            vmem((ne, cap * pieces, 128), BF16),
            vmem((ne, cap * pieces, 128), BF16),
            vmem((ne, cap * pieces, 128), BF16),
            vmem((ne, cap * pieces, 128), BF16),
            vmem((count, width), BF16),
            vmem((nz, count, width), BF16),
            vmem((nz, count, width), BF16),
            vmem((hops, count, width), BF16),
            vmem((hops, count, width), BF16),
            vmem((2 * units, width), BF16),
            vmem((2 * units, width), BF16),
            vmem((2 * units, width), BF16),
            vmem((2 * count, 2 * units), BF16),
            dma((3,)),
            dma((3,)), dma((3,)),
            dma((ne - 1,)), dma((ne - 1,)),
            dma((ne - 1,)), dma((ne - 1,)),
            dma((2,)), dma((2,)),
            dma((nz,)), dma((nz,)),
            dma((2, hops)), dma((2, hops)),
            dma((nz,)), dma((nz,)),
            dma((2, nx + ny)), dma((2, nx + ny)),
            dma((2, nx + ny)), dma((2, nx + ny)),
            dma((ne - 1,)), dma((ne - 1,)),
            dma((ne - 1,)), dma((ne - 1,)),
            dma((2, hops)), dma((2, hops)),
            dma((2, hops)), dma((2, hops)),
        ],
        compiler_params=pltpu.CompilerParams(
            collective_id=0, has_side_effects=True, vmem_limit_bytes=58 * 1024 * 1024
        ),
    )(x, z, xp, dtw, dtb, rates, skip, w, hid, gain, router, place, pick, put, wg, wu, wd)


def body(
    hidden_in,
    mamba_x,
    mamba_z,
    x_proj,
    dt_weight,
    dt_bias,
    state_rates,
    skip_gain,
    out_weight,
    norm_gain,
    router_weight,
    expert_ids,
    w_gate,
    w_up,
    w_down,
):
    ns, ne = lax.axis_size("seq"), lax.axis_size("expert")
    slice_len, docs, channels = mamba_x.shape
    model_width = hidden_in.shape[2]
    token_rows = hidden_in.shape[0] * docs
    experts = router_weight.shape[1]
    top_count = expert_ids.shape[2]
    capacity = max(2, min(token_rows, token_rows * top_count * 5 // (2 * experts)))
    chosen_ids = expert_ids.reshape(token_rows, top_count)
    expert_range = jnp.arange(experts, dtype=jnp.int32)
    flat_ids = chosen_ids.reshape(-1)
    marks = (flat_ids[:, None] == expert_range[None, :]).astype(jnp.int32)
    slots = jnp.sum((jnp.cumsum(marks, axis=0) - 1) * marks, axis=1)
    targets = (flat_ids * capacity + slots).reshape(token_rows, top_count)
    places = jnp.arange(experts * capacity, dtype=jnp.int32)
    place = jnp.any(places[:, None, None] == targets[None], axis=2).astype(jnp.bfloat16)
    pick = (chosen_ids.T[:, :, None] == expert_range).astype(jnp.float32)
    put = (targets.T[:, :, None] == places).astype(jnp.float32)
    result = layer_call(
        ns,
        ne,
        capacity,
        mamba_x.reshape(slice_len * docs, channels),
        mamba_z.reshape(slice_len * docs, channels),
        x_proj.T,
        dt_weight,
        dt_bias[None],
        state_rates.T,
        skip_gain[None],
        out_weight,
        hidden_in.reshape(token_rows, model_width),
        norm_gain[None],
        router_weight.T,
        place,
        pick,
        put,
        w_gate[0].T,
        w_up[0].T,
        w_down[0].T,
    )
    return result.reshape(hidden_in.shape)


def solution(mesh):
    placed = (
        P(("seq", "expert"), None, None),
        P("seq", None, "expert"),
        P("seq", None, "expert"),
        P("expert", None),
        P(None, "expert"),
        P("expert"),
        P("expert", None),
        P("expert"),
        P("expert", "seq"),
        P(),
        P(),
        P(("seq", "expert"), None, None),
        P("expert", None, "seq"),
        P("expert", None, "seq"),
        P("expert", None, "seq"),
    )
    return jax.shard_map(
        body,
        mesh=mesh,
        in_specs=placed,
        out_specs=P(("seq", "expert"), None, None),
        check_vma=False,
    )
```

```python
import functools

import jax
import jax.numpy as jnp
from jax import lax
from jax.experimental import pallas as pl
from jax.experimental.pallas import tpu as pltpu
from jax.sharding import PartitionSpec as P

EPS = 1e-05
F32 = jnp.float32
BF16 = jnp.bfloat16
BLOCK = 16
VMEM = pl.BlockSpec(memory_space=pltpu.VMEM)
HBM = pl.BlockSpec(memory_space=pl.ANY)


def remote(src, dst, send, recv, where):
    return pltpu.make_async_remote_copy(
        src_ref=src,
        dst_ref=dst,
        send_sem=send,
        recv_sem=recv,
        device_id=where,
        device_id_type=pl.DeviceIdType.MESH,
    )


def greet(ns, ne, seq, expert):
    barrier = pltpu.get_barrier_semaphore()

    def to_seq(o, _):
        pl.semaphore_signal(
            barrier, inc=1, device_id={"seq": lax.rem(seq + o, ns)}, device_id_type=pl.DeviceIdType.MESH
        )
        return 0

    def to_expert(o, _):
        pl.semaphore_signal(
            barrier, inc=1, device_id={"expert": lax.rem(expert + o, ne)}, device_id_type=pl.DeviceIdType.MESH
        )
        return 0

    lax.fori_loop(1, ns, to_seq, 0)
    lax.fori_loop(1, ne, to_expert, 0)
    pl.semaphore_wait(barrier, ns + ne - 2)


def layer_kernel(
    ns, ne, cap,
    x_in, z_in, xp_ref, dtw_ref, dtb_ref, rates_ref, skip_ref, w_ref, hid_in,
    gain_ref, router_ref, ids_ref, wg_ref, wu_ref, wd_ref,
    out_ref,
    x_ref, z_ref, hid_ref, place_ref, pick_ref, put_ref,
    part, part_in, part_sum, proj, sizes, running, reading, bc,
    state, state_sib, state_chip, state_in, incoming, gated, wf,
    product, row_in, row_sum, row_last, col_in, col_sum, col_last,
    wide, combine_w, flat, packed_out, packed_in, back_out, back_in, returned,
    held, parts, from_left, from_right, gate_w, up_w, down_w, hidden,
    load_sem, pair_send, pair_recv, p1_send, p1_recv, p2_send, p2_recv,
    h_send, h_recv, s_send, s_recv, ring_send, ring_recv, sib_send, sib_recv,
    a_send, a_recv, b_send, b_recv, d_send, d_recv, e_send, e_recv,
    g_send, g_recv, r_send, r_recv,
):
    seq, expert = lax.axis_index("seq"), lax.axis_index("expert")
    nz = ns // 2
    hops, back = nz // 2, nz - 1 - nz // 2
    ny, nx = product.shape[0], product.shape[1]
    ey, ex = expert // nx, lax.rem(expert, nx)
    plane, core = seq // 2, lax.rem(seq, 2)
    right = lax.rem(plane + 1, nz) * 2 + core
    left = lax.rem(plane + nz - 1, nz) * 2 + core
    sibling = {"seq": plane * 2 + 1 - core}
    rank = dtw_ref.shape[0]
    tokens, channels = x_ref.shape
    state_n = rates_ref.shape[0]
    own, width = hid_ref.shape
    half = width // 2
    low, high = pl.ds(0, half), pl.ds(half, half)
    blocks = tokens // (2 * BLOCK)
    span = 2 * BLOCK
    columns = w_ref.shape[1]
    count = ne * cap
    units = wg_ref.shape[0]
    pieces = width // 128

    def loop(start, stop, action):
        def step(i, carry):
            action(i)
            return carry

        lax.fori_loop(start, stop, step, 0)

    def ring_copy(stage, forward):
        side, to = (0, right) if forward else (1, left)
        index = lax.rem(plane + (nz - stage + 1 if forward else stage - 1), nz) * 2 + core
        return remote(
            wf.at[index], wf.at[index], ring_send.at[side, stage - 1], ring_recv.at[side, stage - 1], {"seq": to}
        )

    def sibling_copy(index):
        return remote(wf.at[index], wf.at[index], sib_send.at[index // 2], sib_recv.at[index // 2], sibling)

    def ring_stage(stage):
        if 1 < stage <= hops + 1:
            ring_copy(stage - 1, True).wait_recv()
            sibling_copy(lax.rem(plane + nz - (stage - 1), nz) * 2 + core).start()
        if 1 < stage <= back + 1:
            ring_copy(stage - 1, False).wait_recv()
            sibling_copy(lax.rem(plane + stage - 1, nz) * 2 + core).start()
        if stage <= hops:
            ring_copy(stage, True).start()
        if stage <= back:
            ring_copy(stage, False).start()

    def choose():
        docs, picks, positions = ids_ref.shape

        def grid(shape, axis):
            return lax.broadcasted_iota(jnp.int32, shape, axis)

        chosen, marks = [], []
        for k in range(picks):
            found = jnp.zeros((own, 1), F32)
            for d in range(docs):
                here = grid((own, positions), 0) == grid((own, positions), 1) * docs + d
                row = ids_ref[d, k : k + 1, :].astype(F32)
                found = found + jnp.sum(jnp.where(here, row, 0.0), axis=1, keepdims=True)
            chosen.append(found)
            marks.append((grid((own, ne), 1).astype(F32) == found).astype(F32))
            pick_ref[k] = marks[k]
        before = (grid((own, own), 0) > grid((own, own), 1)).astype(BF16)
        taken = jnp.dot(before, sum(marks).astype(BF16), preferred_element_type=F32)
        for k in range(picks):
            slot = jnp.sum(marks[k] * taken, axis=1, keepdims=True)
            target = chosen[k] * cap + slot
            put_ref[k] = (grid((own, count), 1).astype(F32) == target).astype(F32)
        eye = (grid((own, own), 0) == grid((own, own), 1)).astype(BF16)
        place_ref[...] = lax.dot_general(
            (put_ref[0] + put_ref[1]).astype(BF16), eye, (((0,), (0,)), ((), ())), preferred_element_type=F32
        ).astype(BF16)

    with jax.named_scope("greet"):
        weights = ((wg_ref, gate_w), (wu_ref, up_w), (wd_ref, down_w))
        loads = [
            pltpu.make_async_copy(src, dst.at[pl.ds(0, units)], load_sem.at[i])
            for i, (src, dst) in enumerate(weights)
        ]
        for copy in loads:
            copy.start()
        wf[seq] = w_ref[...]
        x_ref[...] = x_in[...].reshape(tokens, channels)
        greet(ns, ne, seq, expert)
        ring_stage(1)
        sibling_copy(seq).start()

    with jax.named_scope("proj"):
        partial = lax.dot_general(
            x_ref[...], xp_ref[...], (((1,), (1,)), ((), ())), preferred_element_type=F32
        ).astype(BF16)
        spare = part.shape[2] - partial.shape[1]
        part[...] = jnp.concatenate([partial, jnp.zeros((tokens, spare), BF16)], axis=1).reshape(part.shape)

        def part_copy(o):
            to = lax.rem(expert + o, ne)
            return remote(part.at[to], part_in.at[o - 1], p1_send.at[o - 1], p1_recv.at[o - 1], {"expert": to})

        loop(1, ne, lambda o: part_copy(o).start())
        pairs = [
            remote(src, dst.at[pl.ds(units, units)], pair_send.at[i], pair_recv.at[i], sibling)
            for i, (src, dst) in enumerate(weights)
        ]

        z_ref[...] = z_in[...].reshape(tokens, channels)
        hid_ref[...] = hid_in[...].reshape(own, width)

        def add_part(o, acc):
            part_copy(o).wait_recv()
            return acc + part_in[o - 1].astype(F32)

        summed = lax.fori_loop(1, ne, add_part, part[expert].astype(F32))
        part_sum[...] = summed.astype(BF16)
        proj[expert] = part_sum[...]

        def proj_copy(o):
            to = lax.rem(expert + o, ne)
            return remote(part_sum, proj.at[expert], p2_send.at[o - 1], p2_recv.at[o - 1], {"expert": to})

        loop(1, ne, lambda o: proj_copy(o).start())
        ring_stage(2)
        choose()
        loop(1, ne, lambda o: proj_copy(o).wait_recv())

    with jax.named_scope("sizes"):
        proj_all = proj[...].reshape(tokens, proj.shape[2])
        raw = jnp.dot(proj_all[:, :rank], dtw_ref[...], preferred_element_type=F32) + dtb_ref[...]
        sizes[...] = jnp.maximum(raw, 0.0) + jnp.log1p(jnp.exp(-jnp.abs(raw)))
        turned = proj_all[:, rank:].astype(F32).T
        for b in range(blocks):
            bc[b, :, :span] = turned[: 2 * state_n, b * span : (b + 1) * span]

    with jax.named_scope("scan"):
        rates = -rates_ref[...]
        zero_state = jnp.zeros((state_n, channels), F32)
        zero_row = jnp.zeros((1, channels), F32)

        def scan_block(b, carry):
            states, sums = [carry[0], carry[1]], [carry[2], carry[3]]
            first = pl.multiple_of(b * span, span)
            size_block = sizes[pl.ds(first, span), :]
            drive_block = size_block * x_ref[pl.ds(first, span), :].astype(F32)
            terms = bc[b]
            for r in range(span):
                d = r % 2
                size = size_block[r : r + 1]
                states[d] = (
                    jnp.exp(size * rates) * states[d] + drive_block[r : r + 1] * terms[:state_n, r : r + 1]
                )
                reading[pl.ds(first + r, 1), :] = jnp.sum(
                    states[d] * terms[state_n : 2 * state_n, r : r + 1], axis=0, keepdims=True
                )
                sums[d] = sums[d] + size
                running[pl.ds(first + r, 1), :] = sums[d]
            return states[0], states[1], sums[0], sums[1]

        end0, end1, sum0, sum1 = lax.fori_loop(
            0, blocks, scan_block, (zero_state, zero_state, zero_row, zero_row)
        )
        state[:state_n, :] = end0
        state[state_n : 2 * state_n, :] = end1
        state[2 * state_n : 2 * state_n + 8, :] = jnp.concatenate(
            [sum0, sum1, jnp.zeros((6, channels), F32)], axis=0
        )

    with jax.named_scope("states"):
        side = channels // 2
        mine = pl.ds(pl.multiple_of(core * side, side), side)
        other = pl.ds(pl.multiple_of((1 - core) * side, side), side)
        half_copy = remote(state.at[:, other], state_sib, h_send.at[0], h_recv.at[0], sibling)
        half_copy.start()
        ring_stage(3)
        rates_mine = -rates_ref[:, mine]

        def through(message, d):
            return jnp.exp(message[2 * state_n + d : 2 * state_n + d + 1] * rates_mine)

        def ends(message, d):
            return message[d * state_n : (d + 1) * state_n]

        half_copy.wait_recv()
        first_core = core == 0
        here, there = state[:, mine], state_sib[...]
        early = jnp.where(first_core, here, there)
        late = jnp.where(first_core, there, here)
        for d in range(2):
            state_chip[d * state_n : (d + 1) * state_n, :] = through(late, d) * ends(early, d) + ends(late, d)
        state_chip[2 * state_n :, :] = early[2 * state_n :] + late[2 * state_n :]

        def state_copy(to, source):
            return remote(state_chip, state_in.at[source], s_send.at[to], s_recv.at[source], {"seq": to * 2 + core})

        loop(plane + 1, nz, lambda to: state_copy(to, plane).start())

        def horner(source, carry):
            state_copy(plane, source).wait_recv()
            message = state_in[source]
            return tuple(through(message, d) * carry[d] + ends(message, d) for d in range(2))

        zero_half = jnp.zeros((state_n, side), F32)
        entering = lax.fori_loop(0, plane, horner, (zero_half, zero_half))
        for d in range(2):
            passed = through(early, d) * entering[d] + ends(early, d)
            state_sib[d * state_n : (d + 1) * state_n, :] = jnp.where(first_core, passed, entering[d])
            incoming[d * state_n : (d + 1) * state_n, mine] = jnp.where(first_core, entering[d], passed)
        enter_copy = remote(
            state_sib.at[pl.ds(0, 2 * state_n)], incoming.at[:, mine], h_send.at[1], h_recv.at[1], sibling
        )
        enter_copy.start()
        for stage in range(4, hops + 2):
            ring_stage(stage)
        for copy in pairs:
            copy.start()
        enter_copy.wait_recv()

    with jax.named_scope("gate"):
        skip = skip_ref[...]
        entered = [incoming[d * state_n : (d + 1) * state_n, :] for d in range(2)]

        def gate_block(b):
            first = pl.multiple_of(b * span, span)
            sum_block = running[pl.ds(first, span), :]
            terms = bc[b]
            for r in range(span):
                carried = jnp.exp(sum_block[r : r + 1] * rates) * entered[r % 2]
                reading[pl.ds(first + r, 1), :] += jnp.sum(
                    carried * terms[state_n : 2 * state_n, r : r + 1], axis=0, keepdims=True
                )
            drive = x_ref[pl.ds(first, span), :].astype(F32)
            gate = z_ref[pl.ds(first, span), :].astype(F32)
            value = (reading[pl.ds(first, span), :] + skip * drive) * (gate / (1.0 + jnp.exp(-gate)))
            gated[pl.ds(first, span), :] = value.astype(BF16)

        loop(0, blocks, gate_block)

    with jax.named_scope("project"):
        loop(0, nz, lambda i: sibling_copy(2 * i + 1 - core).wait_recv())

        def multiply(b):
            at = pl.multiple_of(b * columns, columns)
            out = jnp.dot(gated[...], wf[b], preferred_element_type=F32).astype(BF16)
            product[:, :, :, pl.ds(at, columns)] = out.reshape(ny, nx, own, columns)

        def row_copy(o):
            to = lax.rem(ex + o, nx)
            return remote(
                product.at[:, to, :, low], row_in.at[o - 1], a_send.at[0, o - 1], a_recv.at[0, o - 1],
                {"expert": ey * nx + to},
            )

        def col_copy(o):
            to = lax.rem(ey + o, ny)
            return remote(
                product.at[to, :, :, high], col_in.at[o - 1], b_send.at[0, o - 1], b_recv.at[0, o - 1],
                {"expert": to * nx + ex},
            )

        def row_pass(o):
            to = lax.rem(ey + o, ny)
            return remote(
                row_sum.at[to], row_last.at[o - 1], a_send.at[1, o - 1], a_recv.at[1, o - 1],
                {"expert": to * nx + ex},
            )

        def col_pass(o):
            to = lax.rem(ex + o, nx)
            return remote(
                col_sum.at[to], col_last.at[o - 1], b_send.at[1, o - 1], b_recv.at[1, o - 1],
                {"expert": ey * nx + to},
            )

        loop(0, ns // 2, multiply)
        loop(1, nx, lambda o: row_copy(o).start())
        loop(ns // 2, ns, multiply)
        loop(1, ny, lambda o: col_copy(o).start())
        loop(1, nx, lambda o: row_copy(o).wait_recv())

        def add_row(i):
            acc = product[i, ex, :, low].astype(F32)
            for o in range(nx - 1):
                acc = acc + row_in[o, i].astype(F32)
            row_sum[i] = acc.astype(BF16)

        loop(0, ny, add_row)
        loop(1, ny, lambda o: row_pass(o).start())
        loop(1, ny, lambda o: col_copy(o).wait_recv())

        def add_col(i):
            acc = product[ey, i, :, high].astype(F32)
            for o in range(ny - 1):
                acc = acc + col_in[o, i].astype(F32)
            col_sum[i] = acc.astype(BF16)

        loop(0, nx, add_col)
        loop(1, nx, lambda o: col_pass(o).start())
        loop(1, ny, lambda o: row_pass(o).wait_recv())
        acc = hid_ref[:, low].astype(F32) + row_sum[ey].astype(F32)
        for o in range(ny - 1):
            acc = acc + row_last[o].astype(F32)
        wide[:, low] = acc.astype(BF16).astype(F32)
        loop(1, nx, lambda o: col_pass(o).wait_recv())
        acc = hid_ref[:, high].astype(F32) + col_sum[ex].astype(F32)
        for o in range(nx - 1):
            acc = acc + col_last[o].astype(F32)
        wide[:, high] = acc.astype(BF16).astype(F32)

    sides = (low, high)
    each = pieces // 2

    def spread(value_of, target, h):
        for j in range(each):
            flat[pl.ds(j, count, stride=each), :] = value_of(h * each + j)
        target[h] = flat[...].astype(BF16).reshape(target.shape[1:])

    def gather_pieces(source, target, h):
        flat[...] = source[h].astype(F32).reshape(flat.shape)
        for j in range(each):
            at = h * half + j * 128
            target[:, at : at + 128] = flat[pl.ds(j, count, stride=each), :].astype(BF16)

    with jax.named_scope("route"):
        mixed = wide[...]
        mean = jnp.mean(mixed * mixed, axis=-1, keepdims=True)
        normed = (mixed * lax.rsqrt(mean + EPS) * gain_ref[...]).astype(BF16)

        def send_rows(o, h):
            to = lax.rem(expert + o, ne)
            return remote(
                packed_out.at[h, to], packed_in.at[h, expert], d_send.at[h, o - 1], d_recv.at[h, o - 1],
                {"expert": to},
            )

        def placed(j):
            return jnp.dot(place_ref[...], normed[:, j * 128 : (j + 1) * 128], preferred_element_type=F32)

        for h in range(2):
            spread(placed, packed_out, h)
            loop(1, ne, lambda o: send_rows(o, h).start())
            packed_in[h, expert] = packed_out[h, expert]
        logits = lax.dot_general(
            normed, router_ref[...], (((1,), (1,)), ((), ())), preferred_element_type=F32
        )
        scores = []
        for k in range(pick_ref.shape[0]):
            picked = jnp.sum(pick_ref[k] * logits, axis=-1, keepdims=True)
            scores.append(1.0 / (1.0 + jnp.exp(-picked)))
        all_scores = sum(scores)
        combine_w[...] = sum((score / all_scores) * put_ref[k] for k, score in enumerate(scores))

    def gather_copy(stage, forward, h):
        way = 0 if forward else 1
        source = held.at[2 * (stage - 1) + (0 if forward or stage == 1 else 1), :, sides[h]]
        target = held.at[2 * stage + way if stage < hops else 1, :, sides[h]]
        return remote(
            source, target, g_send.at[way, h, stage - 1], g_recv.at[way, h, stage - 1],
            {"seq": right if forward else left},
        )

    def return_copy(stage, forward, h):
        way = 0 if forward else 1
        buffer = from_left if forward else from_right
        slot = 2 * (hops - stage + 1) + way_of(forward) if stage > 1 else 1
        return remote(
            parts.at[slot, :, sides[h]], buffer.at[stage - 1, :, sides[h]],
            r_send.at[way, h, stage - 1], r_recv.at[way, h, stage - 1], {"seq": right if forward else left},
        )

    def way_of(forward):
        return 1 if forward else 0

    ways = ((True, 0, 1), (False, 1, 0))

    def compute(pair):
        rows = held[2 * pair : 2 * pair + 2].reshape(2 * count, width)
        across = (((1,), (1,)), ((), ()))
        gate = lax.dot_general(rows, gate_w[...], across, preferred_element_type=F32)
        up = lax.dot_general(rows, up_w[...], across, preferred_element_type=F32)
        hidden[...] = (gate / (1.0 + jnp.exp(-gate)) * up).astype(BF16)
        step = min(width, 512)

        def down(b):
            at = pl.multiple_of(b * step, step)
            out = jnp.dot(hidden[...], down_w[:, pl.ds(at, step)], preferred_element_type=F32)
            parts[2 * pair : 2 * pair + 2, :, pl.ds(at, step)] = out.astype(BF16).reshape(2, count, step)

        loop(0, width // step, down)

    with jax.named_scope("experts"):
        for h in range(2):
            loop(1, ne, lambda o: send_rows(o, h).wait_recv())
            gather_pieces(packed_in, held.at[0], h)
            for forward, early, late in ways:
                if hops > 1 or h == early:
                    gather_copy(1, forward, h).start()
        for copy in loads:
            copy.wait()
        for copy in pairs:
            copy.wait_recv()
        for stage in range(1, hops - 1):
            last = stage == hops - 2
            for h in range(2):
                for forward, early, late in ways:
                    gather_copy(stage, forward, h).wait_recv()
                    if not last or h == early:
                        gather_copy(stage + 1, forward, h).start()
            compute(stage)
        for forward, early, late in ways:
            if hops > 1:
                gather_copy(hops - 1, forward, early).wait_recv()
                gather_copy(hops, forward, early).start()
                if hops > 2:
                    gather_copy(hops - 1, forward, late).start()
        for forward, early, late in ways:
            gather_copy(hops, forward, early).wait_recv()
        compute(0)
        for forward, early, late in ways:
            return_copy(1, forward, early).start()
        if hops > 1:
            for forward, early, late in ways:
                gather_copy(hops - 1, forward, late).wait_recv()
            compute(hops - 1)

    with jax.named_scope("combine"):
        for stage in range(2, hops + 1):
            for h in range(2):
                for forward, early, late in ways:
                    if stage > 2 or h == early:
                        return_copy(stage - 1, forward, h).wait_recv()
                        buffer = from_left if forward else from_right
                        slot = 2 * (hops - stage + 1) + way_of(forward)
                        parts[slot, :, sides[h]] = (
                            parts[slot, :, sides[h]].astype(F32) + buffer[stage - 2, :, sides[h]].astype(F32)
                        ).astype(BF16)
                    return_copy(stage, forward, h).start()

    with jax.named_scope("home"):

        def summed_piece(j):
            at = pl.ds(j * 128, 128)
            value = parts[0, :, at].astype(F32)
            for forward, early, late in ways:
                if hops > 1 or j // each == early:
                    buffer = from_left if forward else from_right
                    value = value + buffer[hops - 1, :, at].astype(F32)
            return value

        def send_back(o, h):
            to = lax.rem(expert + o, ne)
            return remote(
                back_out.at[h, to], back_in.at[h, expert], e_send.at[h, o - 1], e_recv.at[h, o - 1],
                {"expert": to},
            )

        for h in range(2):
            for forward, early, late in ways:
                if hops > 1 or h == early:
                    return_copy(hops, forward, h).wait_recv()
            spread(summed_piece, back_out, h)
            loop(1, ne, lambda o: send_back(o, h).start())
            back_in[h, expert] = back_out[h, expert]
        weights_high = combine_w[...].astype(BF16)
        weights_low = (combine_w[...] - weights_high.astype(F32)).astype(BF16)
        for h in range(2):
            loop(1, ne, lambda o: send_back(o, h).wait_recv())
            gather_pieces(back_in, returned, h)
            values = returned[:, sides[h]]
            routed = jnp.dot(weights_high, values, preferred_element_type=F32) + jnp.dot(
                weights_low, values, preferred_element_type=F32
            )
            mixed = (wide[:, sides[h]] + routed).astype(BF16)
            out_ref[:, :, sides[h]] = mixed.reshape(out_ref.shape[:2] + (half,))

    with jax.named_scope("finish"):

        def sent_peers(o):
            part_copy(o).wait_send()
            proj_copy(o).wait_send()
            for h in range(2):
                send_rows(o, h).wait_send()
                send_back(o, h).wait_send()

        loop(1, ne, sent_peers)

        def sent_rows(o):
            row_copy(o).wait_send()
            col_pass(o).wait_send()

        def sent_cols(o):
            col_copy(o).wait_send()
            row_pass(o).wait_send()

        loop(1, nx, sent_rows)
        loop(1, ny, sent_cols)
        loop(plane + 1, nz, lambda to: state_copy(to, plane).wait_send())
        half_copy.wait_send()
        enter_copy.wait_send()
        for stage in range(1, hops + 1):
            ring_copy(stage, True).wait_send()
            for forward, early, late in ways:
                for h in range(2):
                    if stage < hops or h == early:
                        gather_copy(stage, forward, h).wait_send()
                    if stage > 1 or h == early:
                        return_copy(stage, forward, h).wait_send()
        for stage in range(1, back + 1):
            ring_copy(stage, False).wait_send()
        loop(0, nz, lambda i: sibling_copy(2 * i + core).wait_send())
        for copy in pairs:
            copy.wait_send()


def layer_call(
    ns, ne, cap, x, z, xp, dtw, dtb, rates, skip, w, hid, gain, router, ids, wg, wu, wd
):
    tokens, channels = x.shape[0] * x.shape[1], x.shape[2]
    own, width = hid.shape[0] * hid.shape[1], hid.shape[2]
    picks = ids.shape[1]
    state_n = rates.shape[0]
    lanes = -(-xp.shape[0] // 128) * 128
    nz = ns // 2
    hops = nz // 2
    ny = 4 if ne == 16 else 2
    nx = ne // ny
    half = width // 2
    units = wg.shape[0]
    count = ne * cap
    pieces = width // 128
    dma = pltpu.SemaphoreType.DMA
    vmem = pltpu.VMEM
    return pl.pallas_call(
        functools.partial(layer_kernel, ns, ne, cap),
        out_shape=jax.ShapeDtypeStruct(hid.shape, BF16),
        in_specs=[VMEM] * 12 + [HBM] * 3,
        out_specs=VMEM,
        scratch_shapes=[
            vmem((tokens, channels), BF16),
            vmem((tokens, channels), BF16),
            vmem((own, width), BF16),
            vmem((count, own), BF16),
            vmem((picks, own, ne), F32),
            vmem((picks, own, count), F32),
            vmem((ne, own, lanes), BF16),
            vmem((ne - 1, own, lanes), BF16),
            vmem((own, lanes), BF16),
            vmem((ne, own, lanes), BF16),
            vmem((tokens, channels), F32),
            vmem((tokens, channels), F32),
            vmem((tokens, channels), F32),
            vmem((tokens // (2 * BLOCK), 2 * state_n, 128), F32),
            vmem((2 * state_n + 8, channels), F32),
            vmem((2 * state_n + 8, channels // 2), F32),
            vmem((2 * state_n + 8, channels // 2), F32),
            vmem((nz, 2 * state_n + 8, channels // 2), F32),
            vmem((2 * state_n, channels), F32),
            vmem((tokens, channels), BF16),
            vmem((ns,) + w.shape, BF16),
            vmem((ny, nx, own, width), BF16),
            vmem((nx - 1, ny, own, half), BF16),
            vmem((ny, own, half), BF16),
            vmem((ny - 1, own, half), BF16),
            vmem((ny - 1, nx, own, half), BF16),
            vmem((nx, own, half), BF16),
            vmem((nx - 1, own, half), BF16),
            vmem((own, width), F32),
            vmem((own, count), F32),
            vmem((count * pieces // 2, 128), F32),
            vmem((2, ne, cap * pieces // 2, 128), BF16),
            vmem((2, ne, cap * pieces // 2, 128), BF16),
            vmem((2, ne, cap * pieces // 2, 128), BF16),
            vmem((2, ne, cap * pieces // 2, 128), BF16),
            vmem((count, width), BF16),
            vmem((nz, count, width), BF16),
            vmem((nz, count, width), BF16),
            vmem((hops, count, width), BF16),
            vmem((hops, count, width), BF16),
            vmem((2 * units, width), BF16),
            vmem((2 * units, width), BF16),
            vmem((2 * units, width), BF16),
            vmem((2 * count, 2 * units), BF16),
            dma((3,)),
            dma((3,)), dma((3,)),
            dma((ne - 1,)), dma((ne - 1,)),
            dma((ne - 1,)), dma((ne - 1,)),
            dma((2,)), dma((2,)),
            dma((nz,)), dma((nz,)),
            dma((2, hops)), dma((2, hops)),
            dma((nz,)), dma((nz,)),
            dma((2, nx + ny)), dma((2, nx + ny)),
            dma((2, nx + ny)), dma((2, nx + ny)),
            dma((2, ne - 1)), dma((2, ne - 1)),
            dma((2, ne - 1)), dma((2, ne - 1)),
            dma((2, 2, hops)), dma((2, 2, hops)),
            dma((2, 2, hops)), dma((2, 2, hops)),
        ],
        compiler_params=pltpu.CompilerParams(
            collective_id=0, has_side_effects=True, vmem_limit_bytes=58 * 1024 * 1024
        ),
    )(x, z, xp, dtw, dtb, rates, skip, w, hid, gain, router, ids, wg, wu, wd)


def body(
    hidden_in,
    mamba_x,
    mamba_z,
    x_proj,
    dt_weight,
    dt_bias,
    state_rates,
    skip_gain,
    out_weight,
    norm_gain,
    router_weight,
    expert_ids,
    w_gate,
    w_up,
    w_down,
):
    ns, ne = lax.axis_size("seq"), lax.axis_size("expert")
    token_rows = hidden_in.shape[0] * hidden_in.shape[1]
    experts = router_weight.shape[1]
    top_count = expert_ids.shape[2]
    capacity = max(2, min(token_rows, token_rows * top_count * 5 // (2 * experts)))
    return layer_call(
        ns,
        ne,
        capacity,
        mamba_x,
        mamba_z,
        x_proj.T,
        dt_weight,
        dt_bias[None],
        state_rates.T,
        skip_gain[None],
        out_weight,
        hidden_in,
        norm_gain[None],
        router_weight.T,
        jnp.transpose(expert_ids, (1, 2, 0)),
        w_gate[0].T,
        w_up[0].T,
        w_down[0].T,
    )


def solution(mesh):
    placed = (
        P(("seq", "expert"), None, None),
        P("seq", None, "expert"),
        P("seq", None, "expert"),
        P("expert", None),
        P(None, "expert"),
        P("expert"),
        P("expert", None),
        P("expert"),
        P("expert", "seq"),
        P(),
        P(),
        P(("seq", "expert"), None, None),
        P("expert", None, "seq"),
        P("expert", None, "seq"),
        P("expert", None, "seq"),
    )
    return jax.shard_map(
        body,
        mesh=mesh,
        in_specs=placed,
        out_specs=P(("seq", "expert"), None, None),
        check_vma=False,
    )
```

```python
import functools

import jax
import jax.numpy as jnp
from jax import lax
from jax.experimental import pallas as pl
from jax.experimental.pallas import tpu as pltpu
from jax.sharding import PartitionSpec as P

EPS = 1e-05
F32 = jnp.float32
BF16 = jnp.bfloat16
BLOCK = 16
VMEM = pl.BlockSpec(memory_space=pltpu.VMEM)
HBM = pl.BlockSpec(memory_space=pl.ANY)


def remote(src, dst, send, recv, where):
    return pltpu.make_async_remote_copy(
        src_ref=src,
        dst_ref=dst,
        send_sem=send,
        recv_sem=recv,
        device_id=where,
        device_id_type=pl.DeviceIdType.MESH,
    )


def greet(ns, ne, seq, expert):
    barrier = pltpu.get_barrier_semaphore()

    def to_seq(o, _):
        pl.semaphore_signal(
            barrier, inc=1, device_id={"seq": lax.rem(seq + o, ns)}, device_id_type=pl.DeviceIdType.MESH
        )
        return 0

    def to_expert(o, _):
        pl.semaphore_signal(
            barrier, inc=1, device_id={"expert": lax.rem(expert + o, ne)}, device_id_type=pl.DeviceIdType.MESH
        )
        return 0

    lax.fori_loop(1, ns, to_seq, 0)
    lax.fori_loop(1, ne, to_expert, 0)
    pl.semaphore_wait(barrier, ns + ne - 2)


def layer_kernel(
    ns, ne, cap,
    x_in, z_in, xp_ref, dtw_ref, dtb_ref, rates_ref, skip_ref, w_ref, hid_in,
    gain_ref, router_ref, ids_ref, wg_ref, wu_ref, wd_ref,
    out_ref,
    x_ref, z_ref, hid_ref, place_ref, pick_ref, put_ref,
    part, part_in, part_sum, proj, sizes, running, reading, bc,
    state, state_sib, state_chip, state_in, incoming, gated, wf,
    product, row_in, row_sum, row_last, col_in, col_sum, col_last,
    scale_out, scale_in, scale_held,
    wide, combine_w, flat, packed_out, packed_in, back_out, back_in, returned,
    q_out, q_in, t_out, t_in, routed_high,
    held, parts, from_left, from_right, gate_w, up_w, down_w, hidden,
    load_sem, pair_send, pair_recv, p1_send, p1_recv, p2_send, p2_recv,
    h_send, h_recv, s_send, s_recv, ring_send, ring_recv, sib_send, sib_recv,
    a_send, a_recv, b_send, b_recv, c_send, c_recv, z_send, z_recv, d_send, d_recv, e_send, e_recv,
    g_send, g_recv, r_send, r_recv, q_send, q_recv, t_send, t_recv, k_send, k_recv,
):
    seq, expert = lax.axis_index("seq"), lax.axis_index("expert")
    nz = ns // 2
    hops, back = nz // 2, nz - 1 - nz // 2
    ny, nx = product.shape[0], product.shape[1]
    ey, ex = expert // nx, lax.rem(expert, nx)
    plane, core = seq // 2, lax.rem(seq, 2)
    right = lax.rem(plane + 1, nz) * 2 + core
    left = lax.rem(plane + nz - 1, nz) * 2 + core
    sibling = {"seq": plane * 2 + 1 - core}
    rank = dtw_ref.shape[0]
    tokens, channels = x_ref.shape
    state_n = rates_ref.shape[0]
    own, width = hid_ref.shape
    half = width // 2
    low, high = pl.ds(0, half), pl.ds(half, half)

    def quarter(i):
        return pl.ds(i * (half // 2), half // 2)

    blocks = tokens // (2 * BLOCK)
    span = 2 * BLOCK
    columns = w_ref.shape[1]
    count = ne * cap
    units = wg_ref.shape[0]
    pieces = width // 128

    def loop(start, stop, action):
        def step(i, carry):
            action(i)
            return carry

        lax.fori_loop(start, stop, step, 0)

    def ring_copy(stage, forward):
        side, to = (0, right) if forward else (1, left)
        index = lax.rem(plane + (nz - stage + 1 if forward else stage - 1), nz) * 2 + core
        return remote(
            wf.at[index], wf.at[index], ring_send.at[side, stage - 1], ring_recv.at[side, stage - 1], {"seq": to}
        )

    def sibling_copy(index):
        return remote(wf.at[index], wf.at[index], sib_send.at[index // 2], sib_recv.at[index // 2], sibling)

    def ring_stage(stage):
        if 1 < stage <= hops + 1:
            ring_copy(stage - 1, True).wait_recv()
            sibling_copy(lax.rem(plane + nz - (stage - 1), nz) * 2 + core).start()
        if 1 < stage <= back + 1:
            ring_copy(stage - 1, False).wait_recv()
            sibling_copy(lax.rem(plane + stage - 1, nz) * 2 + core).start()
        if stage <= hops:
            ring_copy(stage, True).start()
        if stage <= back:
            ring_copy(stage, False).start()

    def grid(shape, axis):
        return lax.broadcasted_iota(jnp.int32, shape, axis)

    def choose():
        docs, picks, positions = ids_ref.shape
        chosen, marks = [], []
        for k in range(picks):
            found = jnp.zeros((own, 1), F32)
            for d in range(docs):
                here = grid((own, positions), 0) == grid((own, positions), 1) * docs + d
                row = ids_ref[d, k : k + 1, :].astype(F32)
                found = found + jnp.sum(jnp.where(here, row, 0.0), axis=1, keepdims=True)
            chosen.append(found)
            marks.append((grid((own, ne), 1).astype(F32) == found).astype(F32))
            pick_ref[k] = marks[k]
        before = (grid((own, own), 0) > grid((own, own), 1)).astype(BF16)
        taken = jnp.dot(before, sum(marks).astype(BF16), preferred_element_type=F32)
        for k in range(picks):
            slot = jnp.sum(marks[k] * taken, axis=1, keepdims=True)
            target = chosen[k] * cap + slot
            put_ref[k] = (grid(put_ref.shape[1:], 1).astype(F32) == target).astype(F32)
        eye = (grid((own, own), 0) == grid((own, own), 1)).astype(BF16)
        place_ref[...] = lax.dot_general(
            sum(put_ref[k] for k in range(picks))[:, :count].astype(BF16), eye, (((0,), (0,)), ((), ())), preferred_element_type=F32
        ).astype(BF16)

    with jax.named_scope("greet"):
        weights = ((wg_ref, gate_w), (wu_ref, up_w), (wd_ref, down_w))
        loads = [
            pltpu.make_async_copy(src, dst.at[pl.ds(0, units)], load_sem.at[i])
            for i, (src, dst) in enumerate(weights)
        ]
        for copy in loads:
            copy.start()
        wf[seq] = w_ref[...]
        x_ref[...] = x_in[...].reshape(tokens, channels)
        greet(ns, ne, seq, expert)
        ring_stage(1)
        sibling_copy(seq).start()

    with jax.named_scope("proj"):
        partial = lax.dot_general(
            x_ref[...], xp_ref[...], (((1,), (1,)), ((), ())), preferred_element_type=F32
        ).astype(BF16)
        spare = part.shape[2] - partial.shape[1]
        part[...] = jnp.concatenate([partial, jnp.zeros((tokens, spare), BF16)], axis=1).reshape(part.shape)

        def part_copy(o):
            to = lax.rem(expert + o, ne)
            return remote(part.at[to], part_in.at[o - 1], p1_send.at[o - 1], p1_recv.at[o - 1], {"expert": to})

        loop(1, ne, lambda o: part_copy(o).start())
        pairs = [
            remote(src, dst.at[pl.ds(units, units)], pair_send.at[i], pair_recv.at[i], sibling)
            for i, (src, dst) in enumerate(weights)
        ]

        z_ref[...] = z_in[...].reshape(tokens, channels)
        hid_ref[...] = hid_in[...].reshape(own, width)

        def add_part(o, acc):
            part_copy(o).wait_recv()
            return acc + part_in[o - 1].astype(F32)

        summed = lax.fori_loop(1, ne, add_part, part[expert].astype(F32))
        part_sum[...] = summed.astype(BF16)
        proj[expert] = part_sum[...]

        def proj_copy(o):
            to = lax.rem(expert + o, ne)
            return remote(part_sum, proj.at[expert], p2_send.at[o - 1], p2_recv.at[o - 1], {"expert": to})

        loop(1, ne, lambda o: proj_copy(o).start())
        ring_stage(2)
        choose()
        loop(1, ne, lambda o: proj_copy(o).wait_recv())
        ring_stage(3)

    with jax.named_scope("sizes"):
        proj_all = proj[...].reshape(tokens, proj.shape[2])
        raw = jnp.dot(proj_all[:, :rank], dtw_ref[...], preferred_element_type=F32) + dtb_ref[...]
        sizes[...] = jnp.maximum(raw, 0.0) + jnp.log1p(jnp.exp(-jnp.abs(raw)))
        turned = proj_all[:, rank:].astype(F32).T
        for b in range(blocks):
            bc[b, :, :span] = turned[: 2 * state_n, b * span : (b + 1) * span]

    with jax.named_scope("scan"):
        rates = -rates_ref[...]
        zero_state = jnp.zeros((state_n, channels), F32)
        zero_row = jnp.zeros((1, channels), F32)

        def scan_block(b, carry):
            states, sums = [carry[0], carry[1]], [carry[2], carry[3]]
            first = pl.multiple_of(b * span, span)
            size_block = sizes[pl.ds(first, span), :]
            drive_block = size_block * x_ref[pl.ds(first, span), :].astype(F32)
            terms = bc[b]
            for r in range(span):
                d = r % 2
                size = size_block[r : r + 1]
                states[d] = (
                    jnp.exp(size * rates) * states[d] + drive_block[r : r + 1] * terms[:state_n, r : r + 1]
                )
                reading[pl.ds(first + r, 1), :] = jnp.sum(
                    states[d] * terms[state_n : 2 * state_n, r : r + 1], axis=0, keepdims=True
                )
                sums[d] = sums[d] + size
                running[pl.ds(first + r, 1), :] = sums[d]
            return states[0], states[1], sums[0], sums[1]

        end0, end1, sum0, sum1 = lax.fori_loop(
            0, blocks, scan_block, (zero_state, zero_state, zero_row, zero_row)
        )
        state[:state_n, :] = end0
        state[state_n : 2 * state_n, :] = end1
        state[2 * state_n : 2 * state_n + 8, :] = jnp.concatenate(
            [sum0, sum1, jnp.zeros((6, channels), F32)], axis=0
        )

    with jax.named_scope("states"):
        side = channels // 2
        mine = pl.ds(pl.multiple_of(core * side, side), side)
        other = pl.ds(pl.multiple_of((1 - core) * side, side), side)
        half_copy = remote(state.at[:, other], state_sib, h_send.at[0], h_recv.at[0], sibling)
        half_copy.start()
        ring_stage(4)
        rates_mine = -rates_ref[:, mine]

        def through(message, d):
            return jnp.exp(message[2 * state_n + d : 2 * state_n + d + 1] * rates_mine)

        def ends(message, d):
            return message[d * state_n : (d + 1) * state_n]

        half_copy.wait_recv()
        first_core = core == 0
        here, there = state[:, mine], state_sib[...]
        early = jnp.where(first_core, here, there)
        late = jnp.where(first_core, there, here)
        for d in range(2):
            state_chip[d * state_n : (d + 1) * state_n, :] = through(late, d) * ends(early, d) + ends(late, d)
        state_chip[2 * state_n :, :] = early[2 * state_n :] + late[2 * state_n :]

        def state_copy(to, source):
            return remote(state_chip, state_in.at[source], s_send.at[to], s_recv.at[source], {"seq": to * 2 + core})

        loop(plane + 1, nz, lambda to: state_copy(to, plane).start())
        ring_stage(5)
        for copy in pairs:
            copy.start()

        def horner(source, carry):
            state_copy(plane, source).wait_recv()
            message = state_in[source]
            return tuple(through(message, d) * carry[d] + ends(message, d) for d in range(2))

        zero_half = jnp.zeros((state_n, side), F32)
        entering = lax.fori_loop(0, plane, horner, (zero_half, zero_half))
        for d in range(2):
            passed = through(early, d) * entering[d] + ends(early, d)
            state_sib[d * state_n : (d + 1) * state_n, :] = jnp.where(first_core, passed, entering[d])
            incoming[d * state_n : (d + 1) * state_n, mine] = jnp.where(first_core, entering[d], passed)
        enter_copy = remote(
            state_sib.at[pl.ds(0, 2 * state_n)], incoming.at[:, mine], h_send.at[1], h_recv.at[1], sibling
        )
        enter_copy.start()
        enter_copy.wait_recv()

    with jax.named_scope("gate"):
        skip = skip_ref[...]
        entered = [incoming[d * state_n : (d + 1) * state_n, :] for d in range(2)]

        def gate_block(b):
            first = pl.multiple_of(b * span, span)
            sum_block = running[pl.ds(first, span), :]
            terms = bc[b]
            for r in range(span):
                carried = jnp.exp(sum_block[r : r + 1] * rates) * entered[r % 2]
                reading[pl.ds(first + r, 1), :] += jnp.sum(
                    carried * terms[state_n : 2 * state_n, r : r + 1], axis=0, keepdims=True
                )
            drive = x_ref[pl.ds(first, span), :].astype(F32)
            gate = z_ref[pl.ds(first, span), :].astype(F32)
            value = (reading[pl.ds(first, span), :] + skip * drive) * (gate / (1.0 + jnp.exp(-gate)))
            gated[pl.ds(first, span), :] = value.astype(BF16)

        loop(0, blocks, gate_block)

    with jax.named_scope("project"):
        loop(0, nz, lambda i: sibling_copy(2 * i + 1 - core).wait_recv())

        def multiply(b):
            at = pl.multiple_of(b * columns, columns)
            out = jnp.dot(gated[...], wf[b], preferred_element_type=F32).astype(BF16)
            product[:, :, :, pl.ds(at, columns)] = out.reshape(ny, nx, own, columns)

        def row_copy(o, g):
            to = lax.rem(ex + o, nx)
            return remote(
                product.at[:, to, :, quarter(2 * g)], row_in.at[g, o - 1], a_send.at[g, o - 1], a_recv.at[g, o - 1],
                {"expert": ey * nx + to},
            )

        def col_copy(o, g):
            to = lax.rem(ey + o, ny)
            return remote(
                product.at[to, :, :, quarter(2 * g + 1)], col_in.at[g, o - 1], b_send.at[g, o - 1], b_recv.at[g, o - 1],
                {"expert": to * nx + ex},
            )

        def row_pass(o, g):
            to = lax.rem(ey + o, ny)
            return remote(
                row_sum.at[g, to], row_last.at[g, o - 1], a_send.at[2 + g, o - 1], a_recv.at[2 + g, o - 1],
                {"expert": to * nx + ex},
            )

        def col_pass(o, g):
            to = lax.rem(ex + o, nx)
            return remote(
                col_sum.at[g, to], col_last.at[g, o - 1], b_send.at[2 + g, o - 1], b_recv.at[2 + g, o - 1],
                {"expert": ey * nx + to},
            )

        def start_group(g):
            loop(1, nx, lambda o: row_copy(o, g).start())
            loop(1, ny, lambda o: col_copy(o, g).start())

        def pass_group(g):
            loop(1, nx, lambda o: row_copy(o, g).wait_recv())

            def add_row(i):
                acc = product[i, ex, :, quarter(2 * g)].astype(F32)
                for o in range(nx - 1):
                    acc = acc + row_in[g, o, i].astype(F32)
                row_sum[g, i] = acc.astype(BF16)

            loop(0, ny, add_row)
            loop(1, ny, lambda o: row_pass(o, g).start())
            loop(1, ny, lambda o: col_copy(o, g).wait_recv())

            def add_col(i):
                acc = product[ey, i, :, quarter(2 * g + 1)].astype(F32)
                for o in range(ny - 1):
                    acc = acc + col_in[g, o, i].astype(F32)
                col_sum[g, i] = acc.astype(BF16)

            loop(0, nx, add_col)
            loop(1, nx, lambda o: col_pass(o, g).start())

        def finish_group(g):
            loop(1, ny, lambda o: row_pass(o, g).wait_recv())
            acc = hid_ref[:, quarter(2 * g)].astype(F32) + row_sum[g, ey].astype(F32)
            for o in range(ny - 1):
                acc = acc + row_last[g, o].astype(F32)
            wide[:, quarter(2 * g)] = acc.astype(BF16).astype(F32)
            loop(1, nx, lambda o: col_pass(o, g).wait_recv())
            acc = hid_ref[:, quarter(2 * g + 1)].astype(F32) + col_sum[g, ex].astype(F32)
            for o in range(nx - 1):
                acc = acc + col_last[g, o].astype(F32)
            wide[:, quarter(2 * g + 1)] = acc.astype(BF16).astype(F32)

        loop(0, ns // 2, multiply)
        start_group(0)
        loop(ns // 2, ns, multiply)
        pass_group(0)
        start_group(1)
        finish_group(0)

    sides = (low, high)
    each = pieces // 2

    def spread(value_of, target, h):
        for j in range(each):
            flat[pl.ds(j, count, stride=each), :] = value_of(h * each + j)
        target[h] = flat[...].astype(BF16).reshape(target.shape[1:])

    def gather_pieces(source, target, h):
        flat[...] = source[h].astype(F32).reshape(flat.shape)
        for j in range(each):
            at = h * half + j * 128
            target[:, at : at + 128] = flat[pl.ds(j, count, stride=each), :].astype(BF16)

    with jax.named_scope("route"):

        def send_rows(o, h):
            to = lax.rem(expert + o, ne)
            return remote(
                packed_out.at[h, to], packed_in.at[h, expert], d_send.at[h, o - 1], d_recv.at[h, o - 1],
                {"expert": to},
            )

        def send_half(h):
            scaled = (wide[:, sides[h]] * gain_ref[:, sides[h]]).astype(BF16)

            def placed(j):
                at = j * 128 - h * half
                return jnp.dot(place_ref[...], scaled[:, at : at + 128], preferred_element_type=F32)

            spread(placed, packed_out, h)
            loop(1, ne, lambda o: send_rows(o, h).start())
            packed_in[h, expert] = packed_out[h, expert]

        def take_half(h):
            loop(1, ne, lambda o: send_rows(o, h).wait_recv())
            gather_pieces(packed_in, held.at[0], h)

        send_half(0)
        pass_group(1)
        take_half(0)

    def gather_copy(stage, forward, h):
        way = 0 if forward else 1
        source = held.at[2 * (stage - 1) + (0 if forward or stage == 1 else 1), :, sides[h]]
        target = held.at[2 * stage + way if stage < hops else 1, :, sides[h]]
        return remote(
            source, target, g_send.at[way, h, stage - 1], g_recv.at[way, h, stage - 1],
            {"seq": right if forward else left},
        )

    def return_copy(stage, forward, u):
        way = 0 if forward else 1
        buffer = from_left if forward else from_right
        slot = 2 * (hops - stage + 1) + way_of(forward) if stage > 1 else 1
        return remote(
            parts.at[slot, :, quarter(u)], buffer.at[stage - 1, :, quarter(u)],
            r_send.at[way, u, stage - 1], r_recv.at[way, u, stage - 1], {"seq": right if forward else left},
        )

    def q_copy(o, slot):
        to = lax.rem(expert + o, ne)
        return remote(
            q_out.at[slot, to], q_in.at[slot, expert], q_send.at[slot, o - 1], q_recv.at[slot, o - 1], {"expert": to}
        )

    def t_copy(slot):
        away = hops if slot == 1 else slot // 2 if slot % 2 else nz - slot // 2
        to = lax.rem(plane + away, nz) * 2 + core
        return remote(t_out.at[slot], t_in.at[slot - 1], t_send.at[slot - 1], t_recv.at[slot - 1], {"seq": to})

    def k_copy(o):
        to = lax.rem(plane + o, nz) * 2 + core
        slot = 2 * o if o < hops else 1 if o == hops else 2 * (nz - o) + 1
        return remote(combine_w.at[0], combine_w.at[slot], k_send.at[o - 1], k_recv.at[o - 1], {"seq": to})

    def weighted(slot, h):
        weights_all = combine_w[slot][:, :count]
        weights_high = weights_all.astype(BF16)
        weights_low = (weights_all - weights_high.astype(F32)).astype(BF16)
        values = returned[:, sides[h]]
        return jnp.dot(weights_high, values, preferred_element_type=F32) + jnp.dot(
            weights_low, values, preferred_element_type=F32
        )

    def spread_q(slot):
        for j in range(each):
            at = half + j * 128
            flat[pl.ds(j, count, stride=each), :] = parts[slot, :, at : at + 128].astype(F32)
        q_out[slot] = flat[...].astype(BF16).reshape(q_out.shape[1:])
        loop(1, ne, lambda o: q_copy(o, slot).start())
        q_in[slot, expert] = q_out[slot, expert]

    def take_q(slot):
        loop(1, ne, lambda o: q_copy(o, slot).wait_recv())
        flat[...] = q_in[slot].astype(F32).reshape(flat.shape)
        for j in range(each):
            at = half + j * 128
            returned[:, at : at + 128] = flat[pl.ds(j, count, stride=each), :].astype(BF16)
        value = weighted(slot, 1)
        if slot == 0:
            routed_high[...] = value
        else:
            t_out[slot] = value.astype(BF16)
            t_copy(slot).start()

    def spread_pair(pair):
        spread_q(2 * pair)
        spread_q(2 * pair + 1)

    def take_pair(pair):
        take_q(2 * pair + 1)
        take_q(2 * pair)

    def way_of(forward):
        return 1 if forward else 0

    ways = ((True, 0, 1), (False, 1, 0))

    def scale_copy(o):
        to = lax.rem(expert + o, ne)
        return remote(scale_out, scale_in.at[expert], c_send.at[o - 1], c_recv.at[o - 1], {"expert": to})

    def plane_copy(o):
        to = lax.rem(plane + o, nz) * 2 + core
        slot = 2 * o if o < hops else 1 if o == hops else 2 * (nz - o) + 1
        return remote(scale_held.at[0], scale_held.at[slot], z_send.at[o - 1], z_recv.at[o - 1], {"seq": to})

    def first_row(value):
        return jnp.where(grid((8, 128), 0) == 0, value, 0.0)

    def send_scales():
        mixed = wide[...]
        scale = lax.rsqrt(jnp.mean(mixed * mixed, axis=-1, keepdims=True) + EPS)
        scale_out[...] = first_row(jnp.sum(scale * (put_ref[0] + put_ref[1]), axis=0, keepdims=True))
        loop(1, ne, lambda o: scale_copy(o).start())
        scale_in[expert] = scale_out[...]
        return (mixed * scale * gain_ref[...]).astype(BF16)

    def take_scales():
        loop(1, ne, lambda o: scale_copy(o).wait_recv())
        rows_in = jnp.sum(scale_in[...], axis=1)
        row, source = grid((count, ne), 0), grid((count, ne), 1)
        sender = ((row >= source * cap) & (row < (source + 1) * cap)).astype(F32)
        spread_rows = jnp.dot(sender, rows_in, preferred_element_type=F32, precision=lax.Precision.HIGHEST)
        passed = jnp.sum((row >= (source + 1) * cap).astype(F32), axis=1, keepdims=True)
        lane, place = grid((count, 128), 1).astype(F32), grid((count, 128), 0).astype(F32)
        wanted = (expert * cap).astype(F32) + place - cap * passed
        column = jnp.sum(jnp.where(lane == wanted, spread_rows, 0.0), axis=1, keepdims=True)
        scale_held[0] = first_row(jnp.sum(jnp.where(lane == place, column, 0.0), axis=0, keepdims=True))
        for o in range(1, nz):
            plane_copy(o).start()

    def scale_column(slot):
        lane, place = grid((count, 128), 1), grid((count, 128), 0)
        return jnp.sum(jnp.where(lane == place, scale_held[slot, 0:1, :], 0.0), axis=1, keepdims=True)

    def compute(pair):
        rows = held[2 * pair : 2 * pair + 2].reshape(2 * count, width)
        scale = jnp.concatenate([scale_column(2 * pair), scale_column(2 * pair + 1)], axis=0)
        across = (((1,), (1,)), ((), ()))
        gate = lax.dot_general(rows, gate_w[...], across, preferred_element_type=F32) * scale
        up = lax.dot_general(rows, up_w[...], across, preferred_element_type=F32) * scale
        hidden[...] = (gate / (1.0 + jnp.exp(-gate)) * up).astype(BF16)
        step = min(width, 512)

        def down(b):
            at = pl.multiple_of(b * step, step)
            out = jnp.dot(hidden[...], down_w[:, pl.ds(at, step)], preferred_element_type=F32)
            parts[2 * pair : 2 * pair + 2, :, pl.ds(at, step)] = out.astype(BF16).reshape(2, count, step)

        loop(0, width // step, down)

    def start_gather(stage, h):
        for forward, early, late in ways:
            if stage < hops or h == early:
                gather_copy(stage, forward, h).start()

    def wait_gather(stage, h):
        for forward, early, late in ways:
            gather_copy(stage, forward, h).wait_recv()

    with jax.named_scope("experts"):
        start_gather(1, 0)
        finish_group(1)
        send_half(1)
        normed = send_scales()
        if hops > 2:
            wait_gather(1, 0)
            start_gather(2, 0)
        take_half(1)
        start_gather(1, 1)
        take_scales()
        logits = lax.dot_general(
            normed, router_ref[...], (((1,), (1,)), ((), ())), preferred_element_type=F32
        )
        scores = []
        for k in range(pick_ref.shape[0]):
            picked = jnp.sum(pick_ref[k] * logits, axis=-1, keepdims=True)
            scores.append(1.0 / (1.0 + jnp.exp(-picked)))
        all_scores = sum(scores)
        combine_w[0] = sum((score / all_scores) * put_ref[k] for k, score in enumerate(scores))
        for o in range(1, nz):
            k_copy(o).start()
        for copy in loads:
            copy.wait()
        for copy in pairs:
            copy.wait_recv()
        for o in range(1, nz):
            plane_copy(o).wait_recv()
        if hops > 2:
            wait_gather(1, 1)
            start_gather(2, 1)
            wait_gather(2, 0)
            gather_copy(3, True, 0).start()
            compute(1)
            wait_gather(2, 1)
            gather_copy(3, False, 1).start()
            spread_pair(1)
            compute(2)
        for forward, early, late in ways:
            if hops > 1:
                gather_copy(hops - 1, forward, early).wait_recv()
                gather_copy(hops, forward, early).start()
                if hops > 2:
                    gather_copy(hops - 1, forward, late).start()
        if hops > 2:
            spread_pair(2)
        for forward, early, late in ways:
            gather_copy(hops, forward, early).wait_recv()
        compute(0)
        for forward, early, late in ways:
            return_copy(1, forward, early).start()
        spread_pair(0)
        if hops > 1:
            for forward, early, late in ways:
                gather_copy(hops - 1, forward, late).wait_recv()
            compute(hops - 1)

    with jax.named_scope("combine"):
        for stage in range(2, hops + 1):
            for u in range(2):
                for forward, early, late in ways:
                    if stage > 2 or u == early:
                        return_copy(stage - 1, forward, u).wait_recv()
                        buffer = from_left if forward else from_right
                        slot = 2 * (hops - stage + 1) + way_of(forward)
                        parts[slot, :, quarter(u)] = (
                            parts[slot, :, quarter(u)].astype(F32) + buffer[stage - 2, :, quarter(u)].astype(F32)
                        ).astype(BF16)
                    return_copy(stage, forward, u).start()
            if stage == 2:
                spread_pair(hops - 1)
                for o in range(1, nz):
                    k_copy(o).wait_recv()
            take_pair(stage - 1)
        if hops == 1:
            for o in range(1, nz):
                k_copy(o).wait_recv()
        take_pair(0)

    with jax.named_scope("home"):

        def summed_piece(j):
            at = pl.ds(j * 128, 128)
            value = parts[0, :, at].astype(F32)
            for forward, early, late in ways:
                if hops > 1 or 2 * j // each == early:
                    buffer = from_left if forward else from_right
                    value = value + buffer[hops - 1, :, at].astype(F32)
            return value

        def send_back(o, h):
            to = lax.rem(expert + o, ne)
            return remote(
                back_out.at[h, to], back_in.at[h, expert], e_send.at[h, o - 1], e_recv.at[h, o - 1],
                {"expert": to},
            )

        def finish_half(h, routed):
            mixed = (wide[:, sides[h]] + routed).astype(BF16)
            out_ref[:, :, sides[h]] = mixed.reshape(out_ref.shape[:2] + (half,))

        for u in range(2):
            for forward, early, late in ways:
                if hops > 1 or u == early:
                    return_copy(hops, forward, u).wait_recv()
        spread(summed_piece, back_out, 0)
        loop(1, ne, lambda o: send_back(o, 0).start())
        back_in[0, expert] = back_out[0, expert]
        total = routed_high[...]
        for slot in range(1, nz):
            t_copy(slot).wait_recv()
            total = total + t_in[slot - 1].astype(F32)
        finish_half(1, total)
        loop(1, ne, lambda o: send_back(o, 0).wait_recv())
        gather_pieces(back_in, returned, 0)
        finish_half(0, weighted(0, 0))

    with jax.named_scope("finish"):

        def sent_peers(o):
            part_copy(o).wait_send()
            proj_copy(o).wait_send()
            for h in range(2):
                send_rows(o, h).wait_send()
            send_back(o, 0).wait_send()
            for slot in range(nz):
                q_copy(o, slot).wait_send()

        loop(1, ne, sent_peers)

        loop(1, ne, lambda o: scale_copy(o).wait_send())
        for o in range(1, nz):
            plane_copy(o).wait_send()
            k_copy(o).wait_send()
            t_copy(o).wait_send()
        for g in range(2):

            def sent_rows(o):
                row_copy(o, g).wait_send()
                col_pass(o, g).wait_send()

            def sent_cols(o):
                col_copy(o, g).wait_send()
                row_pass(o, g).wait_send()

            loop(1, nx, sent_rows)
            loop(1, ny, sent_cols)
        loop(plane + 1, nz, lambda to: state_copy(to, plane).wait_send())
        half_copy.wait_send()
        enter_copy.wait_send()
        for stage in range(1, hops + 1):
            ring_copy(stage, True).wait_send()
            for forward, early, late in ways:
                for h in range(2):
                    if stage < hops or h == early:
                        gather_copy(stage, forward, h).wait_send()
                    if stage > 1 or h == early:
                        return_copy(stage, forward, h).wait_send()
        for stage in range(1, back + 1):
            ring_copy(stage, False).wait_send()
        loop(0, nz, lambda i: sibling_copy(2 * i + core).wait_send())
        for copy in pairs:
            copy.wait_send()


def layer_call(
    ns, ne, cap, x, z, xp, dtw, dtb, rates, skip, w, hid, gain, router, ids, wg, wu, wd
):
    tokens, channels = x.shape[0] * x.shape[1], x.shape[2]
    own, width = hid.shape[0] * hid.shape[1], hid.shape[2]
    picks = ids.shape[1]
    state_n = rates.shape[0]
    lanes = -(-xp.shape[0] // 128) * 128
    nz = ns // 2
    hops = nz // 2
    ny = 4 if ne == 16 else 2
    nx = ne // ny
    half = width // 2
    units = wg.shape[0]
    count = ne * cap
    pieces = width // 128
    dma = pltpu.SemaphoreType.DMA
    vmem = pltpu.VMEM
    return pl.pallas_call(
        functools.partial(layer_kernel, ns, ne, cap),
        out_shape=jax.ShapeDtypeStruct(hid.shape, BF16),
        in_specs=[VMEM] * 12 + [HBM] * 3,
        out_specs=VMEM,
        scratch_shapes=[
            vmem((tokens, channels), BF16),
            vmem((tokens, channels), BF16),
            vmem((own, width), BF16),
            vmem((count, own), BF16),
            vmem((picks, own, ne), F32),
            vmem((picks, own, 128), F32),
            vmem((ne, own, lanes), BF16),
            vmem((ne - 1, own, lanes), BF16),
            vmem((own, lanes), BF16),
            vmem((ne, own, lanes), BF16),
            vmem((tokens, channels), F32),
            vmem((tokens, channels), F32),
            vmem((tokens, channels), F32),
            vmem((tokens // (2 * BLOCK), 2 * state_n, 128), F32),
            vmem((2 * state_n + 8, channels), F32),
            vmem((2 * state_n + 8, channels // 2), F32),
            vmem((2 * state_n + 8, channels // 2), F32),
            vmem((nz, 2 * state_n + 8, channels // 2), F32),
            vmem((2 * state_n, channels), F32),
            vmem((tokens, channels), BF16),
            vmem((ns,) + w.shape, BF16),
            vmem((ny, nx, own, width), BF16),
            vmem((2, nx - 1, ny, own, half // 2), BF16),
            vmem((2, ny, own, half // 2), BF16),
            vmem((2, ny - 1, own, half // 2), BF16),
            vmem((2, ny - 1, nx, own, half // 2), BF16),
            vmem((2, nx, own, half // 2), BF16),
            vmem((2, nx - 1, own, half // 2), BF16),
            vmem((8, 128), F32),
            vmem((ne, 8, 128), F32),
            vmem((nz, 8, 128), F32),
            vmem((own, width), F32),
            vmem((nz, own, 128), F32),
            vmem((count * pieces // 2, 128), F32),
            vmem((2, ne, cap * pieces // 2, 128), BF16),
            vmem((2, ne, cap * pieces // 2, 128), BF16),
            vmem((1, ne, cap * pieces // 2, 128), BF16),
            vmem((1, ne, cap * pieces // 2, 128), BF16),
            vmem((count, width), BF16),
            vmem((nz, ne, cap * pieces // 2, 128), BF16),
            vmem((nz, ne, cap * pieces // 2, 128), BF16),
            vmem((nz, own, half), BF16),
            vmem((nz - 1, own, half), BF16),
            vmem((own, half), F32),
            vmem((nz, count, width), BF16),
            vmem((nz, count, width), BF16),
            vmem((hops, count, half), BF16),
            vmem((hops, count, half), BF16),
            vmem((2 * units, width), BF16),
            vmem((2 * units, width), BF16),
            vmem((2 * units, width), BF16),
            vmem((2 * count, 2 * units), BF16),
            dma((3,)),
            dma((3,)), dma((3,)),
            dma((ne - 1,)), dma((ne - 1,)),
            dma((ne - 1,)), dma((ne - 1,)),
            dma((2,)), dma((2,)),
            dma((nz,)), dma((nz,)),
            dma((2, hops)), dma((2, hops)),
            dma((nz,)), dma((nz,)),
            dma((4, nx + ny)), dma((4, nx + ny)),
            dma((4, nx + ny)), dma((4, nx + ny)),
            dma((ne - 1,)), dma((ne - 1,)),
            dma((nz - 1,)), dma((nz - 1,)),
            dma((2, ne - 1)), dma((2, ne - 1)),
            dma((2, ne - 1)), dma((2, ne - 1)),
            dma((2, 2, hops)), dma((2, 2, hops)),
            dma((2, 2, hops)), dma((2, 2, hops)),
            dma((nz, ne - 1)), dma((nz, ne - 1)),
            dma((nz - 1,)), dma((nz - 1,)),
            dma((nz - 1,)), dma((nz - 1,)),
        ],
        compiler_params=pltpu.CompilerParams(
            collective_id=0, has_side_effects=True, vmem_limit_bytes=58 * 1024 * 1024
        ),
    )(x, z, xp, dtw, dtb, rates, skip, w, hid, gain, router, ids, wg, wu, wd)


def body(
    hidden_in,
    mamba_x,
    mamba_z,
    x_proj,
    dt_weight,
    dt_bias,
    state_rates,
    skip_gain,
    out_weight,
    norm_gain,
    router_weight,
    expert_ids,
    w_gate,
    w_up,
    w_down,
):
    ns, ne = lax.axis_size("seq"), lax.axis_size("expert")
    token_rows = hidden_in.shape[0] * hidden_in.shape[1]
    experts = router_weight.shape[1]
    top_count = expert_ids.shape[2]
    capacity = max(2, min(token_rows, token_rows * top_count * 5 // (2 * experts)))
    return layer_call(
        ns,
        ne,
        capacity,
        mamba_x,
        mamba_z,
        x_proj.T,
        dt_weight,
        dt_bias[None],
        state_rates.T,
        skip_gain[None],
        out_weight,
        hidden_in,
        norm_gain[None],
        router_weight.T,
        jnp.transpose(expert_ids, (1, 2, 0)),
        w_gate[0].T,
        w_up[0].T,
        w_down[0].T,
    )


def solution(mesh):
    placed = (
        P(("seq", "expert"), None, None),
        P("seq", None, "expert"),
        P("seq", None, "expert"),
        P("expert", None),
        P(None, "expert"),
        P("expert"),
        P("expert", None),
        P("expert"),
        P("expert", "seq"),
        P(),
        P(),
        P(("seq", "expert"), None, None),
        P("expert", None, "seq"),
        P("expert", None, "seq"),
        P("expert", None, "seq"),
    )
    return jax.shard_map(
        body,
        mesh=mesh,
        in_specs=placed,
        out_specs=P(("seq", "expert"), None, None),
        check_vma=False,
    )
```

```python
import functools

import jax
import jax.numpy as jnp
from jax import lax
from jax.experimental import pallas as pl
from jax.experimental.pallas import tpu as pltpu
from jax.sharding import PartitionSpec as P

EPS = 1e-05
F32 = jnp.float32
BF16 = jnp.bfloat16
BLOCK = 16
VMEM = pl.BlockSpec(memory_space=pltpu.VMEM)
HBM = pl.BlockSpec(memory_space=pl.ANY)


def remote(src, dst, send, recv, where):
    return pltpu.make_async_remote_copy(
        src_ref=src,
        dst_ref=dst,
        send_sem=send,
        recv_sem=recv,
        device_id=where,
        device_id_type=pl.DeviceIdType.MESH,
    )


def greet(ns, ne, seq, expert):
    barrier = pltpu.get_barrier_semaphore()

    def to_seq(o, _):
        pl.semaphore_signal(
            barrier, inc=1, device_id={"seq": lax.rem(seq + o, ns)}, device_id_type=pl.DeviceIdType.MESH
        )
        return 0

    def to_expert(o, _):
        pl.semaphore_signal(
            barrier, inc=1, device_id={"expert": lax.rem(expert + o, ne)}, device_id_type=pl.DeviceIdType.MESH
        )
        return 0

    lax.fori_loop(1, ns, to_seq, 0)
    lax.fori_loop(1, ne, to_expert, 0)
    pl.semaphore_wait(barrier, ns + ne - 2)


def layer_kernel(
    ns, ne, cap,
    x_in, z_in, xp_ref, dtw_ref, dtb_ref, rates_ref, skip_ref, w_ref, hid_in,
    gain_ref, router_ref, ids_ref, wg_ref, wu_ref, wd_ref,
    out_ref,
    x_ref, z_ref, hid_ref, place_ref, pick_ref, put_ref,
    part, part_in, part_sum, proj, sizes, running, reading, bc,
    state, state_sib, state_chip, state_in, incoming, gated, wf,
    product, row_in, row_sum, row_last, col_in, col_sum, col_last,
    scale_out, scale_in, scale_held,
    wide, combine_w, flat, packed_out, packed_in, back_out, back_in, returned,
    q_out, q_in, t_out, t_left, t_right, routed_high,
    held, parts, from_left, from_right, gate_w, up_w, down_w, hidden,
    load_sem, pair_send, pair_recv, p1_send, p1_recv, p2_send, p2_recv,
    h_send, h_recv, s_send, s_recv, ring_send, ring_recv, sib_send, sib_recv,
    a_send, a_recv, b_send, b_recv, c_send, c_recv, z_send, z_recv, d_send, d_recv, e_send, e_recv,
    g_send, g_recv, r_send, r_recv, q_send, q_recv, t_send, t_recv, k_send, k_recv,
):
    seq, expert = lax.axis_index("seq"), lax.axis_index("expert")
    nz = ns // 2
    hops, back = nz // 2, nz - 1 - nz // 2
    ny, nx = product.shape[0], product.shape[1]
    ey, ex = expert // nx, lax.rem(expert, nx)
    plane, core = seq // 2, lax.rem(seq, 2)
    right = lax.rem(plane + 1, nz) * 2 + core
    left = lax.rem(plane + nz - 1, nz) * 2 + core
    sibling = {"seq": plane * 2 + 1 - core}
    rank = dtw_ref.shape[0]
    tokens, channels = x_ref.shape
    state_n = rates_ref.shape[0]
    own, width = hid_ref.shape
    half = width // 2
    low, high = pl.ds(0, half), pl.ds(half, half)

    def quarter(i):
        return pl.ds(i * (half // 2), half // 2)

    blocks = tokens // (2 * BLOCK)
    span = 2 * BLOCK
    columns = w_ref.shape[1]
    count = ne * cap
    units = wg_ref.shape[0]
    pieces = width // 128

    def loop(start, stop, action):
        def step(i, carry):
            action(i)
            return carry

        lax.fori_loop(start, stop, step, 0)

    def ring_copy(stage, forward):
        side, to = (0, right) if forward else (1, left)
        index = lax.rem(plane + (nz - stage + 1 if forward else stage - 1), nz) * 2 + core
        return remote(
            wf.at[index], wf.at[index], ring_send.at[side, stage - 1], ring_recv.at[side, stage - 1], {"seq": to}
        )

    def sibling_copy(index):
        return remote(wf.at[index], wf.at[index], sib_send.at[index // 2], sib_recv.at[index // 2], sibling)

    def ring_stage(stage):
        if 1 < stage <= hops + 1:
            ring_copy(stage - 1, True).wait_recv()
            sibling_copy(lax.rem(plane + nz - (stage - 1), nz) * 2 + core).start()
        if 1 < stage <= back + 1:
            ring_copy(stage - 1, False).wait_recv()
            sibling_copy(lax.rem(plane + stage - 1, nz) * 2 + core).start()
        if stage <= hops:
            ring_copy(stage, True).start()
        if stage <= back:
            ring_copy(stage, False).start()

    def grid(shape, axis):
        return lax.broadcasted_iota(jnp.int32, shape, axis)

    def choose():
        docs, picks, positions = ids_ref.shape
        chosen, marks = [], []
        for k in range(picks):
            found = jnp.zeros((own, 1), F32)
            for d in range(docs):
                here = grid((own, positions), 0) == grid((own, positions), 1) * docs + d
                row = ids_ref[d, k : k + 1, :].astype(F32)
                found = found + jnp.sum(jnp.where(here, row, 0.0), axis=1, keepdims=True)
            chosen.append(found)
            marks.append((grid((own, ne), 1).astype(F32) == found).astype(F32))
            pick_ref[k] = marks[k]
        before = (grid((own, own), 0) > grid((own, own), 1)).astype(BF16)
        taken = jnp.dot(before, sum(marks).astype(BF16), preferred_element_type=F32)
        for k in range(picks):
            slot = jnp.sum(marks[k] * taken, axis=1, keepdims=True)
            target = chosen[k] * cap + slot
            put_ref[k] = (grid(put_ref.shape[1:], 1).astype(F32) == target).astype(F32)
        eye = (grid((own, own), 0) == grid((own, own), 1)).astype(BF16)
        place_ref[...] = lax.dot_general(
            sum(put_ref[k] for k in range(picks))[:, :count].astype(BF16), eye, (((0,), (0,)), ((), ())), preferred_element_type=F32
        ).astype(BF16)

    with jax.named_scope("greet"):
        weights = ((wg_ref, gate_w), (wu_ref, up_w), (wd_ref, down_w))
        loads = [
            pltpu.make_async_copy(src, dst.at[pl.ds(0, units)], load_sem.at[i])
            for i, (src, dst) in enumerate(weights)
        ]
        for copy in loads:
            copy.start()
        wf[seq] = w_ref[...]
        x_ref[...] = x_in[...].reshape(tokens, channels)
        greet(ns, ne, seq, expert)
        ring_stage(1)
        sibling_copy(seq).start()

    with jax.named_scope("proj"):
        partial = lax.dot_general(
            x_ref[...], xp_ref[...], (((1,), (1,)), ((), ())), preferred_element_type=F32
        ).astype(BF16)
        spare = part.shape[2] - partial.shape[1]
        part[...] = jnp.concatenate([partial, jnp.zeros((tokens, spare), BF16)], axis=1).reshape(part.shape)

        def part_copy(o):
            to = lax.rem(expert + o, ne)
            return remote(part.at[to], part_in.at[o - 1], p1_send.at[o - 1], p1_recv.at[o - 1], {"expert": to})

        loop(1, ne, lambda o: part_copy(o).start())
        pairs = [
            remote(src, dst.at[pl.ds(units, units)], pair_send.at[i], pair_recv.at[i], sibling)
            for i, (src, dst) in enumerate(weights)
        ]

        z_ref[...] = z_in[...].reshape(tokens, channels)
        hid_ref[...] = hid_in[...].reshape(own, width)

        def add_part(o, acc):
            part_copy(o).wait_recv()
            return acc + part_in[o - 1].astype(F32)

        summed = lax.fori_loop(1, ne, add_part, part[expert].astype(F32))
        part_sum[...] = summed.astype(BF16)
        proj[expert] = part_sum[...]

        def proj_copy(o):
            to = lax.rem(expert + o, ne)
            return remote(part_sum, proj.at[expert], p2_send.at[o - 1], p2_recv.at[o - 1], {"expert": to})

        loop(1, ne, lambda o: proj_copy(o).start())
        ring_stage(2)
        choose()
        loop(1, ne, lambda o: proj_copy(o).wait_recv())
        ring_stage(3)

    with jax.named_scope("sizes"):
        proj_all = proj[...].reshape(tokens, proj.shape[2])
        raw = jnp.dot(proj_all[:, :rank], dtw_ref[...], preferred_element_type=F32) + dtb_ref[...]
        sizes[...] = jnp.maximum(raw, 0.0) + jnp.log1p(jnp.exp(-jnp.abs(raw)))
        turned = proj_all[:, rank:].astype(F32).T
        for b in range(blocks):
            bc[b, :, :span] = turned[: 2 * state_n, b * span : (b + 1) * span]

    with jax.named_scope("scan"):
        rates = -rates_ref[...]
        zero_state = jnp.zeros((state_n, channels), F32)
        zero_row = jnp.zeros((1, channels), F32)

        def scan_block(b, carry):
            states, sums = [carry[0], carry[1]], [carry[2], carry[3]]
            first = pl.multiple_of(b * span, span)
            size_block = sizes[pl.ds(first, span), :]
            drive_block = size_block * x_ref[pl.ds(first, span), :].astype(F32)
            terms = bc[b]
            for r in range(span):
                d = r % 2
                size = size_block[r : r + 1]
                states[d] = (
                    jnp.exp(size * rates) * states[d] + drive_block[r : r + 1] * terms[:state_n, r : r + 1]
                )
                reading[pl.ds(first + r, 1), :] = jnp.sum(
                    states[d] * terms[state_n : 2 * state_n, r : r + 1], axis=0, keepdims=True
                )
                sums[d] = sums[d] + size
                running[pl.ds(first + r, 1), :] = sums[d]
            return states[0], states[1], sums[0], sums[1]

        end0, end1, sum0, sum1 = lax.fori_loop(
            0, blocks, scan_block, (zero_state, zero_state, zero_row, zero_row)
        )
        state[:state_n, :] = end0
        state[state_n : 2 * state_n, :] = end1
        state[2 * state_n : 2 * state_n + 8, :] = jnp.concatenate(
            [sum0, sum1, jnp.zeros((6, channels), F32)], axis=0
        )

    with jax.named_scope("states"):
        side = channels // 2
        mine = pl.ds(pl.multiple_of(core * side, side), side)
        other = pl.ds(pl.multiple_of((1 - core) * side, side), side)
        half_copy = remote(state.at[:, other], state_sib, h_send.at[0], h_recv.at[0], sibling)
        half_copy.start()
        ring_stage(4)
        rates_mine = -rates_ref[:, mine]

        def through(message, d):
            return jnp.exp(message[2 * state_n + d : 2 * state_n + d + 1] * rates_mine)

        def ends(message, d):
            return message[d * state_n : (d + 1) * state_n]

        half_copy.wait_recv()
        first_core = core == 0
        here, there = state[:, mine], state_sib[...]
        early = jnp.where(first_core, here, there)
        late = jnp.where(first_core, there, here)
        for d in range(2):
            state_chip[d * state_n : (d + 1) * state_n, :] = through(late, d) * ends(early, d) + ends(late, d)
        state_chip[2 * state_n :, :] = early[2 * state_n :] + late[2 * state_n :]

        def state_copy(to, source):
            return remote(state_chip, state_in.at[source], s_send.at[to], s_recv.at[source], {"seq": to * 2 + core})

        loop(plane + 1, nz, lambda to: state_copy(to, plane).start())
        ring_stage(5)
        for copy in pairs:
            copy.start()

        def horner(source, carry):
            state_copy(plane, source).wait_recv()
            message = state_in[source]
            return tuple(through(message, d) * carry[d] + ends(message, d) for d in range(2))

        zero_half = jnp.zeros((state_n, side), F32)
        entering = lax.fori_loop(0, plane, horner, (zero_half, zero_half))
        for d in range(2):
            passed = through(early, d) * entering[d] + ends(early, d)
            state_sib[d * state_n : (d + 1) * state_n, :] = jnp.where(first_core, passed, entering[d])
            incoming[d * state_n : (d + 1) * state_n, mine] = jnp.where(first_core, entering[d], passed)
        enter_copy = remote(
            state_sib.at[pl.ds(0, 2 * state_n)], incoming.at[:, mine], h_send.at[1], h_recv.at[1], sibling
        )
        enter_copy.start()
        enter_copy.wait_recv()

    with jax.named_scope("gate"):
        skip = skip_ref[...]
        entered = [incoming[d * state_n : (d + 1) * state_n, :] for d in range(2)]

        def gate_block(b):
            first = pl.multiple_of(b * span, span)
            sum_block = running[pl.ds(first, span), :]
            terms = bc[b]
            for r in range(span):
                carried = jnp.exp(sum_block[r : r + 1] * rates) * entered[r % 2]
                reading[pl.ds(first + r, 1), :] += jnp.sum(
                    carried * terms[state_n : 2 * state_n, r : r + 1], axis=0, keepdims=True
                )
            drive = x_ref[pl.ds(first, span), :].astype(F32)
            gate = z_ref[pl.ds(first, span), :].astype(F32)
            value = (reading[pl.ds(first, span), :] + skip * drive) * (gate / (1.0 + jnp.exp(-gate)))
            gated[pl.ds(first, span), :] = value.astype(BF16)

        loop(0, blocks, gate_block)

    with jax.named_scope("project"):
        loop(0, nz, lambda i: sibling_copy(2 * i + 1 - core).wait_recv())

        def multiply(b):
            at = pl.multiple_of(b * columns, columns)
            out = jnp.dot(gated[...], wf[b], preferred_element_type=F32).astype(BF16)
            product[:, :, :, pl.ds(at, columns)] = out.reshape(ny, nx, own, columns)

        def row_copy(o, g):
            to = lax.rem(ex + o, nx)
            return remote(
                product.at[:, to, :, quarter(2 * g)], row_in.at[g, o - 1], a_send.at[g, o - 1], a_recv.at[g, o - 1],
                {"expert": ey * nx + to},
            )

        def col_copy(o, g):
            to = lax.rem(ey + o, ny)
            return remote(
                product.at[to, :, :, quarter(2 * g + 1)], col_in.at[g, o - 1], b_send.at[g, o - 1], b_recv.at[g, o - 1],
                {"expert": to * nx + ex},
            )

        def row_pass(o, g):
            to = lax.rem(ey + o, ny)
            return remote(
                row_sum.at[g, to], row_last.at[g, o - 1], a_send.at[2 + g, o - 1], a_recv.at[2 + g, o - 1],
                {"expert": to * nx + ex},
            )

        def col_pass(o, g):
            to = lax.rem(ex + o, nx)
            return remote(
                col_sum.at[g, to], col_last.at[g, o - 1], b_send.at[2 + g, o - 1], b_recv.at[2 + g, o - 1],
                {"expert": ey * nx + to},
            )

        def start_group(g):
            loop(1, nx, lambda o: row_copy(o, g).start())
            loop(1, ny, lambda o: col_copy(o, g).start())

        def pass_group(g):
            loop(1, nx, lambda o: row_copy(o, g).wait_recv())

            def add_row(i):
                acc = product[i, ex, :, quarter(2 * g)].astype(F32)
                for o in range(nx - 1):
                    acc = acc + row_in[g, o, i].astype(F32)
                row_sum[g, i] = acc.astype(BF16)

            loop(0, ny, add_row)
            loop(1, ny, lambda o: row_pass(o, g).start())
            loop(1, ny, lambda o: col_copy(o, g).wait_recv())

            def add_col(i):
                acc = product[ey, i, :, quarter(2 * g + 1)].astype(F32)
                for o in range(ny - 1):
                    acc = acc + col_in[g, o, i].astype(F32)
                col_sum[g, i] = acc.astype(BF16)

            loop(0, nx, add_col)
            loop(1, nx, lambda o: col_pass(o, g).start())

        def finish_group(g):
            loop(1, ny, lambda o: row_pass(o, g).wait_recv())
            acc = hid_ref[:, quarter(2 * g)].astype(F32) + row_sum[g, ey].astype(F32)
            for o in range(ny - 1):
                acc = acc + row_last[g, o].astype(F32)
            wide[:, quarter(2 * g)] = acc.astype(BF16).astype(F32)
            loop(1, nx, lambda o: col_pass(o, g).wait_recv())
            acc = hid_ref[:, quarter(2 * g + 1)].astype(F32) + col_sum[g, ex].astype(F32)
            for o in range(nx - 1):
                acc = acc + col_last[g, o].astype(F32)
            wide[:, quarter(2 * g + 1)] = acc.astype(BF16).astype(F32)

        loop(0, ns // 2, multiply)
        start_group(0)
        loop(ns // 2, ns, multiply)
        pass_group(0)
        start_group(1)
        finish_group(0)

    sides = (low, high)
    each = pieces // 2

    def spread(value_of, target, h):
        for j in range(each):
            flat[pl.ds(j, count, stride=each), :] = value_of(h * each + j)
        target[h] = flat[...].astype(BF16).reshape(target.shape[1:])

    def gather_pieces(source, target, h):
        flat[...] = source[h].astype(F32).reshape(flat.shape)
        for j in range(each):
            at = h * half + j * 128
            target[:, at : at + 128] = flat[pl.ds(j, count, stride=each), :].astype(BF16)

    with jax.named_scope("route"):

        def send_rows(o, h):
            to = lax.rem(expert + o, ne)
            return remote(
                packed_out.at[h, to], packed_in.at[h, expert], d_send.at[h, o - 1], d_recv.at[h, o - 1],
                {"expert": to},
            )

        def send_half(h):
            scaled = (wide[:, sides[h]] * gain_ref[:, sides[h]]).astype(BF16)

            def placed(j):
                at = j * 128 - h * half
                return jnp.dot(place_ref[...], scaled[:, at : at + 128], preferred_element_type=F32)

            spread(placed, packed_out, h)
            loop(1, ne, lambda o: send_rows(o, h).start())
            packed_in[h, expert] = packed_out[h, expert]

        def take_half(h):
            loop(1, ne, lambda o: send_rows(o, h).wait_recv())
            gather_pieces(packed_in, held.at[0], h)

        send_half(0)
        pass_group(1)
        take_half(0)

    def gather_copy(stage, forward, h):
        way = 0 if forward else 1
        source = held.at[2 * (stage - 1) + (0 if forward or stage == 1 else 1), :, sides[h]]
        target = held.at[2 * stage + way if stage < hops else 1, :, sides[h]]
        return remote(
            source, target, g_send.at[way, h, stage - 1], g_recv.at[way, h, stage - 1],
            {"seq": right if forward else left},
        )

    def return_copy(stage, forward, u):
        way = 0 if forward else 1
        buffer = from_left if forward else from_right
        slot = 2 * (hops - stage + 1) + way_of(forward) if stage > 1 else 1
        return remote(
            parts.at[slot, :, quarter(u)], buffer.at[stage - 1, :, quarter(u)],
            r_send.at[way, u, stage - 1], r_recv.at[way, u, stage - 1], {"seq": right if forward else left},
        )

    def q_copy(o, slot):
        to = lax.rem(expert + o, ne)
        return remote(
            q_out.at[slot, to], q_in.at[slot, expert], q_send.at[slot, o - 1], q_recv.at[slot, o - 1], {"expert": to}
        )

    def t_copy(stage, forward, u):
        way = 0 if forward else 1
        buffer = t_left if forward else t_right
        slot = 2 * (hops - stage + 1) + way_of(forward) if stage > 1 else 1
        picked = quarter(u) if stage == 1 else pl.ds(0, half)
        return remote(
            t_out.at[slot, :, picked], buffer.at[stage - 1, :, picked],
            t_send.at[way, stage - 1], t_recv.at[way, stage - 1], {"seq": right if forward else left},
        )

    def k_copy(o):
        to = lax.rem(plane + o, nz) * 2 + core
        slot = 2 * o if o < hops else 1 if o == hops else 2 * (nz - o) + 1
        return remote(combine_w.at[0], combine_w.at[slot], k_send.at[o - 1], k_recv.at[o - 1], {"seq": to})

    def weighted(slot, h):
        weights_all = combine_w[slot][:, :count]
        weights_high = weights_all.astype(BF16)
        weights_low = (weights_all - weights_high.astype(F32)).astype(BF16)
        values = returned[:, sides[h]]
        return jnp.dot(weights_high, values, preferred_element_type=F32) + jnp.dot(
            weights_low, values, preferred_element_type=F32
        )

    def spread_q(slot):
        for j in range(each):
            at = half + j * 128
            flat[pl.ds(j, count, stride=each), :] = parts[slot, :, at : at + 128].astype(F32)
        q_out[slot] = flat[...].astype(BF16).reshape(q_out.shape[1:])
        loop(1, ne, lambda o: q_copy(o, slot).start())
        q_in[slot, expert] = q_out[slot, expert]

    def take_q(slot):
        loop(1, ne, lambda o: q_copy(o, slot).wait_recv())
        flat[...] = q_in[slot].astype(F32).reshape(flat.shape)
        for j in range(each):
            at = half + j * 128
            returned[:, at : at + 128] = flat[pl.ds(j, count, stride=each), :].astype(BF16)
        value = weighted(slot, 1)
        if slot == 0:
            routed_high[...] = value
        else:
            t_out[slot] = value.astype(BF16)

    def spread_pair(pair):
        spread_q(2 * pair)
        spread_q(2 * pair + 1)

    def take_pair(pair):
        take_q(2 * pair + 1)
        take_q(2 * pair)

    def t_stage(stage):
        for forward, early, late in ways:
            if stage > 1:
                t_copy(stage - 1, forward, early).wait_recv()
                buffer = t_left if forward else t_right
                slot = 2 * (hops - stage + 1) + way_of(forward)
                picked = quarter(early) if stage == 2 else pl.ds(0, half)
                t_out[slot, :, picked] = (
                    t_out[slot, :, picked].astype(F32) + buffer[stage - 2, :, picked].astype(F32)
                ).astype(BF16)
            t_copy(stage, forward, early).start()

    def sent_early():
        def sent_peers(o):
            part_copy(o).wait_send()
            proj_copy(o).wait_send()
            scale_copy(o).wait_send()
            for h in range(2):
                send_rows(o, h).wait_send()

        loop(1, ne, sent_peers)
        for g in range(2):

            def sent_rows(o):
                row_copy(o, g).wait_send()
                col_pass(o, g).wait_send()

            def sent_cols(o):
                col_copy(o, g).wait_send()
                row_pass(o, g).wait_send()

            loop(1, nx, sent_rows)
            loop(1, ny, sent_cols)
        loop(plane + 1, nz, lambda to: state_copy(to, plane).wait_send())
        half_copy.wait_send()
        enter_copy.wait_send()
        for stage in range(1, hops + 1):
            ring_copy(stage, True).wait_send()
        for stage in range(1, back + 1):
            ring_copy(stage, False).wait_send()
        loop(0, nz, lambda i: sibling_copy(2 * i + core).wait_send())
        for copy in pairs:
            copy.wait_send()

    def sent_pair(pair):
        def sent(o):
            q_copy(o, 2 * pair).wait_send()
            q_copy(o, 2 * pair + 1).wait_send()

        loop(1, ne, sent)

    def way_of(forward):
        return 1 if forward else 0

    ways = ((True, 0, 1), (False, 1, 0))

    def scale_copy(o):
        to = lax.rem(expert + o, ne)
        return remote(scale_out, scale_in.at[expert], c_send.at[o - 1], c_recv.at[o - 1], {"expert": to})

    def plane_copy(o):
        to = lax.rem(plane + o, nz) * 2 + core
        slot = 2 * o if o < hops else 1 if o == hops else 2 * (nz - o) + 1
        return remote(scale_held.at[0], scale_held.at[slot], z_send.at[o - 1], z_recv.at[o - 1], {"seq": to})

    def first_row(value):
        return jnp.where(grid((8, 128), 0) == 0, value, 0.0)

    def send_scales():
        mixed = wide[...]
        scale = lax.rsqrt(jnp.mean(mixed * mixed, axis=-1, keepdims=True) + EPS)
        scale_out[...] = first_row(jnp.sum(scale * (put_ref[0] + put_ref[1]), axis=0, keepdims=True))
        loop(1, ne, lambda o: scale_copy(o).start())
        scale_in[expert] = scale_out[...]
        return (mixed * scale * gain_ref[...]).astype(BF16)

    def take_scales():
        loop(1, ne, lambda o: scale_copy(o).wait_recv())
        rows_in = jnp.sum(scale_in[...], axis=1)
        row, source = grid((count, ne), 0), grid((count, ne), 1)
        sender = ((row >= source * cap) & (row < (source + 1) * cap)).astype(F32)
        spread_rows = jnp.dot(sender, rows_in, preferred_element_type=F32, precision=lax.Precision.HIGHEST)
        passed = jnp.sum((row >= (source + 1) * cap).astype(F32), axis=1, keepdims=True)
        lane, place = grid((count, 128), 1).astype(F32), grid((count, 128), 0).astype(F32)
        wanted = (expert * cap).astype(F32) + place - cap * passed
        column = jnp.sum(jnp.where(lane == wanted, spread_rows, 0.0), axis=1, keepdims=True)
        scale_held[0] = first_row(jnp.sum(jnp.where(lane == place, column, 0.0), axis=0, keepdims=True))
        for o in range(1, nz):
            plane_copy(o).start()

    def scale_column(slot):
        lane, place = grid((count, 128), 1), grid((count, 128), 0)
        return jnp.sum(jnp.where(lane == place, scale_held[slot, 0:1, :], 0.0), axis=1, keepdims=True)

    def compute(pair):
        rows = held[2 * pair : 2 * pair + 2].reshape(2 * count, width)
        scale = jnp.concatenate([scale_column(2 * pair), scale_column(2 * pair + 1)], axis=0)
        across = (((1,), (1,)), ((), ()))
        gate = lax.dot_general(rows, gate_w[...], across, preferred_element_type=F32) * scale
        up = lax.dot_general(rows, up_w[...], across, preferred_element_type=F32) * scale
        hidden[...] = (gate / (1.0 + jnp.exp(-gate)) * up).astype(BF16)
        finish_compute(pair, 0)

    def finish_compute(pair, h):
        step = min(half, 512)
        blocks_half = half // step

        def down(b):
            at = pl.multiple_of(b * step, step)
            out = jnp.dot(hidden[...], down_w[:, pl.ds(at, step)], preferred_element_type=F32)
            parts[2 * pair : 2 * pair + 2, :, pl.ds(at, step)] = out.astype(BF16).reshape(2, count, step)

        loop(h * blocks_half, (h + 1) * blocks_half, down)

    def start_gather(stage, h):
        for forward, early, late in ways:
            if stage < hops or h == early:
                gather_copy(stage, forward, h).start()

    def wait_gather(stage, h):
        for forward, early, late in ways:
            gather_copy(stage, forward, h).wait_recv()

    with jax.named_scope("experts"):
        start_gather(1, 0)
        finish_group(1)
        send_half(1)
        normed = send_scales()
        if hops > 2:
            wait_gather(1, 0)
            start_gather(2, 0)
        take_half(1)
        start_gather(1, 1)
        take_scales()
        logits = lax.dot_general(
            normed, router_ref[...], (((1,), (1,)), ((), ())), preferred_element_type=F32
        )
        scores = []
        for k in range(pick_ref.shape[0]):
            picked = jnp.sum(pick_ref[k] * logits, axis=-1, keepdims=True)
            scores.append(1.0 / (1.0 + jnp.exp(-picked)))
        all_scores = sum(scores)
        combine_w[0] = sum((score / all_scores) * put_ref[k] for k, score in enumerate(scores))
        for o in range(1, nz):
            k_copy(o).start()
        for copy in loads:
            copy.wait()
        for copy in pairs:
            copy.wait_recv()
        for o in range(1, nz):
            plane_copy(o).wait_recv()
        sent_early()
        if hops > 2:
            wait_gather(1, 1)
            start_gather(2, 1)
            wait_gather(2, 0)
            gather_copy(3, True, 0).start()
            compute(1)
            finish_compute(1, 1)
            wait_gather(2, 1)
            gather_copy(3, False, 1).start()
            spread_pair(1)
            compute(2)
            finish_compute(2, 1)
        for forward, early, late in ways:
            if hops > 1:
                gather_copy(hops - 1, forward, early).wait_recv()
                gather_copy(hops, forward, early).start()
                if hops > 2:
                    gather_copy(hops - 1, forward, late).start()
        if hops > 2:
            spread_pair(2)
        for forward, early, late in ways:
            gather_copy(hops, forward, early).wait_recv()
        compute(0)
        for forward, early, late in ways:
            return_copy(1, forward, early).start()
        finish_compute(0, 1)
        if hops > 1:
            for forward, early, late in ways:
                gather_copy(hops - 1, forward, late).wait_recv()
            compute(hops - 1)

    with jax.named_scope("combine"):
        for stage in range(2, hops + 1):
            for u in range(2):
                for forward, early, late in ways:
                    if stage > 2 or u == early:
                        return_copy(stage - 1, forward, u).wait_recv()
                        buffer = from_left if forward else from_right
                        slot = 2 * (hops - stage + 1) + way_of(forward)
                        parts[slot, :, quarter(u)] = (
                            parts[slot, :, quarter(u)].astype(F32) + buffer[stage - 2, :, quarter(u)].astype(F32)
                        ).astype(BF16)
                    return_copy(stage, forward, u).start()
            if stage == 2:
                finish_compute(hops - 1, 1)
                spread_pair(0)
                spread_pair(hops - 1)
                for o in range(1, nz):
                    k_copy(o).wait_recv()
            elif stage == 3:
                take_pair(0)
                t_stage(1)
                sent_pair(1)
                sent_pair(2)
        if hops == 1:
            spread_pair(0)
            for o in range(1, nz):
                k_copy(o).wait_recv()
        if hops < 3:
            take_pair(0)
            t_stage(1)
        for stage in range(2, hops + 1):
            take_pair(hops - stage + 1)
            t_stage(stage)
        sent_pair(0)
        if hops > 1:
            sent_pair(hops - 1)
        for stage in range(1, hops + 1):
            for forward, early, late in ways:
                for h in range(2):
                    if stage < hops or h == early:
                        gather_copy(stage, forward, h).wait_send()
        for o in range(1, nz):
            plane_copy(o).wait_send()
            k_copy(o).wait_send()

    with jax.named_scope("home"):

        def summed_piece(j):
            at = pl.ds(j * 128, 128)
            value = parts[0, :, at].astype(F32)
            for forward, early, late in ways:
                if hops > 1 or 2 * j // each == early:
                    buffer = from_left if forward else from_right
                    value = value + buffer[hops - 1, :, at].astype(F32)
            return value

        def send_back(o, h):
            to = lax.rem(expert + o, ne)
            return remote(
                back_out.at[h, to], back_in.at[h, expert], e_send.at[h, o - 1], e_recv.at[h, o - 1],
                {"expert": to},
            )

        def finish_half(h, routed):
            mixed = (wide[:, sides[h]] + routed).astype(BF16)
            out_ref[:, :, sides[h]] = mixed.reshape(out_ref.shape[:2] + (half,))

        for u in range(2):
            for forward, early, late in ways:
                if hops > 1 or u == early:
                    return_copy(hops, forward, u).wait_recv()
        spread(summed_piece, back_out, 0)
        loop(1, ne, lambda o: send_back(o, 0).start())
        back_in[0, expert] = back_out[0, expert]
        for forward, early, late in ways:
            t_copy(hops, forward, early).wait_recv()
            buffer = t_left if forward else t_right
            picked = quarter(early) if hops == 1 else pl.ds(0, half)
            routed_high[:, picked] += buffer[hops - 1, :, picked].astype(F32)
        finish_half(1, routed_high[...])
        loop(1, ne, lambda o: send_back(o, 0).wait_recv())
        gather_pieces(back_in, returned, 0)
        finish_half(0, weighted(0, 0))

    with jax.named_scope("finish"):

        loop(1, ne, lambda o: send_back(o, 0).wait_send())
        for stage in range(1, hops + 1):
            for forward, early, late in ways:
                t_copy(stage, forward, early).wait_send()
                for h in range(2):
                    if stage > 1 or h == early:
                        return_copy(stage, forward, h).wait_send()


def layer_call(
    ns, ne, cap, x, z, xp, dtw, dtb, rates, skip, w, hid, gain, router, ids, wg, wu, wd
):
    tokens, channels = x.shape[0] * x.shape[1], x.shape[2]
    own, width = hid.shape[0] * hid.shape[1], hid.shape[2]
    picks = ids.shape[1]
    state_n = rates.shape[0]
    lanes = -(-xp.shape[0] // 128) * 128
    nz = ns // 2
    hops = nz // 2
    ny = 4 if ne == 16 else 2
    nx = ne // ny
    half = width // 2
    units = wg.shape[0]
    count = ne * cap
    pieces = width // 128
    dma = pltpu.SemaphoreType.DMA
    vmem = pltpu.VMEM
    return pl.pallas_call(
        functools.partial(layer_kernel, ns, ne, cap),
        out_shape=jax.ShapeDtypeStruct(hid.shape, BF16),
        in_specs=[VMEM] * 12 + [HBM] * 3,
        out_specs=VMEM,
        scratch_shapes=[
            vmem((tokens, channels), BF16),
            vmem((tokens, channels), BF16),
            vmem((own, width), BF16),
            vmem((count, own), BF16),
            vmem((picks, own, ne), F32),
            vmem((picks, own, 128), F32),
            vmem((ne, own, lanes), BF16),
            vmem((ne - 1, own, lanes), BF16),
            vmem((own, lanes), BF16),
            vmem((ne, own, lanes), BF16),
            vmem((tokens, channels), F32),
            vmem((tokens, channels), F32),
            vmem((tokens, channels), F32),
            vmem((tokens // (2 * BLOCK), 2 * state_n, 128), F32),
            vmem((2 * state_n + 8, channels), F32),
            vmem((2 * state_n + 8, channels // 2), F32),
            vmem((2 * state_n + 8, channels // 2), F32),
            vmem((nz, 2 * state_n + 8, channels // 2), F32),
            vmem((2 * state_n, channels), F32),
            vmem((tokens, channels), BF16),
            vmem((ns,) + w.shape, BF16),
            vmem((ny, nx, own, width), BF16),
            vmem((2, nx - 1, ny, own, half // 2), BF16),
            vmem((2, ny, own, half // 2), BF16),
            vmem((2, ny - 1, own, half // 2), BF16),
            vmem((2, ny - 1, nx, own, half // 2), BF16),
            vmem((2, nx, own, half // 2), BF16),
            vmem((2, nx - 1, own, half // 2), BF16),
            vmem((8, 128), F32),
            vmem((ne, 8, 128), F32),
            vmem((nz, 8, 128), F32),
            vmem((own, width), F32),
            vmem((nz, own, 128), F32),
            vmem((count * pieces // 2, 128), F32),
            vmem((2, ne, cap * pieces // 2, 128), BF16),
            vmem((2, ne, cap * pieces // 2, 128), BF16),
            vmem((1, ne, cap * pieces // 2, 128), BF16),
            vmem((1, ne, cap * pieces // 2, 128), BF16),
            vmem((count, width), BF16),
            vmem((nz, ne, cap * pieces // 2, 128), BF16),
            vmem((nz, ne, cap * pieces // 2, 128), BF16),
            vmem((nz, own, half), BF16),
            vmem((hops, own, half), BF16),
            vmem((hops, own, half), BF16),
            vmem((own, half), F32),
            vmem((nz, count, width), BF16),
            vmem((nz, count, width), BF16),
            vmem((hops, count, half), BF16),
            vmem((hops, count, half), BF16),
            vmem((2 * units, width), BF16),
            vmem((2 * units, width), BF16),
            vmem((2 * units, width), BF16),
            vmem((2 * count, 2 * units), BF16),
            dma((3,)),
            dma((3,)), dma((3,)),
            dma((ne - 1,)), dma((ne - 1,)),
            dma((ne - 1,)), dma((ne - 1,)),
            dma((2,)), dma((2,)),
            dma((nz,)), dma((nz,)),
            dma((2, hops)), dma((2, hops)),
            dma((nz,)), dma((nz,)),
            dma((4, nx + ny)), dma((4, nx + ny)),
            dma((4, nx + ny)), dma((4, nx + ny)),
            dma((ne - 1,)), dma((ne - 1,)),
            dma((nz - 1,)), dma((nz - 1,)),
            dma((2, ne - 1)), dma((2, ne - 1)),
            dma((2, ne - 1)), dma((2, ne - 1)),
            dma((2, 2, hops)), dma((2, 2, hops)),
            dma((2, 2, hops)), dma((2, 2, hops)),
            dma((nz, ne - 1)), dma((nz, ne - 1)),
            dma((2, hops)), dma((2, hops)),
            dma((nz - 1,)), dma((nz - 1,)),
        ],
        compiler_params=pltpu.CompilerParams(
            collective_id=0, has_side_effects=True, vmem_limit_bytes=58 * 1024 * 1024
        ),
    )(x, z, xp, dtw, dtb, rates, skip, w, hid, gain, router, ids, wg, wu, wd)


def body(
    hidden_in,
    mamba_x,
    mamba_z,
    x_proj,
    dt_weight,
    dt_bias,
    state_rates,
    skip_gain,
    out_weight,
    norm_gain,
    router_weight,
    expert_ids,
    w_gate,
    w_up,
    w_down,
):
    ns, ne = lax.axis_size("seq"), lax.axis_size("expert")
    token_rows = hidden_in.shape[0] * hidden_in.shape[1]
    experts = router_weight.shape[1]
    top_count = expert_ids.shape[2]
    capacity = max(2, min(token_rows, token_rows * top_count * 5 // (2 * experts)))
    return layer_call(
        ns,
        ne,
        capacity,
        mamba_x,
        mamba_z,
        x_proj.T,
        dt_weight,
        dt_bias[None],
        state_rates.T,
        skip_gain[None],
        out_weight,
        hidden_in,
        norm_gain[None],
        router_weight.T,
        jnp.transpose(expert_ids, (1, 2, 0)),
        w_gate[0].T,
        w_up[0].T,
        w_down[0].T,
    )


def solution(mesh):
    placed = (
        P(("seq", "expert"), None, None),
        P("seq", None, "expert"),
        P("seq", None, "expert"),
        P("expert", None),
        P(None, "expert"),
        P("expert"),
        P("expert", None),
        P("expert"),
        P("expert", "seq"),
        P(),
        P(),
        P(("seq", "expert"), None, None),
        P("expert", None, "seq"),
        P("expert", None, "seq"),
        P("expert", None, "seq"),
    )
    return jax.shard_map(
        body,
        mesh=mesh,
        in_specs=placed,
        out_specs=P(("seq", "expert"), None, None),
        check_vma=False,
    )
```

```python
import functools

import jax
import jax.numpy as jnp
from jax import lax
from jax.experimental import pallas as pl
from jax.experimental.pallas import tpu as pltpu
from jax.sharding import PartitionSpec as P

EPS = 1e-05
F32 = jnp.float32
BF16 = jnp.bfloat16
BLOCK = 16
VMEM = pl.BlockSpec(memory_space=pltpu.VMEM)
HBM = pl.BlockSpec(memory_space=pl.ANY)


def remote(src, dst, send, recv, where):
    return pltpu.make_async_remote_copy(
        src_ref=src,
        dst_ref=dst,
        send_sem=send,
        recv_sem=recv,
        device_id=where,
        device_id_type=pl.DeviceIdType.MESH,
    )


def greet(ns, ne, seq, expert):
    barrier = pltpu.get_barrier_semaphore()

    def to_seq(o, _):
        pl.semaphore_signal(
            barrier, inc=1, device_id={"seq": lax.rem(seq + o, ns)}, device_id_type=pl.DeviceIdType.MESH
        )
        return 0

    def to_expert(o, _):
        pl.semaphore_signal(
            barrier, inc=1, device_id={"expert": lax.rem(expert + o, ne)}, device_id_type=pl.DeviceIdType.MESH
        )
        return 0

    lax.fori_loop(1, ns, to_seq, 0)
    lax.fori_loop(1, ne, to_expert, 0)
    pl.semaphore_wait(barrier, ns + ne - 2)


def layer_kernel(
    ns, ne, cap,
    x_in, z_in, xp_ref, dtw_ref, dtb_ref, rates_ref, skip_ref, w_ref, hid_in,
    gain_ref, router_ref, ids_ref, wg_ref, wu_ref, wd_ref,
    out_ref,
    x_ref, z_ref, hid_ref, place_ref, pick_ref, put_ref,
    part, part_in, part_sum, proj, sizes, running, reading, bc,
    state, state_sib, state_chip, state_in, incoming, gated, wf,
    product, row_in, row_sum, row_last, col_in, col_sum, col_last,
    scale_out, scale_in, scale_held,
    wide, combine_w, flat, packed_out, packed_in, back_out, back_in, returned,
    q_out, q_in, t_out, t_left, t_right, routed_high,
    held, parts, from_left, from_right, gate_w, up_w, down_w, hidden,
    load_sem, pair_send, pair_recv, p1_send, p1_recv, p2_send, p2_recv,
    h_send, h_recv, s_send, s_recv, ring_send, ring_recv, sib_send, sib_recv,
    a_send, a_recv, b_send, b_recv, c_send, c_recv, z_send, z_recv, d_send, d_recv, e_send, e_recv,
    g_send, g_recv, r_send, r_recv, q_send, q_recv, t_send, t_recv, k_send, k_recv,
):
    seq, expert = lax.axis_index("seq"), lax.axis_index("expert")
    nz = ns // 2
    hops, back = nz // 2, nz - 1 - nz // 2
    ny, nx = product.shape[0], product.shape[1]
    ey, ex = expert // nx, lax.rem(expert, nx)
    plane, core = seq // 2, lax.rem(seq, 2)
    right = lax.rem(plane + 1, nz) * 2 + core
    left = lax.rem(plane + nz - 1, nz) * 2 + core
    sibling = {"seq": plane * 2 + 1 - core}
    rank = dtw_ref.shape[0]
    tokens, channels = x_ref.shape
    state_n = rates_ref.shape[0]
    own, width = hid_ref.shape
    half = width // 2
    low, high = pl.ds(0, half), pl.ds(half, half)

    def quarter(i):
        return pl.ds(i * (half // 2), half // 2)

    blocks = tokens // (2 * BLOCK)
    span = 2 * BLOCK
    columns = w_ref.shape[1]
    count = ne * cap
    units = wg_ref.shape[0]
    pieces = width // 128

    def loop(start, stop, action):
        def step(i, carry):
            action(i)
            return carry

        lax.fori_loop(start, stop, step, 0)

    def ring_copy(stage, forward):
        side, to = (0, right) if forward else (1, left)
        index = lax.rem(plane + (nz - stage + 1 if forward else stage - 1), nz) * 2 + core
        return remote(
            wf.at[index], wf.at[index], ring_send.at[side, stage - 1], ring_recv.at[side, stage - 1], {"seq": to}
        )

    def sibling_copy(index):
        return remote(wf.at[index], wf.at[index], sib_send.at[index // 2], sib_recv.at[index // 2], sibling)

    def ring_stage(stage):
        if 1 < stage <= hops + 1:
            ring_copy(stage - 1, True).wait_recv()
            sibling_copy(lax.rem(plane + nz - (stage - 1), nz) * 2 + core).start()
        if 1 < stage <= back + 1:
            ring_copy(stage - 1, False).wait_recv()
            sibling_copy(lax.rem(plane + stage - 1, nz) * 2 + core).start()
        if stage <= hops:
            ring_copy(stage, True).start()
        if stage <= back:
            ring_copy(stage, False).start()

    def grid(shape, axis):
        return lax.broadcasted_iota(jnp.int32, shape, axis)

    def choose():
        docs, picks, positions = ids_ref.shape
        chosen, marks = [], []
        for k in range(picks):
            found = jnp.zeros((own, 1), F32)
            for d in range(docs):
                here = grid((own, positions), 0) == grid((own, positions), 1) * docs + d
                row = ids_ref[d, k : k + 1, :].astype(F32)
                found = found + jnp.sum(jnp.where(here, row, 0.0), axis=1, keepdims=True)
            chosen.append(found)
            marks.append((grid((own, ne), 1).astype(F32) == found).astype(F32))
            pick_ref[k] = marks[k]
        before = (grid((own, own), 0) > grid((own, own), 1)).astype(BF16)
        taken = jnp.dot(before, sum(marks).astype(BF16), preferred_element_type=F32)
        for k in range(picks):
            slot = jnp.sum(marks[k] * taken, axis=1, keepdims=True)
            target = chosen[k] * cap + slot
            put_ref[k] = (grid(put_ref.shape[1:], 1).astype(F32) == target).astype(F32)
        eye = (grid((own, own), 0) == grid((own, own), 1)).astype(BF16)
        place_ref[...] = lax.dot_general(
            sum(put_ref[k] for k in range(picks))[:, :count].astype(BF16), eye, (((0,), (0,)), ((), ())), preferred_element_type=F32
        ).astype(BF16)

    with jax.named_scope("greet"):
        weights = ((wg_ref, gate_w), (wu_ref, up_w), (wd_ref, down_w))
        loads = [
            pltpu.make_async_copy(src, dst.at[pl.ds(0, units)], load_sem.at[i])
            for i, (src, dst) in enumerate(weights)
        ]
        for copy in loads:
            copy.start()
        wf[seq] = w_ref[...]
        x_ref[...] = x_in[...].reshape(tokens, channels)
        greet(ns, ne, seq, expert)
        ring_stage(1)
        sibling_copy(seq).start()

    with jax.named_scope("proj"):
        partial = lax.dot_general(
            x_ref[...], xp_ref[...], (((1,), (1,)), ((), ())), preferred_element_type=F32
        ).astype(BF16)
        spare = part.shape[2] - partial.shape[1]
        part[...] = jnp.concatenate([partial, jnp.zeros((tokens, spare), BF16)], axis=1).reshape(part.shape)

        def part_copy(o):
            to = lax.rem(expert + o, ne)
            return remote(part.at[to], part_in.at[o - 1], p1_send.at[o - 1], p1_recv.at[o - 1], {"expert": to})

        loop(1, ne, lambda o: part_copy(o).start())
        pairs = [
            remote(src, dst.at[pl.ds(units, units)], pair_send.at[i], pair_recv.at[i], sibling)
            for i, (src, dst) in enumerate(weights)
        ]

        z_ref[...] = z_in[...].reshape(tokens, channels)
        hid_ref[...] = hid_in[...].reshape(own, width)

        def add_part(o, acc):
            part_copy(o).wait_recv()
            return acc + part_in[o - 1].astype(F32)

        summed = lax.fori_loop(1, ne, add_part, part[expert].astype(F32))
        part_sum[...] = summed.astype(BF16)
        proj[expert] = part_sum[...]

        def proj_copy(o):
            to = lax.rem(expert + o, ne)
            return remote(part_sum, proj.at[expert], p2_send.at[o - 1], p2_recv.at[o - 1], {"expert": to})

        loop(1, ne, lambda o: proj_copy(o).start())
        ring_stage(2)
        choose()
        loop(1, ne, lambda o: proj_copy(o).wait_recv())
        ring_stage(3)

    with jax.named_scope("sizes"):
        proj_all = proj[...].reshape(tokens, proj.shape[2])
        raw = jnp.dot(proj_all[:, :rank], dtw_ref[...], preferred_element_type=F32) + dtb_ref[...]
        sizes[...] = jnp.maximum(raw, 0.0) + jnp.log1p(jnp.exp(-jnp.abs(raw)))
        turned = proj_all[:, rank:].astype(F32).T
        for b in range(blocks):
            bc[b, :, :span] = turned[: 2 * state_n, b * span : (b + 1) * span]

    with jax.named_scope("scan"):
        rates = -rates_ref[...]
        zero_state = jnp.zeros((state_n, channels), F32)
        zero_row = jnp.zeros((1, channels), F32)

        def scan_block(b, carry):
            states, sums = [carry[0], carry[1]], [carry[2], carry[3]]
            first = pl.multiple_of(b * span, span)
            size_block = sizes[pl.ds(first, span), :]
            drive_block = size_block * x_ref[pl.ds(first, span), :].astype(F32)
            terms = bc[b]
            for r in range(span):
                d = r % 2
                size = size_block[r : r + 1]
                states[d] = (
                    jnp.exp(size * rates) * states[d] + drive_block[r : r + 1] * terms[:state_n, r : r + 1]
                )
                reading[pl.ds(first + r, 1), :] = jnp.sum(
                    states[d] * terms[state_n : 2 * state_n, r : r + 1], axis=0, keepdims=True
                )
                sums[d] = sums[d] + size
                running[pl.ds(first + r, 1), :] = sums[d]
            return states[0], states[1], sums[0], sums[1]

        end0, end1, sum0, sum1 = lax.fori_loop(
            0, blocks, scan_block, (zero_state, zero_state, zero_row, zero_row)
        )
        state[:state_n, :] = end0
        state[state_n : 2 * state_n, :] = end1
        state[2 * state_n : 2 * state_n + 8, :] = jnp.concatenate(
            [sum0, sum1, jnp.zeros((6, channels), F32)], axis=0
        )

    with jax.named_scope("states"):
        side = channels // 2
        mine = pl.ds(pl.multiple_of(core * side, side), side)
        other = pl.ds(pl.multiple_of((1 - core) * side, side), side)
        half_copy = remote(state.at[:, other], state_sib, h_send.at[0], h_recv.at[0], sibling)
        half_copy.start()
        ring_stage(4)
        rates_mine = -rates_ref[:, mine]

        def through(message, d):
            return jnp.exp(message[2 * state_n + d : 2 * state_n + d + 1] * rates_mine)

        def ends(message, d):
            return message[d * state_n : (d + 1) * state_n]

        half_copy.wait_recv()
        first_core = core == 0
        here, there = state[:, mine], state_sib[...]
        early = jnp.where(first_core, here, there)
        late = jnp.where(first_core, there, here)
        for d in range(2):
            state_chip[d * state_n : (d + 1) * state_n, :] = through(late, d) * ends(early, d) + ends(late, d)
        state_chip[2 * state_n :, :] = early[2 * state_n :] + late[2 * state_n :]

        def state_copy(to, source):
            return remote(state_chip, state_in.at[source], s_send.at[to], s_recv.at[source], {"seq": to * 2 + core})

        loop(plane + 1, nz, lambda to: state_copy(to, plane).start())
        ring_stage(5)
        for copy in pairs:
            copy.start()

        def horner(source, carry):
            state_copy(plane, source).wait_recv()
            message = state_in[source]
            return tuple(through(message, d) * carry[d] + ends(message, d) for d in range(2))

        zero_half = jnp.zeros((state_n, side), F32)
        entering = lax.fori_loop(0, plane, horner, (zero_half, zero_half))
        for d in range(2):
            passed = through(early, d) * entering[d] + ends(early, d)
            state_sib[d * state_n : (d + 1) * state_n, :] = jnp.where(first_core, passed, entering[d])
            incoming[d * state_n : (d + 1) * state_n, mine] = jnp.where(first_core, entering[d], passed)
        enter_copy = remote(
            state_sib.at[pl.ds(0, 2 * state_n)], incoming.at[:, mine], h_send.at[1], h_recv.at[1], sibling
        )
        enter_copy.start()
        enter_copy.wait_recv()

    with jax.named_scope("gate"):
        skip = skip_ref[...]
        entered = [incoming[d * state_n : (d + 1) * state_n, :] for d in range(2)]

        def gate_block(b):
            first = pl.multiple_of(b * span, span)
            sum_block = running[pl.ds(first, span), :]
            terms = bc[b]
            for r in range(span):
                carried = jnp.exp(sum_block[r : r + 1] * rates) * entered[r % 2]
                reading[pl.ds(first + r, 1), :] += jnp.sum(
                    carried * terms[state_n : 2 * state_n, r : r + 1], axis=0, keepdims=True
                )
            drive = x_ref[pl.ds(first, span), :].astype(F32)
            gate = z_ref[pl.ds(first, span), :].astype(F32)
            value = (reading[pl.ds(first, span), :] + skip * drive) * (gate / (1.0 + jnp.exp(-gate)))
            gated[pl.ds(first, span), :] = value.astype(BF16)

        loop(0, blocks, gate_block)

    with jax.named_scope("project"):
        loop(0, nz, lambda i: sibling_copy(2 * i + 1 - core).wait_recv())

        def multiply(b):
            at = pl.multiple_of(b * columns, columns)
            out = jnp.dot(gated[...], wf[b], preferred_element_type=F32).astype(BF16)
            product[:, :, :, pl.ds(at, columns)] = out.reshape(ny, nx, own, columns)

        def row_copy(o, g):
            to = lax.rem(ex + o, nx)
            return remote(
                product.at[:, to, :, quarter(2 * g)], row_in.at[g, o - 1], a_send.at[g, o - 1], a_recv.at[g, o - 1],
                {"expert": ey * nx + to},
            )

        def col_copy(o, g):
            to = lax.rem(ey + o, ny)
            return remote(
                product.at[to, :, :, quarter(2 * g + 1)], col_in.at[g, o - 1], b_send.at[g, o - 1], b_recv.at[g, o - 1],
                {"expert": to * nx + ex},
            )

        def row_pass(o, g):
            to = lax.rem(ey + o, ny)
            return remote(
                row_sum.at[g, to], row_last.at[g, o - 1], a_send.at[2 + g, o - 1], a_recv.at[2 + g, o - 1],
                {"expert": to * nx + ex},
            )

        def col_pass(o, g):
            to = lax.rem(ex + o, nx)
            return remote(
                col_sum.at[g, to], col_last.at[g, o - 1], b_send.at[2 + g, o - 1], b_recv.at[2 + g, o - 1],
                {"expert": ey * nx + to},
            )

        def start_group(g):
            loop(1, nx, lambda o: row_copy(o, g).start())
            loop(1, ny, lambda o: col_copy(o, g).start())

        def pass_group(g):
            loop(1, nx, lambda o: row_copy(o, g).wait_recv())

            def add_row(i):
                acc = product[i, ex, :, quarter(2 * g)].astype(F32)
                for o in range(nx - 1):
                    acc = acc + row_in[g, o, i].astype(F32)
                row_sum[g, i] = acc.astype(BF16)

            loop(0, ny, add_row)
            loop(1, ny, lambda o: row_pass(o, g).start())
            loop(1, ny, lambda o: col_copy(o, g).wait_recv())

            def add_col(i):
                acc = product[ey, i, :, quarter(2 * g + 1)].astype(F32)
                for o in range(ny - 1):
                    acc = acc + col_in[g, o, i].astype(F32)
                col_sum[g, i] = acc.astype(BF16)

            loop(0, nx, add_col)
            loop(1, nx, lambda o: col_pass(o, g).start())

        def finish_group(g):
            loop(1, ny, lambda o: row_pass(o, g).wait_recv())
            acc = hid_ref[:, quarter(2 * g)].astype(F32) + row_sum[g, ey].astype(F32)
            for o in range(ny - 1):
                acc = acc + row_last[g, o].astype(F32)
            wide[:, quarter(2 * g)] = acc.astype(BF16).astype(F32)
            loop(1, nx, lambda o: col_pass(o, g).wait_recv())
            acc = hid_ref[:, quarter(2 * g + 1)].astype(F32) + col_sum[g, ex].astype(F32)
            for o in range(nx - 1):
                acc = acc + col_last[g, o].astype(F32)
            wide[:, quarter(2 * g + 1)] = acc.astype(BF16).astype(F32)

        loop(0, ns // 2, multiply)
        start_group(0)
        loop(ns // 2, ns, multiply)
        pass_group(0)
        start_group(1)
        finish_group(0)

    sides = (low, high)
    each = pieces // 2

    def spread(value_of, target, h):
        for j in range(each):
            flat[pl.ds(j, count, stride=each), :] = value_of(h * each + j)
        target[h] = flat[...].astype(BF16).reshape(target.shape[1:])

    def gather_pieces(source, target, h):
        flat[...] = source[h].astype(F32).reshape(flat.shape)
        for j in range(each):
            at = h * half + j * 128
            target[:, at : at + 128] = flat[pl.ds(j, count, stride=each), :].astype(BF16)

    with jax.named_scope("route"):

        def send_rows(o, h):
            to = lax.rem(expert + o, ne)
            return remote(
                packed_out.at[h, to], packed_in.at[h, expert], d_send.at[h, o - 1], d_recv.at[h, o - 1],
                {"expert": to},
            )

        def send_half(h):
            scaled = (wide[:, sides[h]] * gain_ref[:, sides[h]]).astype(BF16)

            def placed(j):
                at = j * 128 - h * half
                return jnp.dot(place_ref[...], scaled[:, at : at + 128], preferred_element_type=F32)

            spread(placed, packed_out, h)
            loop(1, ne, lambda o: send_rows(o, h).start())
            packed_in[h, expert] = packed_out[h, expert]

        def take_half(h):
            loop(1, ne, lambda o: send_rows(o, h).wait_recv())
            gather_pieces(packed_in, held.at[0], h)

        send_half(0)
        pass_group(1)
        take_half(0)

    def gather_copy(stage, forward, h):
        way = 0 if forward else 1
        source = held.at[2 * (stage - 1) + (0 if forward or stage == 1 else 1), :, sides[h]]
        target = held.at[2 * stage + way if stage < hops else 1, :, sides[h]]
        return remote(
            source, target, g_send.at[way, h, stage - 1], g_recv.at[way, h, stage - 1],
            {"seq": right if forward else left},
        )

    def return_copy(stage, forward, u):
        way = 0 if forward else 1
        buffer = from_left if forward else from_right
        slot = 2 * (hops - stage + 1) + way_of(forward) if stage > 1 else 1
        return remote(
            parts.at[slot, :, quarter(u)], buffer.at[stage - 1, :, quarter(u)],
            r_send.at[way, u, stage - 1], r_recv.at[way, u, stage - 1], {"seq": right if forward else left},
        )

    def q_copy(o, slot):
        to = lax.rem(expert + o, ne)
        return remote(
            q_out.at[slot, to], q_in.at[slot, expert], q_send.at[slot, o - 1], q_recv.at[slot, o - 1], {"expert": to}
        )

    def t_copy(stage, forward, u):
        way = 0 if forward else 1
        buffer = t_left if forward else t_right
        slot = 2 * (hops - stage + 1) + way_of(forward) if stage > 1 else 1
        picked = quarter(u) if stage == 1 else pl.ds(0, half)
        return remote(
            t_out.at[slot, :, picked], buffer.at[stage - 1, :, picked],
            t_send.at[way, stage - 1], t_recv.at[way, stage - 1], {"seq": right if forward else left},
        )

    def k_copy(o):
        to = lax.rem(plane + o, nz) * 2 + core
        slot = 2 * o if o < hops else 1 if o == hops else 2 * (nz - o) + 1
        return remote(combine_w.at[0], combine_w.at[slot], k_send.at[o - 1], k_recv.at[o - 1], {"seq": to})

    def weighted(slot, h):
        weights_all = combine_w[slot][:, :count]
        weights_high = weights_all.astype(BF16)
        weights_low = (weights_all - weights_high.astype(F32)).astype(BF16)
        values = returned[:, sides[h]]
        return jnp.dot(weights_high, values, preferred_element_type=F32) + jnp.dot(
            weights_low, values, preferred_element_type=F32
        )

    def spread_q(slot):
        for j in range(each):
            at = half + j * 128
            flat[pl.ds(j, count, stride=each), :] = parts[slot, :, at : at + 128].astype(F32)
        q_out[slot] = flat[...].astype(BF16).reshape(q_out.shape[1:])
        loop(1, ne, lambda o: q_copy(o, slot).start())
        q_in[slot, expert] = q_out[slot, expert]

    def take_q(slot):
        loop(1, ne, lambda o: q_copy(o, slot).wait_recv())
        flat[...] = q_in[slot].astype(F32).reshape(flat.shape)
        for j in range(each):
            at = half + j * 128
            returned[:, at : at + 128] = flat[pl.ds(j, count, stride=each), :].astype(BF16)
        value = weighted(slot, 1)
        if slot == 0:
            routed_high[...] = value
        else:
            t_out[slot] = value.astype(BF16)

    def spread_pair(pair):
        spread_q(2 * pair)
        spread_q(2 * pair + 1)

    def take_pair(pair):
        take_q(2 * pair + 1)
        take_q(2 * pair)

    def t_stage(stage):
        for forward, early, late in ways:
            if stage > 1:
                t_copy(stage - 1, forward, early).wait_recv()
                buffer = t_left if forward else t_right
                slot = 2 * (hops - stage + 1) + way_of(forward)
                picked = quarter(early) if stage == 2 else pl.ds(0, half)
                t_out[slot, :, picked] = (
                    t_out[slot, :, picked].astype(F32) + buffer[stage - 2, :, picked].astype(F32)
                ).astype(BF16)
            t_copy(stage, forward, early).start()

    def sent_early():
        def sent_peers(o):
            part_copy(o).wait_send()
            proj_copy(o).wait_send()
            scale_copy(o).wait_send()
            for h in range(2):
                send_rows(o, h).wait_send()

        loop(1, ne, sent_peers)
        for g in range(2):

            def sent_rows(o):
                row_copy(o, g).wait_send()
                col_pass(o, g).wait_send()

            def sent_cols(o):
                col_copy(o, g).wait_send()
                row_pass(o, g).wait_send()

            loop(1, nx, sent_rows)
            loop(1, ny, sent_cols)
        loop(plane + 1, nz, lambda to: state_copy(to, plane).wait_send())
        half_copy.wait_send()
        enter_copy.wait_send()
        for stage in range(1, hops + 1):
            ring_copy(stage, True).wait_send()
        for stage in range(1, back + 1):
            ring_copy(stage, False).wait_send()
        loop(0, nz, lambda i: sibling_copy(2 * i + core).wait_send())
        for copy in pairs:
            copy.wait_send()

    def sent_pair(pair):
        def sent(o):
            q_copy(o, 2 * pair).wait_send()
            q_copy(o, 2 * pair + 1).wait_send()

        loop(1, ne, sent)

    def way_of(forward):
        return 1 if forward else 0

    ways = ((True, 0, 1), (False, 1, 0))

    def scale_copy(o):
        to = lax.rem(expert + o, ne)
        return remote(scale_out, scale_in.at[expert], c_send.at[o - 1], c_recv.at[o - 1], {"expert": to})

    def plane_copy(o):
        to = lax.rem(plane + o, nz) * 2 + core
        slot = 2 * o if o < hops else 1 if o == hops else 2 * (nz - o) + 1
        return remote(scale_held.at[0], scale_held.at[slot], z_send.at[o - 1], z_recv.at[o - 1], {"seq": to})

    def first_row(value):
        return jnp.where(grid((8, 128), 0) == 0, value, 0.0)

    def send_scales():
        mixed = wide[...]
        scale = lax.rsqrt(jnp.mean(mixed * mixed, axis=-1, keepdims=True) + EPS)
        scale_out[...] = first_row(jnp.sum(scale * (put_ref[0] + put_ref[1]), axis=0, keepdims=True))
        loop(1, ne, lambda o: scale_copy(o).start())
        scale_in[expert] = scale_out[...]
        return (mixed * scale * gain_ref[...]).astype(BF16)

    def take_scales():
        loop(1, ne, lambda o: scale_copy(o).wait_recv())
        rows_in = jnp.sum(scale_in[...], axis=1)
        row, source = grid((count, ne), 0), grid((count, ne), 1)
        sender = ((row >= source * cap) & (row < (source + 1) * cap)).astype(F32)
        spread_rows = jnp.dot(sender, rows_in, preferred_element_type=F32, precision=lax.Precision.HIGHEST)
        passed = jnp.sum((row >= (source + 1) * cap).astype(F32), axis=1, keepdims=True)
        lane, place = grid((count, 128), 1).astype(F32), grid((count, 128), 0).astype(F32)
        wanted = (expert * cap).astype(F32) + place - cap * passed
        column = jnp.sum(jnp.where(lane == wanted, spread_rows, 0.0), axis=1, keepdims=True)
        scale_held[0] = first_row(jnp.sum(jnp.where(lane == place, column, 0.0), axis=0, keepdims=True))
        for o in range(1, nz):
            plane_copy(o).start()

    def scale_column(slot):
        lane, place = grid((count, 128), 1), grid((count, 128), 0)
        return jnp.sum(jnp.where(lane == place, scale_held[slot, 0:1, :], 0.0), axis=1, keepdims=True)

    def compute(pair):
        rows = held[2 * pair : 2 * pair + 2].reshape(2 * count, width)
        scale = jnp.concatenate([scale_column(2 * pair), scale_column(2 * pair + 1)], axis=0)
        across = (((1,), (1,)), ((), ()))
        gate = lax.dot_general(rows, gate_w[...], across, preferred_element_type=F32) * scale
        up = lax.dot_general(rows, up_w[...], across, preferred_element_type=F32) * scale
        hidden[...] = (gate / (1.0 + jnp.exp(-gate)) * up).astype(BF16)
        finish_compute(pair, 0)

    def finish_compute(pair, h):
        step = min(half, 512)
        blocks_half = half // step

        def down(b):
            at = pl.multiple_of(b * step, step)
            out = jnp.dot(hidden[...], down_w[:, pl.ds(at, step)], preferred_element_type=F32)
            parts[2 * pair : 2 * pair + 2, :, pl.ds(at, step)] = out.astype(BF16).reshape(2, count, step)

        loop(h * blocks_half, (h + 1) * blocks_half, down)

    def start_gather(stage, h):
        for forward, early, late in ways:
            if stage < hops or h == early:
                gather_copy(stage, forward, h).start()

    def wait_gather(stage, h):
        for forward, early, late in ways:
            gather_copy(stage, forward, h).wait_recv()

    with jax.named_scope("experts"):
        start_gather(1, 0)
        finish_group(1)
        send_half(1)
        normed = send_scales()
        if hops > 2:
            wait_gather(1, 0)
            start_gather(2, 0)
        take_half(1)
        start_gather(1, 1)
        take_scales()
        logits = lax.dot_general(
            normed, router_ref[...], (((1,), (1,)), ((), ())), preferred_element_type=F32
        )
        scores = []
        for k in range(pick_ref.shape[0]):
            picked = jnp.sum(pick_ref[k] * logits, axis=-1, keepdims=True)
            scores.append(1.0 / (1.0 + jnp.exp(-picked)))
        all_scores = sum(scores)
        combine_w[0] = sum((score / all_scores) * put_ref[k] for k, score in enumerate(scores))
        for o in range(1, nz):
            k_copy(o).start()
        for copy in loads:
            copy.wait()
        for copy in pairs:
            copy.wait_recv()
        for o in range(1, nz):
            plane_copy(o).wait_recv()
        sent_early()
        if hops > 2:
            wait_gather(1, 1)
            start_gather(2, 1)
            wait_gather(2, 0)
            gather_copy(3, True, 0).start()
            compute(1)
            finish_compute(1, 1)
            wait_gather(2, 1)
            gather_copy(3, False, 1).start()
            compute(2)
            finish_compute(2, 1)
        for forward, early, late in ways:
            if hops > 1:
                gather_copy(hops - 1, forward, early).wait_recv()
                gather_copy(hops, forward, early).start()
                if hops > 2:
                    gather_copy(hops - 1, forward, late).start()
        if hops > 2:
            spread_pair(1)
            spread_pair(2)
        for forward, early, late in ways:
            gather_copy(hops, forward, early).wait_recv()
        compute(0)
        for forward, early, late in ways:
            return_copy(1, forward, early).start()
        finish_compute(0, 1)
        if hops > 1:
            for forward, early, late in ways:
                gather_copy(hops - 1, forward, late).wait_recv()
            compute(hops - 1)

    with jax.named_scope("combine"):
        for stage in range(2, hops + 1):
            for u in range(2):
                for forward, early, late in ways:
                    if stage > 2 or u == early:
                        return_copy(stage - 1, forward, u).wait_recv()
                        buffer = from_left if forward else from_right
                        slot = 2 * (hops - stage + 1) + way_of(forward)
                        parts[slot, :, quarter(u)] = (
                            parts[slot, :, quarter(u)].astype(F32) + buffer[stage - 2, :, quarter(u)].astype(F32)
                        ).astype(BF16)
                    return_copy(stage, forward, u).start()
            if stage == 2:
                finish_compute(hops - 1, 1)
                spread_pair(0)
                spread_pair(hops - 1)
                for o in range(1, nz):
                    k_copy(o).wait_recv()
            elif stage == 3:
                take_pair(0)
                t_stage(1)
                sent_pair(1)
                sent_pair(2)
        if hops == 1:
            spread_pair(0)
            for o in range(1, nz):
                k_copy(o).wait_recv()
        if hops < 3:
            take_pair(0)
            t_stage(1)
        for stage in range(2, hops + 1):
            take_pair(hops - stage + 1)
            t_stage(stage)
        sent_pair(0)
        if hops > 1:
            sent_pair(hops - 1)
        for stage in range(1, hops + 1):
            for forward, early, late in ways:
                for h in range(2):
                    if stage < hops or h == early:
                        gather_copy(stage, forward, h).wait_send()
        for o in range(1, nz):
            plane_copy(o).wait_send()
            k_copy(o).wait_send()

    with jax.named_scope("home"):

        def summed_piece(j):
            at = pl.ds(j * 128, 128)
            value = parts[0, :, at].astype(F32)
            for forward, early, late in ways:
                if hops > 1 or 2 * j // each == early:
                    buffer = from_left if forward else from_right
                    value = value + buffer[hops - 1, :, at].astype(F32)
            return value

        def send_back(o, h):
            to = lax.rem(expert + o, ne)
            return remote(
                back_out.at[h, to], back_in.at[h, expert], e_send.at[h, o - 1], e_recv.at[h, o - 1],
                {"expert": to},
            )

        def finish_half(h, routed):
            mixed = (wide[:, sides[h]] + routed).astype(BF16)
            out_ref[:, :, sides[h]] = mixed.reshape(out_ref.shape[:2] + (half,))

        for u in range(2):
            for forward, early, late in ways:
                if hops > 1 or u == early:
                    return_copy(hops, forward, u).wait_recv()
        spread(summed_piece, back_out, 0)
        loop(1, ne, lambda o: send_back(o, 0).start())
        back_in[0, expert] = back_out[0, expert]
        for forward, early, late in ways:
            t_copy(hops, forward, early).wait_recv()
            buffer = t_left if forward else t_right
            picked = quarter(early) if hops == 1 else pl.ds(0, half)
            routed_high[:, picked] += buffer[hops - 1, :, picked].astype(F32)
        finish_half(1, routed_high[...])
        loop(1, ne, lambda o: send_back(o, 0).wait_recv())
        gather_pieces(back_in, returned, 0)
        finish_half(0, weighted(0, 0))

    with jax.named_scope("finish"):

        loop(1, ne, lambda o: send_back(o, 0).wait_send())
        for stage in range(1, hops + 1):
            for forward, early, late in ways:
                t_copy(stage, forward, early).wait_send()
                for h in range(2):
                    if stage > 1 or h == early:
                        return_copy(stage, forward, h).wait_send()


def layer_call(
    ns, ne, cap, x, z, xp, dtw, dtb, rates, skip, w, hid, gain, router, ids, wg, wu, wd
):
    tokens, channels = x.shape[0] * x.shape[1], x.shape[2]
    own, width = hid.shape[0] * hid.shape[1], hid.shape[2]
    picks = ids.shape[1]
    state_n = rates.shape[0]
    lanes = -(-xp.shape[0] // 128) * 128
    nz = ns // 2
    hops = nz // 2
    ny = 4 if ne == 16 else 2
    nx = ne // ny
    half = width // 2
    units = wg.shape[0]
    count = ne * cap
    pieces = width // 128
    dma = pltpu.SemaphoreType.DMA
    vmem = pltpu.VMEM
    return pl.pallas_call(
        functools.partial(layer_kernel, ns, ne, cap),
        out_shape=jax.ShapeDtypeStruct(hid.shape, BF16),
        in_specs=[VMEM] * 12 + [HBM] * 3,
        out_specs=VMEM,
        scratch_shapes=[
            vmem((tokens, channels), BF16),
            vmem((tokens, channels), BF16),
            vmem((own, width), BF16),
            vmem((count, own), BF16),
            vmem((picks, own, ne), F32),
            vmem((picks, own, 128), F32),
            vmem((ne, own, lanes), BF16),
            vmem((ne - 1, own, lanes), BF16),
            vmem((own, lanes), BF16),
            vmem((ne, own, lanes), BF16),
            vmem((tokens, channels), F32),
            vmem((tokens, channels), F32),
            vmem((tokens, channels), F32),
            vmem((tokens // (2 * BLOCK), 2 * state_n, 128), F32),
            vmem((2 * state_n + 8, channels), F32),
            vmem((2 * state_n + 8, channels // 2), F32),
            vmem((2 * state_n + 8, channels // 2), F32),
            vmem((nz, 2 * state_n + 8, channels // 2), F32),
            vmem((2 * state_n, channels), F32),
            vmem((tokens, channels), BF16),
            vmem((ns,) + w.shape, BF16),
            vmem((ny, nx, own, width), BF16),
            vmem((2, nx - 1, ny, own, half // 2), BF16),
            vmem((2, ny, own, half // 2), BF16),
            vmem((2, ny - 1, own, half // 2), BF16),
            vmem((2, ny - 1, nx, own, half // 2), BF16),
            vmem((2, nx, own, half // 2), BF16),
            vmem((2, nx - 1, own, half // 2), BF16),
            vmem((8, 128), F32),
            vmem((ne, 8, 128), F32),
            vmem((nz, 8, 128), F32),
            vmem((own, width), F32),
            vmem((nz, own, 128), F32),
            vmem((count * pieces // 2, 128), F32),
            vmem((2, ne, cap * pieces // 2, 128), BF16),
            vmem((2, ne, cap * pieces // 2, 128), BF16),
            vmem((1, ne, cap * pieces // 2, 128), BF16),
            vmem((1, ne, cap * pieces // 2, 128), BF16),
            vmem((count, width), BF16),
            vmem((nz, ne, cap * pieces // 2, 128), BF16),
            vmem((nz, ne, cap * pieces // 2, 128), BF16),
            vmem((nz, own, half), BF16),
            vmem((hops, own, half), BF16),
            vmem((hops, own, half), BF16),
            vmem((own, half), F32),
            vmem((nz, count, width), BF16),
            vmem((nz, count, width), BF16),
            vmem((hops, count, half), BF16),
            vmem((hops, count, half), BF16),
            vmem((2 * units, width), BF16),
            vmem((2 * units, width), BF16),
            vmem((2 * units, width), BF16),
            vmem((2 * count, 2 * units), BF16),
            dma((3,)),
            dma((3,)), dma((3,)),
            dma((ne - 1,)), dma((ne - 1,)),
            dma((ne - 1,)), dma((ne - 1,)),
            dma((2,)), dma((2,)),
            dma((nz,)), dma((nz,)),
            dma((2, hops)), dma((2, hops)),
            dma((nz,)), dma((nz,)),
            dma((4, nx + ny)), dma((4, nx + ny)),
            dma((4, nx + ny)), dma((4, nx + ny)),
            dma((ne - 1,)), dma((ne - 1,)),
            dma((nz - 1,)), dma((nz - 1,)),
            dma((2, ne - 1)), dma((2, ne - 1)),
            dma((2, ne - 1)), dma((2, ne - 1)),
            dma((2, 2, hops)), dma((2, 2, hops)),
            dma((2, 2, hops)), dma((2, 2, hops)),
            dma((nz, ne - 1)), dma((nz, ne - 1)),
            dma((2, hops)), dma((2, hops)),
            dma((nz - 1,)), dma((nz - 1,)),
        ],
        compiler_params=pltpu.CompilerParams(
            collective_id=0, has_side_effects=True, vmem_limit_bytes=58 * 1024 * 1024
        ),
    )(x, z, xp, dtw, dtb, rates, skip, w, hid, gain, router, ids, wg, wu, wd)


def body(
    hidden_in,
    mamba_x,
    mamba_z,
    x_proj,
    dt_weight,
    dt_bias,
    state_rates,
    skip_gain,
    out_weight,
    norm_gain,
    router_weight,
    expert_ids,
    w_gate,
    w_up,
    w_down,
):
    ns, ne = lax.axis_size("seq"), lax.axis_size("expert")
    token_rows = hidden_in.shape[0] * hidden_in.shape[1]
    experts = router_weight.shape[1]
    top_count = expert_ids.shape[2]
    capacity = max(2, min(token_rows, token_rows * top_count * 5 // (2 * experts)))
    return layer_call(
        ns,
        ne,
        capacity,
        mamba_x,
        mamba_z,
        x_proj.T,
        dt_weight,
        dt_bias[None],
        state_rates.T,
        skip_gain[None],
        out_weight,
        hidden_in,
        norm_gain[None],
        router_weight.T,
        jnp.transpose(expert_ids, (1, 2, 0)),
        w_gate[0].T,
        w_up[0].T,
        w_down[0].T,
    )


def solution(mesh):
    placed = (
        P(("seq", "expert"), None, None),
        P("seq", None, "expert"),
        P("seq", None, "expert"),
        P("expert", None),
        P(None, "expert"),
        P("expert"),
        P("expert", None),
        P("expert"),
        P("expert", "seq"),
        P(),
        P(),
        P(("seq", "expert"), None, None),
        P("expert", None, "seq"),
        P("expert", None, "seq"),
        P("expert", None, "seq"),
    )
    return jax.shard_map(
        body,
        mesh=mesh,
        in_specs=placed,
        out_specs=P(("seq", "expert"), None, None),
        check_vma=False,
    )
```
